32 devices in a mesh: fsdp: 8 (over z, core), sp: 4 (over y, x).
Axes of the slice: x: 2, y: 2, z: 4, core: 2. Of those that a mesh axis runs over, the one named last changes fastest.
Arguments:
- tokens: bfloat16 [8192, 2048], P(('fsdp', 'sp')), may hold values from -6 to 6
- segments: int32 [8192], P('fsdp'), may hold values from -1 to 2, as said below
- routes: int32 [8192, 4], P('fsdp'), may hold values from 0 to 15, all different within a row; in each aligned block of 1024 rows (0 to 1023, 1024 to 2047, ...) at most 384 rows name the same one
- cotangent: bfloat16 [8192, 2048], P(('fsdp', 'sp')), may hold values from -6 to 6
- gain_attn: bfloat16 [2048], replicated, may hold values from 0.5 to 1.5
- w_query: bfloat16 [2048, 2048], P('fsdp', 'sp'), may hold values from -0.125 to 0.125
- w_key: bfloat16 [2048, 2048], P('fsdp', 'sp'), may hold values from -0.125 to 0.125
- w_value: bfloat16 [2048, 2048], P('fsdp', 'sp'), may hold values from -0.125 to 0.125
- bias_query: bfloat16 [2048], P('sp'), may hold values from -3 to 3
- bias_key: bfloat16 [2048], P('sp'), may hold values from -3 to 3
- bias_value: bfloat16 [2048], P('sp'), may hold values from -3 to 3
- w_out: bfloat16 [2048, 2048], P('sp', 'fsdp'), may hold values from -0.75 to 0.75
- gain_mlp: bfloat16 [2048], replicated, may hold values from 0.5 to 1.5
- router: bfloat16 [2048, 16], replicated, may hold values from -0.0625 to 0.0625
- mix_gate: bfloat16 [2048], replicated, may hold values from -0.125 to 0.125
- shared_gate: bfloat16 [2048, 5632], P('fsdp', 'sp'), may hold values from -0.125 to 0.125
- shared_up: bfloat16 [2048, 5632], P('fsdp', 'sp'), may hold values from -0.125 to 0.125
- shared_down: bfloat16 [5632, 2048], P('sp', 'fsdp'), may hold values from -0.21875 to 0.21875
- expert_gate: bfloat16 [16, 2048, 1408], P('fsdp', None, 'sp'), may hold values from -0.125 to 0.125
- expert_up: bfloat16 [16, 2048, 1408], P('fsdp', None, 'sp'), may hold values from -0.125 to 0.125
- expert_down: bfloat16 [16, 1408, 2048], P('fsdp', 'sp'), may hold values from -2.5 to 2.5
Outputs:
- output: bfloat16 [8192, 2048], P(('fsdp', 'sp'))
- grad_tokens: float32 [8192, 2048], P(('fsdp', 'sp'))
- grad_gain_attn: float32 [2048], replicated
- grad_w_query: float32 [2048, 2048], P('fsdp', 'sp')
- grad_w_key: float32 [2048, 2048], P('fsdp', 'sp')
- grad_w_value: float32 [2048, 2048], P('fsdp', 'sp')
- grad_bias_query: float32 [2048], P('sp')
- grad_bias_key: float32 [2048], P('sp')
- grad_bias_value: float32 [2048], P('sp')
- grad_w_out: float32 [2048, 2048], P('sp', 'fsdp')
- grad_gain_mlp: float32 [2048], replicated
- grad_router: float32 [2048, 16], replicated
- grad_mix_gate: float32 [2048], replicated
- grad_shared_gate: float32 [2048, 5632], P('fsdp', 'sp')
- grad_shared_up: float32 [2048, 5632], P('fsdp', 'sp')
- grad_shared_down: float32 [5632, 2048], P('sp', 'fsdp')
- grad_expert_gate: float32 [16, 2048, 1408], P('fsdp', None, 'sp')
- grad_expert_up: float32 [16, 2048, 1408], P('fsdp', None, 'sp')
- grad_expert_down: float32 [16, 1408, 2048], P('fsdp', 'sp')
The draws below stay inside these ranges and needn't reach their ends.
Inputs may be any that keep to these rules, and one draw needn't show every extreme that they name: `segments`: each sequence of 1024 tokens holds documents 0, 1 and 2 in this order, then at least one padding token marked -1; document 0 ends within the sequence's first 256 tokens and document 1 within its last 256. `routes`: each row names 4 different experts. Within each sequence no expert is named by more than 384 rows, a bound that some block reaches.
All inputs are finite; a program needn't handle non-finite values.
Results may differ from the reference program's by a relative error of at most 0.025.
Values may be sent and summed in bfloat16 or wider, within the bound.
A program may use at most 384 MiB of HBM per device.

```python
import math
import jax
import jax.numpy as jnp
import numpy as np
from jax import lax

D = 2048
HEADS = 16
HEAD = 128
FF_E = 1408
FF_S = 5632
TOP = 4
SEQ = 1024
TOK_DEV = 256
TOKENS = 8192
EXPERTS = 16
CAP = 384
N_SP = 4


def draw_segments(key, part):
    key = jax.random.fold_in(key, 11)
    seq_count = TOKENS // SEQ
    first_key, second_key, third_key = jax.random.split(key, 3)
    first_end = jax.random.randint(first_key, (seq_count, 1), 1, TOK_DEV)
    second_end = jax.random.randint(second_key, (seq_count, 1), SEQ - TOK_DEV + 1, SEQ - 1)
    third_end = jax.random.randint(third_key, (seq_count, 1), second_end + 1, SEQ)
    position = jnp.arange(SEQ, dtype=jnp.int32)[None, :]
    numbers = jnp.where(position < first_end, 0, jnp.where(position < second_end, 1, jnp.where(position < third_end, 2, -1)))
    return numbers.reshape(-1).astype(jnp.int32)


def steps_of(own_key, extent, cuts, low, high):
    factor_of = 1.0
    for axis_at, blocks in cuts:
        draws = jax.random.uniform(jax.random.fold_in(jax.random.fold_in(own_key, 6), axis_at), (blocks,), jnp.float32, low / len(cuts), high / len(cuts))
        factor_of = factor_of * jnp.repeat(jnp.exp(draws), extent[axis_at] // blocks).reshape((-1,) + (1,) * (len(extent) - 1 - axis_at))
    return factor_of


def deal_out(own_key, own, number, rows, amount, top, limit, slope):
    order = jax.random.permutation(own_key, amount)
    crowded, common = load_shares(amount, rows * top, limit, slope, True), load_shares(amount, rows * top, limit, slope, False)
    places = jnp.arange(amount)

    def named(tallies, offset_by):
        used = int((tallies > 0).sum())
        fixed = max(1, used // 4)
        passed = fixed + (places - fixed + offset_by * (used - fixed)) % max(1, amount - fixed)
        return jnp.zeros((amount,), jnp.int32).at[order[jnp.where(places < fixed, places, passed)]].set(jnp.asarray(tallies, jnp.int32))

    tallies = jnp.where(number % 4 == 0, named(crowded, number // 4), named(common, number - number // 4 - 1))
    mixed = jax.random.permutation(jax.random.fold_in(own, 3), amount)
    donor, taker = mixed[0:amount // 2 * 2:2], mixed[1:amount // 2 * 2:2]
    room = jnp.minimum(tallies[donor] - 1, limit - tallies[taker]) // 2
    room = jnp.where((donor == order[0]) | (taker == order[0]) | (tallies[taker] == 0), 0, jnp.maximum(room, 0))
    passed = jax.random.randint(jax.random.fold_in(own, 4), (amount // 2,), 0, 1 << 20) % (room + 1)
    tallies = tallies.at[donor].add(-passed).at[taker].add(passed)
    members = jnp.searchsorted(jnp.cumsum(tallies), jnp.arange(rows * top), side="right").astype(jnp.int32)
    grid = members.reshape(top, rows).T
    grid = grid[jax.random.permutation(jax.random.fold_in(own, 1), rows)]
    offset_by = jax.random.randint(jax.random.fold_in(own, 2), (rows, 1), 0, top)
    return jnp.take_along_axis(grid, (jnp.arange(top)[None, :] + offset_by) % top, axis=1)


def load_shares(amount, total, most, skew, full):
    weights = [(1 << 20) // math.isqrt(standing ** skew) + 1 for standing in range(1, amount + 1)]
    largest = most if full else min(most, max(-(-total // amount), total * weights[0] // sum(weights)))
    least = 1 if total - largest >= amount - 1 else 0
    holding, spare = [largest] + [least] * (amount - 1), total - largest - least * (amount - 1)
    while spare > 0:
        candidates = [i for i in range(1, amount) if holding[i] < largest] or [i for i in range(1, amount) if holding[i] < most]
        whole, left = sum([weights[i] for i in candidates]), spare
        for i in candidates:
            extra = min(most - holding[i], max(1, left * weights[i] // whole), spare)
            holding[i] = holding[i] + extra
            spare = spare - extra
    return np.array(holding)


def centred(own_key, shape, width, bound, pieces=(), kind=jnp.bfloat16):
    array = jax.random.normal(own_key, shape, jnp.float32) * width
    if len(pieces) > 0:
        array = steps_of(own_key, shape, pieces, -0.22, 0.18) * array
    return jnp.clip(array, min=-bound, max=bound).astype(kind)


def setup_inputs(seed: int = 0) -> dict:
    key_of = jax.random.split(jax.random.key(seed), 22)
    tokens = centred(key_of[0], (TOKENS, D), 1.0, 6.0, ((0, 32),))
    segments = draw_segments(jax.random.fold_in(key_of[21], 71), 0)
    routes_keys = jax.random.split(jax.random.fold_in(key_of[2], 1), TOKENS // SEQ)
    routes_turns = jax.random.permutation(jax.random.fold_in(key_of[2], 3), TOKENS // SEQ)
    routes = jax.vmap(lambda own, number: deal_out(jax.random.fold_in(key_of[2], 2), own, number, SEQ, EXPERTS, TOP, CAP, 1))(routes_keys, routes_turns).reshape((TOKENS, TOP))
    cotangent = centred(key_of[3], (TOKENS, D), 1.0, 6.0, ((0, 32),))
    gain_attn = jnp.clip(1.0 + 0.1 * jax.random.normal(key_of[4], (D,), jnp.float32), 0.5, 1.5).astype(jnp.bfloat16)
    w_query = centred(key_of[5], (D, HEADS * HEAD), D ** -0.5, 0.125, ((0, 8), (1, 4)))
    w_key = centred(key_of[6], (D, HEADS * HEAD), D ** -0.5, 0.125, ((0, 8), (1, 4)))
    w_value = centred(key_of[7], (D, HEADS * HEAD), D ** -0.5, 0.125, ((0, 8), (1, 4)))
    bias_query = centred(key_of[8], (HEADS * HEAD,), 0.5, 3.0, ((0, 4),))
    bias_key = centred(key_of[9], (HEADS * HEAD,), 0.5, 3.0, ((0, 4),))
    bias_value = centred(key_of[10], (HEADS * HEAD,), 0.5, 3.0, ((0, 4),))
    w_out = centred(key_of[11], (HEADS * HEAD, D), (HEADS * HEAD // 32) ** -0.5, 0.75, ((0, 4), (1, 8)))
    gain_mlp = jnp.clip(1.0 + 0.1 * jax.random.normal(key_of[12], (D,), jnp.float32), 0.5, 1.5).astype(jnp.bfloat16)
    router = centred(key_of[13], (D, EXPERTS), (4 * D) ** -0.5, 0.0625)
    mix_gate = centred(key_of[14], (D,), D ** -0.5, 0.125)
    shared_gate = centred(key_of[15], (D, FF_S), D ** -0.5, 0.125, ((0, 8), (1, 4)))
    shared_up = centred(key_of[16], (D, FF_S), D ** -0.5, 0.125, ((0, 8), (1, 4)))
    shared_down = centred(key_of[17], (FF_S, D), (FF_S // 8) ** -0.5, 0.21875, ((0, 4), (1, 8)))
    expert_gate = centred(key_of[18], (EXPERTS, D, FF_E), D ** -0.5, 0.125, ((0, 8), (2, 4)))
    expert_up = centred(key_of[19], (EXPERTS, D, FF_E), D ** -0.5, 0.125, ((0, 8), (2, 4)))
    expert_down = centred(key_of[20], (EXPERTS, FF_E, D), (max(FF_E // 256, 2)) ** -0.5, 2.5, ((0, 8), (1, 4)))
    return {"tokens": tokens, "segments": segments, "routes": routes, "cotangent": cotangent, "gain_attn": gain_attn, "w_query": w_query, "w_key": w_key, "w_value": w_value, "bias_query": bias_query, "bias_key": bias_key, "bias_value": bias_value, "w_out": w_out, "gain_mlp": gain_mlp, "router": router, "mix_gate": mix_gate, "shared_gate": shared_gate, "shared_up": shared_up, "shared_down": shared_down, "expert_gate": expert_gate, "expert_up": expert_up, "expert_down": expert_down}


EPSILON = 1e-06
ROPE_BASE = 1000000.0
PRECISE = lax.Precision.HIGHEST

@jax.custom_vjp
def low(v):
    return lax.optimization_barrier(v.astype(jnp.bfloat16)).astype(jnp.float32)

@jax.custom_vjp
def low_back(v):
    return v

def low_keep(v):
    return (low(v), None)

def low_pass(kept, grad):
    return (grad,)

def back_keep(v):
    return (v, None)

def back_low(kept, grad):
    return (low(grad),)
low.defvjp(low_keep, low_pass)
low_back.defvjp(back_keep, back_low)

def matmul(left, right):
    return jnp.dot(left, right, precision=PRECISE)

def rms_norm(values, gain_vector):
    return values * lax.rsqrt(lax.optimization_barrier(jnp.mean(values * values, axis=-1, keepdims=True)) + EPSILON) * gain_vector

def rope_tables(length, head_width):
    half_size = head_width // 2
    frequency = ROPE_BASE ** (-jnp.arange(half_size, dtype=jnp.float32) * 2.0 / head_width)
    angles = jnp.arange(length, dtype=jnp.float32)[:, None] * frequency[None, :]
    return (jnp.cos(angles)[:, None, :], jnp.sin(angles)[:, None, :])

def rotate(values, cosine, sine_table):
    half_size = values.shape[-1] // 2
    front_half = values[..., :half_size]
    back_half = values[..., half_size:]
    return jnp.concatenate([front_half * cosine - back_half * sine_table, back_half * cosine + front_half * sine_table], axis=-1)

def slot_table(routes, expert_count, capacity):
    flat_routes = routes.reshape(-1)
    one_hot = (flat_routes[:, None] == jnp.arange(expert_count, dtype=jnp.int32)[None, :]).astype(jnp.int32)
    slot_index = (lax.optimization_barrier(jnp.sum(jnp.cumsum(one_hot, axis=0) * one_hot, axis=1)) - 1).astype(jnp.int32)
    destination = (flat_routes * capacity + slot_index).astype(jnp.int32)
    source = (jnp.arange(flat_routes.shape[0], dtype=jnp.int32) // routes.shape[1]).astype(jnp.int32)
    holder = jnp.zeros((expert_count * capacity,), jnp.int32).at[destination].set(source)
    filled = jnp.zeros((expert_count * capacity,), jnp.int32).at[destination].set(1)
    return (destination.reshape(routes.shape), holder, filled)

def attention(query_rot, key_rot, value_rows, segments):
    length = query_rot.shape[0]
    row_block = min(512, length)
    block_count = length // row_block
    position = jnp.arange(length, dtype=jnp.int32)

    def attend_block(block_items):
        query_block, seg_block, pos_block = block_items
        raw_scores = low_back(jnp.einsum('qhd,khd->hqk', query_block, key_rot, precision=PRECISE) * HEAD ** (-0.5))
        allowed = ((seg_block[:, None] == segments[None, :]) & (position[None, :] <= pos_block[:, None]))[None]
        row_max = lax.optimization_barrier(jnp.max(jnp.where(allowed, raw_scores, -jnp.inf), axis=-1, keepdims=True))
        exponent = jnp.exp(jnp.where(allowed, raw_scores - row_max, -jnp.inf))
        probability = exponent / lax.optimization_barrier(jnp.sum(exponent, axis=-1, keepdims=True))
        attended = jnp.einsum('hqk,khd->qhd', low(probability), value_rows, precision=PRECISE)
        return low(low_back(attended))
    attended = lax.map(jax.checkpoint(attend_block), (query_rot.reshape(block_count, row_block, HEADS, HEAD), segments.reshape(block_count, row_block), position.reshape(block_count, row_block)))
    return attended.reshape(length, HEADS * HEAD)

def expert_layer(inputs, expert_gate, expert_up, expert_down):
    slice_width = expert_gate.shape[2] // N_SP
    results = jnp.zeros_like(inputs)
    for slice_index in range(N_SP):
        lower_edge = slice_index * slice_width
        copies = low_back(inputs)
        gate_act = low_back(jnp.einsum('ecd,edf->ecf', copies, expert_gate[:, :, lower_edge:lower_edge + slice_width], precision=PRECISE))
        up_act = low_back(jnp.einsum('ecd,edf->ecf', copies, expert_up[:, :, lower_edge:lower_edge + slice_width], precision=PRECISE))
        activation = low(jax.nn.silu(gate_act) * up_act)
        results = results + low(low_back(jnp.einsum('ecf,efd->ecd', activation, expert_down[:, lower_edge:lower_edge + slice_width, :], precision=PRECISE)))
    return results

def sequence_layer(params, tokens, segments, routes):
    gain_attn, w_query, w_key, w_value, bias_query, bias_key, bias_value, w_out, gain_mlp, router, mix_gate, shared_gate, shared_up, shared_down, expert_gate, expert_up, expert_down = params
    length = tokens.shape[0]
    live_rows = (segments >= 0).astype(jnp.float32)[:, None]
    cosine, sine_table = rope_tables(length, HEAD)
    normed_attn = low(rms_norm(tokens, gain_attn))
    query_rot = low(rotate(low_back(matmul(normed_attn, w_query) + bias_query).reshape(length, HEADS, HEAD), cosine, sine_table))
    key_rot = low(rotate(low_back(matmul(normed_attn, w_key) + bias_key).reshape(length, HEADS, HEAD), cosine, sine_table))
    value_rows = low(low_back(matmul(normed_attn, w_value) + bias_value)).reshape(length, HEADS, HEAD)
    attended = attention(query_rot, key_rot, value_rows, segments)
    hidden = tokens + live_rows * low_back(matmul(attended, w_out))
    normed_mlp = low(rms_norm(hidden, gain_mlp))
    shared_gate_act = low_back(matmul(normed_mlp, shared_gate))
    shared_up_act = low_back(matmul(normed_mlp, shared_up))
    shared_result = low_back(matmul(low(jax.nn.silu(shared_gate_act) * shared_up_act), shared_down))
    switch = jax.nn.sigmoid(matmul(normed_mlp, mix_gate))
    probability = jax.nn.softmax(matmul(normed_mlp, router), axis=-1)
    one_hot = (routes[:, :, None] == jnp.arange(EXPERTS, dtype=jnp.int32)[None, None, :]).astype(jnp.float32)
    gate_weights = lax.optimization_barrier(jnp.sum(probability[:, None, :] * one_hot, axis=-1))
    destination, holder, filled = slot_table(routes, EXPERTS, CAP)
    inputs = jnp.where(filled[:, None] > 0, normed_mlp[holder], 0.0).reshape(EXPERTS, CAP, D)
    results = expert_layer(inputs, expert_gate, expert_up, expert_down).reshape(EXPERTS * CAP, D)
    combined = switch[:, None] * shared_result
    for route_slot in range(TOP):
        combined = combined + gate_weights[:, route_slot:route_slot + 1] * results[destination[:, route_slot]]
    return hidden + live_rows * low_back(combined)

def reference(tokens, segments, routes, cotangent, gain_attn, w_query, w_key, w_value, bias_query, bias_key, bias_value, w_out, gain_mlp, router, mix_gate, shared_gate, shared_up, shared_down, expert_gate, expert_up, expert_down):
    params = tuple((weight.astype(jnp.float32) for weight in (gain_attn, w_query, w_key, w_value, bias_query, bias_key, bias_value, w_out, gain_mlp, router, mix_gate, shared_gate, shared_up, shared_down, expert_gate, expert_up, expert_down)))
    inputs = tokens.astype(jnp.float32).reshape(-1, SEQ, D)
    seg_rows = segments.reshape(-1, SEQ)
    route_rows = routes.reshape(-1, SEQ, TOP)
    layer = jax.checkpoint(sequence_layer)

    def whole_layer(params, inputs):

        def scan_step(carry_in, seq_item):
            return (carry_in, layer(params, seq_item[0], seq_item[1], seq_item[2]))
        return lax.scan(scan_step, jnp.zeros((), jnp.float32), (inputs, seg_rows, route_rows))[1]
    outputs, pull_back = jax.vjp(whole_layer, params, inputs)
    param_grads, input_grads = pull_back(cotangent.astype(jnp.float32).reshape(inputs.shape))
    g_gain_attn, g_query, g_key, g_value, g_bias_query, g_bias_key, g_bias_value, g_out, g_gain_mlp, g_router, g_mix_gate, g_shared_gate, g_shared_up, g_shared_down, g_expert_gate, g_expert_up, g_expert_down = param_grads
    return (outputs.reshape(-1, D).astype(jnp.bfloat16), input_grads.reshape(-1, D), g_gain_attn, g_query, g_key, g_value, g_bias_query, g_bias_key, g_bias_value, g_out, g_gain_mlp, g_router, g_mix_gate, g_shared_gate, g_shared_up, g_shared_down, g_expert_gate, g_expert_up, g_expert_down)
```

```python
import functools

import jax
import jax.numpy as jnp
from jax import lax
from jax.experimental import pallas as pl
from jax.experimental.pallas import tpu as pltpu
from jax.sharding import PartitionSpec as P

HEAD = 128


EPSILON = 1e-06
ROPE_BASE = 1000000.0


def rms_scale(values):
    return lax.rsqrt(jnp.mean(values * values, axis=-1, keepdims=True) + EPSILON)


def norm_back(grad_rows, values, inverse_rms, gain_vector):
    weighted = grad_rows * gain_vector
    return inverse_rms * (
        weighted
        - values * inverse_rms * inverse_rms * jnp.mean(weighted * values, axis=-1, keepdims=True)
    )


def rope_tables(length, head_width):
    half_size = head_width // 2
    frequency = ROPE_BASE ** (-jnp.arange(half_size, dtype=jnp.float32) * 2.0 / head_width)
    angles = jnp.arange(length, dtype=jnp.float32)[:, None] * frequency[None, :]
    return (jnp.cos(angles)[:, None, :], jnp.sin(angles)[:, None, :])


def rotate(values, cosine, sine_table):
    half_size = values.shape[-1] // 2
    front_half = values[..., :half_size]
    back_half = values[..., half_size:]
    return jnp.concatenate(
        [
            front_half * cosine - back_half * sine_table,
            back_half * cosine + front_half * sine_table,
        ],
        axis=-1,
    )


def unrotate(gradient, cosine, sine_table):
    half_size = gradient.shape[-1] // 2
    front_half = gradient[..., :half_size]
    back_half = gradient[..., half_size:]
    return jnp.concatenate(
        [
            front_half * cosine + back_half * sine_table,
            back_half * cosine - front_half * sine_table,
        ],
        axis=-1,
    )


def silu_slope(activation):
    sigmoid_act = jax.nn.sigmoid(activation)
    return sigmoid_act * (1.0 + activation * (1.0 - sigmoid_act))


BF = jnp.bfloat16
F32 = jnp.float32


def dot(left, right):
    return jnp.dot(left, right, preferred_element_type=F32)


def swap(values, axis_name, mask):
    count = lax.axis_size(axis_name)
    return lax.ppermute(values, axis_name, [(i, i ^ mask) for i in range(count)])


def reorder(blocks, place):
    return jnp.stack(
        [lax.dynamic_index_in_dim(blocks, i ^ place, keepdims=False) for i in range(blocks.shape[0])]
    )


def after(value, other):
    return lax.optimization_barrier((value, other))[0]


MESH = pl.DeviceIdType.MESH


def flip(index, mask):
    bit = 1
    while bit <= mask:
        if mask & bit:
            index = index + bit - 2 * bit * lax.rem(lax.div(index, bit), 2)
        bit *= 2
    return index


def sp_bits():
    return ((1, 2), (2, 1))


def greet(barrier_partners):
    barrier = pltpu.get_barrier_semaphore()
    for axis, place in barrier_partners:
        pl.semaphore_signal(barrier, inc=1, device_id={axis: place}, device_id_type=MESH)
    pl.semaphore_wait(barrier, len(barrier_partners))


class Copies:
    def __init__(self, send_sems, recv_sems):
        self.send_sems, self.recv_sems, self.made = send_sems, recv_sems, []

    def start(self, source, target, axis, place):
        number = len(self.made)
        copy = pltpu.make_async_remote_copy(
            src_ref=source,
            dst_ref=target,
            send_sem=self.send_sems.at[number],
            recv_sem=self.recv_sems.at[number],
            device_id={axis: place},
            device_id_type=MESH,
        )
        copy.start()
        self.made.append(copy)
        return copy

    def finish(self):
        for copy in self.made:
            copy.wait_send()


def gather_kernel(pair_count, with_core, x_ref, out_ref, own_sem, send_sems, recv_sems):
    f, s = lax.axis_index("fsdp"), lax.axis_index("sp")
    middle = x_ref.shape[0] // 2
    partners = [("sp", flip(s, 1)), ("sp", flip(s, 2))]
    partners += [("fsdp", flip(f, 1))] if with_core else []
    partners += [("fsdp", flip(f, 2 * k)) for k in range(1, pair_count)]
    greet(partners)
    copies = Copies(send_sems, recv_sems)

    def row(k):
        return flip(f, 2 * k) if with_core else 0

    def block(k, j, h):
        return out_ref.at[row(k), flip(s, j), pl.ds(h * middle, middle)]

    def own(h):
        return x_ref.at[pl.ds(h * middle, middle)]

    local = pltpu.make_async_copy(x_ref, out_ref.at[row(0), s], own_sem)
    local.start()
    distant = {}
    for k in range(1, pair_count):
        for h in range(2):
            distant[k, h] = copies.start(own(h), block(0, 0, h), "fsdp", flip(f, 2 * k))
    near, crossing = {}, []

    def core(k, j, h):
        if with_core:
            source = own(h) if k == 0 and j == 0 else block(k, j, h)
            crossing.append(copies.start(source, block(k, j, h), "fsdp", flip(f, 1)))

    def first(k):
        for h in range(2):
            if k:
                distant[k, h].wait_recv()
            source = own(h) if k == 0 else block(k, 0, h)
            a, b = sp_bits()[h]
            near[k, a, h] = copies.start(source, block(k, 0, h), "sp", flip(s, a))
        for h in range(2):
            source = own(h) if k == 0 else block(k, 0, h)
            a, b = sp_bits()[h]
            near[k, b, h] = copies.start(source, block(k, 0, h), "sp", flip(s, b))
            core(k, 0, h)

    def second(k):
        for h in range(2):
            a, b = sp_bits()[h]
            near[k, a, h].wait_recv()
            near[k, 3, h] = copies.start(block(k, a, h), block(k, a, h), "sp", flip(s, b))
            core(k, a, h)

    def third(k):
        for h in range(2):
            a, b = sp_bits()[h]
            near[k, b, h].wait_recv()
            core(k, b, h)

    def fourth(k):
        for h in range(2):
            near[k, 3, h].wait_recv()
            core(k, 3, h)

    for step in range(pair_count + 2):
        if step < pair_count:
            first(step)
        if 0 <= step - 1 < pair_count:
            second(step - 1)
            third(step - 1)
        if 0 <= step - 2 < pair_count:
            fourth(step - 2)
    local.wait()
    for copy in crossing:
        copy.wait_recv()
    copies.finish()


def gather_call(rows, pair_count, with_core, number):
    height, width = rows.shape
    fsdp_count, sp_count = lax.axis_size("fsdp"), lax.axis_size("sp")
    count = 2 * (pair_count - 1) + 6 * pair_count + (8 * pair_count if with_core else 0)
    outer = fsdp_count if with_core else 1
    return pl.pallas_call(
        functools.partial(gather_kernel, pair_count, with_core),
        out_shape=jax.ShapeDtypeStruct((outer, sp_count, height, width), rows.dtype),
        in_specs=[pl.BlockSpec(memory_space=pl.ANY)],
        out_specs=pl.BlockSpec(memory_space=pl.ANY),
        scratch_shapes=[
            pltpu.SemaphoreType.DMA,
            pltpu.SemaphoreType.DMA((count,)),
            pltpu.SemaphoreType.DMA((count,)),
        ],
        compiler_params=pltpu.CompilerParams(collective_id=number, has_side_effects=True),
    )(rows)


def scatter_kernel(
    pair_count, with_core, p_ref, out_ref, held, loads, came, last, far, load_sems, send_sems, recv_sems
):
    f, s = lax.axis_index("fsdp"), lax.axis_index("sp")
    middle = held.shape[3]
    partners = [("sp", flip(s, 1)), ("sp", flip(s, 2))]
    partners += [("fsdp", flip(f, 1))] if with_core else []
    partners += [("fsdp", flip(f, 2 * k)) for k in range(1, pair_count)]
    greet(partners)
    copies = Copies(send_sems, recv_sems)
    order = list(range(pair_count))[::-1]

    def rows_of(k, h):
        return p_ref.at[flip(f, 2 * k) if with_core else 0, :, pl.ds(h * middle, middle)]

    crossing, loading = {}, {}
    if with_core:
        for k in order:
            for h in range(2):
                source = p_ref.at[flip(flip(f, 2 * k), 1), :, pl.ds(h * middle, middle)]
                crossing[k, h] = copies.start(source, held.at[k, h], "fsdp", flip(f, 1))

    def load(k):
        for h in range(2):
            target = loads.at[k % 2, h] if with_core else held.at[k, h]
            loading[k, h] = pltpu.make_async_copy(rows_of(k, h), target, load_sems.at[k % 2, h])
            loading[k, h].start()

    def add(target, source):
        def body(n, _):
            part = block_of(n, 16)
            target[part, :] = (target[part, :].astype(F32) + source[part, :].astype(F32)).astype(BF)
            return 0

        lax.fori_loop(0, middle // 16, body, 0)

    near, late, distant = {}, {}, {}

    def first(n):
        k = order[n]
        if with_core and n + 1 < pair_count:
            load(order[n + 1])
        for h in range(2):
            loading[k, h].wait()
            a, b = sp_bits()[h]
            if with_core:
                crossing[k, h].wait_recv()
            for i, j in enumerate((a, 3)):
                piece = held.at[k, h, flip(s, j)]
                if with_core:
                    add(piece, loads.at[k % 2, h, flip(s, j)])
                near[k, h, i] = copies.start(piece, came.at[k, h, i], "sp", flip(s, a))
        if with_core:
            for h in range(2):
                a, b = sp_bits()[h]
                for j in (0, b):
                    add(held.at[k, h, flip(s, j)], loads.at[k % 2, h, flip(s, j)])

    def second(n):
        k = order[n]
        for h in range(2):
            a, b = sp_bits()[h]
            near[k, h, 1].wait_recv()
            piece = held.at[k, h, flip(s, b)]
            add(piece, came.at[k, h, 1])
            late[k, h] = copies.start(piece, last.at[k, h], "sp", flip(s, b))
        for h in range(2):
            near[k, h, 0].wait_recv()
            add(held.at[k, h, s], came.at[k, h, 0])

    def third(n):
        k = order[n]
        for h in range(2):
            late[k, h].wait_recv()
            piece = held.at[k, h, s]
            add(piece, last.at[k, h])
            if k:
                distant[k, h] = copies.start(piece, far.at[k - 1, h], "fsdp", flip(f, 2 * k))

    load(order[0])
    for step in range(pair_count + 2):
        if step < pair_count:
            first(step)
        if 0 <= step - 1 < pair_count:
            second(step - 1)
        if 0 <= step - 2 < pair_count:
            third(step - 2)
    for h in range(2):
        for k in range(1, pair_count):
            distant[k, h].wait_recv()

        def total(n, _):
            part = block_of(n, 16)
            value = held[0, h, s, part, :].astype(F32)
            for k in range(1, pair_count):
                value = value + far[k - 1, h, part, :].astype(F32)
            out_ref[pl.ds(pl.multiple_of(h * middle + n * 16, 16), 16), :] = value
            return 0

        lax.fori_loop(0, middle // 16, total, 0)
    copies.finish()


def scatter_call(blocks, pair_count, with_core, number):
    _, sp_count, height, width = blocks.shape
    middle = height // 2
    count = 6 * pair_count + 2 * (pair_count - 1) + (2 * pair_count if with_core else 0)
    used = 2 * pair_count * (sp_count + 3) + (4 * sp_count if with_core else 0) + 2 * pair_count
    return pl.pallas_call(
        functools.partial(scatter_kernel, pair_count, with_core),
        out_shape=jax.ShapeDtypeStruct((height, width), F32),
        in_specs=[pl.BlockSpec(memory_space=pl.ANY)],
        out_specs=pl.BlockSpec(memory_space=pltpu.VMEM),
        scratch_shapes=[
            pltpu.VMEM((pair_count, 2, sp_count, middle, width), BF),
            pltpu.VMEM((2, 2, sp_count if with_core else 1, middle if with_core else 16, width), BF),
            pltpu.VMEM((pair_count, 2, 2, middle, width), BF),
            pltpu.VMEM((pair_count, 2, middle, width), BF),
            pltpu.VMEM((max(pair_count - 1, 1), 2, middle if pair_count > 1 else 16, width), BF),
            pltpu.SemaphoreType.DMA((2, 2)),
            pltpu.SemaphoreType.DMA((count,)),
            pltpu.SemaphoreType.DMA((count,)),
        ],
        compiler_params=pltpu.CompilerParams(
            collective_id=number,
            has_side_effects=True,
            vmem_limit_bytes=min(60 * 1024 * 1024, (2 * used * middle + 4 * height) * width + (8 << 20)),
        ),
    )(blocks)


def nt_dot(left, right):
    return lax.dot_general(left, right, (((1,), (1,)), ((), ())), preferred_element_type=F32)


def silu_pair(values):
    gate = jax.nn.sigmoid(values)
    return values * gate, gate * (1.0 + values * (1.0 - gate))


def block_of(index, size):
    return pl.ds(pl.multiple_of(index * size, size), size)


def moe_kernel(
    hidden,
    expert_count,
    share,
    x_ref,
    dm_ref,
    slot_ref,
    col_ref,
    own_ref,
    wgu_ref,
    wd_ref,
    sgu_ref,
    sd_ref,
    mixer_ref,
    dout_ref,
    rows_ref,
    drows_ref,
    act_ref,
    dgu_ref,
    sact_ref,
    dsgu_ref,
    pick,
    gu,
    y_all,
    dx_all,
    put,
    sgu,
):
    step = pl.program_id(1)
    experts, width, both = wgu_ref.shape
    hp = both // 2
    shared_pad = sd_ref.shape[0]
    capacity = pick.shape[0]
    length = x_ref.shape[1]
    tile = 512
    span = 64
    low = hidden // 128 * 128

    @pl.when(step < experts)
    def _():
        e = step
        slots = lax.broadcasted_iota(jnp.int32, (capacity, length), 0)
        pick[...] = jnp.where(slot_ref[0, pl.ds(e, 1), :] == slots, 1.0, 0.0).astype(BF)

        def take(n, _):
            cols = block_of(n, tile)
            rows_ref[0, 0, :, cols] = dot(pick[...], x_ref[0, :, cols]).astype(BF)
            drows_ref[0, 0, :, cols] = dot(pick[...], dm_ref[0, :, cols]).astype(BF)
            return 0

        lax.fori_loop(0, width // tile, take, 0)
        gu[:, : 2 * hp] = dot(rows_ref[0, 0], wgu_ref[e])
        gu[:, 2 * hp :] = nt_dot(drows_ref[0, 0], wd_ref[e])

        def middle(n, _):
            part = block_of(n, span)
            g, u, d = gu[part, :hp], gu[part, hp : 2 * hp], gu[part, 2 * hp :]
            lane = lax.broadcasted_iota(jnp.int32, (span, 128), 1) + low
            inside = (lane >= hidden) & (lane < hidden + expert_count)
            logits = jnp.where(inside, g[:, low : low + 128], -1e30)
            exponent = jnp.exp(logits - jnp.max(logits, axis=-1, keepdims=True))
            prob = exponent / jnp.sum(exponent, axis=-1, keepdims=True)
            own = own_ref[pl.ds(e, 1), :]
            gate = jnp.sum(prob * own, axis=-1, keepdims=True)
            s, slope = silu_pair(g)
            scaled = gate * (s * u)
            act_ref[0, 0, part, :] = scaled.astype(BF)
            pull = jnp.sum(scaled * d, axis=-1, keepdims=True)
            d = d * gate
            dg = d * u * slope
            extra = pull * jnp.where(inside, own - prob, 0.0)
            dgu_ref[0, 0, part, :hp] = dg.astype(BF)
            dgu_ref[0, 0, part, low : low + 128] = (dg[:, low : low + 128] + extra).astype(BF)
            dgu_ref[0, 0, part, hp:] = (d * s).astype(BF)
            return 0

        lax.fori_loop(0, capacity // span, middle, 0)
        place = block_of(e, capacity)

        def back(n, _):
            cols = block_of(n, tile)
            y_all[place, cols] = dot(act_ref[0, 0], wd_ref[e, :, cols]).astype(BF)
            dx_all[place, cols] = nt_dot(dgu_ref[0, 0], wgu_ref[e, cols, :]).astype(BF)
            return 0

        lax.fori_loop(0, width // tile, back, 0)

    @pl.when(step >= experts)
    def _():
        rows = mixer_ref.shape[1]
        here = block_of(step - experts, rows)
        slots = lax.broadcasted_iota(jnp.int32, (rows, capacity), 1)
        for e in range(experts):
            put[:, e * capacity : (e + 1) * capacity] = jnp.where(
                col_ref[0, :, e : e + 1] == slots, 1.0, 0.0
            ).astype(BF)
        sgu[:, : 2 * shared_pad] = dot(x_ref[0, here, :], sgu_ref[...])
        sgu[:, 2 * shared_pad :] = nt_dot(dm_ref[0, here, :], sd_ref[...])

        def middle(n, _):
            part = block_of(n, span)
            g, u = sgu[part, :shared_pad], sgu[part, shared_pad : 2 * shared_pad]
            d = sgu[part, 2 * shared_pad :]
            mixing = lax.broadcasted_iota(jnp.int32, (span, shared_pad), 1) == share
            switch = jax.nn.sigmoid(
                jnp.sum(jnp.where(mixing, g, 0.0), axis=-1, keepdims=True)
            )
            s, slope = silu_pair(g)
            scaled = switch * (s * u)
            sact_ref[0, part, :] = scaled.astype(BF)
            pull = jnp.sum(scaled * d, axis=-1, keepdims=True) * (1.0 - switch)
            d = d * switch
            dsgu_ref[0, part, :shared_pad] = jnp.where(mixing, pull, d * u * slope).astype(BF)
            dsgu_ref[0, part, shared_pad:] = (d * s).astype(BF)
            return 0

        lax.fori_loop(0, rows // span, middle, 0)

        def finish(n, _):
            cols = block_of(n, tile)
            mixer_ref[0, :, cols] = (
                dot(put[...], y_all[:, cols]) + dot(sact_ref[0], sd_ref[:, cols])
            ).astype(BF)
            dout_ref[0, :, cols] = (
                dot(put[...], dx_all[:, cols]) + nt_dot(dsgu_ref[0], sgu_ref[cols, :])
            ).astype(BF)
            return 0

        lax.fori_loop(0, width // tile, finish, 0)


def moe_call(rows, d_rows, codes, own, weights, sizes):
    hidden, expert_count, share, capacity = sizes
    wide_gu, wide_down, shared_gu, shared_down = weights
    seqs, length, width = rows.shape
    experts, _, both = wide_gu.shape
    hp = both // 2
    shared_pad = shared_down.shape[0]
    token_rows = min(512, length)
    token_steps = length // token_rows
    last = experts - 1

    def fixed(array):
        return pl.BlockSpec(
            array.shape, lambda s, i: (0,) * array.ndim, pipeline_mode=pl.Buffered(1)
        )

    def token_block(columns):
        return pl.BlockSpec(
            (1, token_rows, columns), lambda s, i: (s, jnp.maximum(i - experts, 0), 0)
        )

    def slot_block(columns):
        return pl.BlockSpec(
            (1, 1, capacity, columns), lambda s, i: (jnp.minimum(i, last), s, 0, 0)
        )

    def token_out(columns):
        return jax.ShapeDtypeStruct((seqs, length, columns), BF)

    def slot_out(columns):
        return jax.ShapeDtypeStruct((experts, seqs, capacity, columns), BF)

    slots = experts * capacity
    flops = seqs * 2 * (
        slots * width * (2 * length + 3 * both) + length * width * (2 * slots + 6 * shared_pad)
    )
    return pl.pallas_call(
        functools.partial(moe_kernel, hidden, expert_count, share),
        grid=(seqs, experts + token_steps),
        in_specs=[
            pl.BlockSpec((1, length, width), lambda s, i: (s, 0, 0)),
            pl.BlockSpec((1, length, width), lambda s, i: (s, 0, 0)),
            pl.BlockSpec((1, experts, length), lambda s, i: (s, 0, 0)),
            token_block(experts),
            fixed(own),
            fixed(wide_gu),
            fixed(wide_down),
            fixed(shared_gu),
            fixed(shared_down),
        ],
        out_specs=[
            token_block(width),
            token_block(width),
            slot_block(width),
            slot_block(width),
            slot_block(hp),
            slot_block(both),
            token_block(shared_pad),
            token_block(2 * shared_pad),
        ],
        out_shape=[
            token_out(width),
            token_out(width),
            slot_out(width),
            slot_out(width),
            slot_out(hp),
            slot_out(both),
            token_out(shared_pad),
            token_out(2 * shared_pad),
        ],
        scratch_shapes=[
            pltpu.VMEM((capacity, length), BF),
            pltpu.VMEM((capacity, 3 * hp), F32),
            pltpu.VMEM((slots, width), BF),
            pltpu.VMEM((slots, width), BF),
            pltpu.VMEM((token_rows, slots), BF),
            pltpu.VMEM((token_rows, 3 * shared_pad), F32),
        ],
        compiler_params=pltpu.CompilerParams(
            dimension_semantics=("arbitrary", "arbitrary"), vmem_limit_bytes=60 * 1024 * 1024
        ),
        cost_estimate=pl.CostEstimate(
            flops=flops, bytes_accessed=seqs * 24 * length * width, transcendentals=0
        ),
    )(rows, d_rows, codes, codes.transpose(0, 2, 1), own, *weights)


def moe_grads(rows, d_rows, slot_rows, slot_d_rows, act, d_gu, s_act, d_sgu):
    def flat(array):
        return array.reshape(array.shape[0], -1, array.shape[-1])

    def tokens_of(array):
        return array.reshape(-1, array.shape[-1])

    return (
        jnp.einsum("ecd,ecf->edf", flat(slot_rows), flat(d_gu), preferred_element_type=F32),
        jnp.einsum("ecf,ecd->efd", flat(act), flat(slot_d_rows), preferred_element_type=F32),
        dot(tokens_of(rows).T, tokens_of(d_sgu)),
        dot(tokens_of(d_rows).T, tokens_of(s_act)),
    )


def pad_last(array, size):
    return jnp.pad(array, [(0, 0)] * (array.ndim - 1) + [(0, size - array.shape[-1])])


def round_up(value, unit):
    return -(-value // unit) * unit


def local(
    tokens,
    segments,
    routes,
    cotangent,
    gain_attn,
    w_query,
    w_key,
    w_value,
    bias_query,
    bias_key,
    bias_value,
    w_out,
    gain_mlp,
    router,
    mix_gate,
    shared_gate,
    shared_up,
    shared_down,
    expert_gate,
    expert_up,
    expert_down,
):
    fsdp_count = lax.axis_size("fsdp")
    sp_count = lax.axis_size("sp")
    sp_place = lax.axis_index("sp")
    fsdp_place = lax.axis_index("fsdp")
    pair_count = fsdp_count // 2
    tok_count = tokens.shape[0]
    seq_len = segments.shape[0]
    width = tokens.shape[1]
    top_count = routes.shape[1]
    expert_count = router.shape[1]
    local_experts = expert_gate.shape[0]
    capacity = 3 * seq_len * top_count // (2 * expert_count)
    local_heads = w_query.shape[1] // HEAD
    head_width = w_query.shape[1]
    row_block = min(512, seq_len)
    block_count = seq_len // row_block
    score_scale = HEAD ** (-0.5)
    own_segments = lax.dynamic_slice_in_dim(segments, sp_place * tok_count, tok_count)
    live_rows = (own_segments >= 0).astype(F32)[:, None]
    position = jnp.arange(seq_len, dtype=jnp.int32)
    cosine, sine_table = rope_tables(seq_len, HEAD)
    whole_axes = ("fsdp", "sp")
    own_kernels = sp_count == 4 and pair_count == 4

    def spread(local_rows, number):
        if not own_kernels:
            return lax.all_gather(local_rows, "sp", axis=0, tiled=True)
        return gather_call(local_rows, 1, False, number).reshape(seq_len, width)

    def collect(partial_rows, number):
        partial_rows = partial_rows.astype(BF)
        if not own_kernels:
            rows = lax.psum_scatter(partial_rows, "sp", scatter_dimension=0, tiled=True)
            return rows.astype(F32)
        blocks = partial_rows.reshape(1, sp_count, tok_count, width)
        return scatter_call(blocks, 1, False, number)

    def home(parts, number):
        return scatter_call(
            parts.reshape(fsdp_count, sp_count, tok_count, width), pair_count, True, number
        )

    inputs = tokens.astype(F32)
    attn_rms = rms_scale(inputs)
    gain_one = gain_attn.astype(F32)
    normed_attn = spread((inputs * attn_rms * gain_one).astype(BF), 1)
    full_qkv = lax.all_gather(
        jnp.concatenate([w_query, w_key, w_value], 1), "fsdp", axis=0, tiled=True
    )
    full_out = lax.all_gather(after(w_out, full_qkv), "fsdp", axis=1, tiled=True)
    upstream = cotangent.astype(F32)
    d_mixer = after((live_rows * upstream).astype(BF), full_out)
    if own_kernels:
        all_d_rows = lax.all_gather(d_mixer, whole_axes, axis=0, tiled=True)
        all_d_rows = all_d_rows.reshape(fsdp_count, seq_len, width)
    share = shared_gate.shape[1] // fsdp_count
    packed = jnp.concatenate(
        [
            shared_gate.reshape(-1, fsdp_count, share),
            shared_up.reshape(-1, fsdp_count, share),
            shared_down.T.reshape(-1, fsdp_count, share),
        ],
        2,
    ).transpose(1, 0, 2)
    packed = lax.all_to_all(
        after(packed, full_qkv), "fsdp", split_axis=0, concat_axis=0, tiled=True
    ).reshape(width, 3 * share)
    hidden_units = expert_gate.shape[2]
    hp = round_up(hidden_units + expert_count, 128)
    shared_pad = round_up(share + 1, 128)
    experts_like = jnp.broadcast_to(router, (local_experts, width, expert_count))
    wide_gu = jnp.concatenate(
        [
            pad_last(jnp.concatenate([expert_gate, experts_like], 2), hp),
            pad_last(expert_up, hp),
        ],
        2,
    )
    wide_down = jnp.pad(expert_down, ((0, 0), (0, hp - hidden_units), (0, 0)))
    shared_gu = jnp.concatenate(
        [
            pad_last(jnp.concatenate([packed[:, :share], mix_gate[:, None]], 1), shared_pad),
            pad_last(packed[:, share : 2 * share], shared_pad),
        ],
        1,
    )
    shared_down_rows = pad_last(packed[:, 2 * share :], shared_pad).T
    all_routes = routes.T[None]
    bit = 1
    while bit < fsdp_count:
        all_routes = jnp.concatenate([all_routes, swap(all_routes, "fsdp", bit)], 0)
        bit *= 2
    all_routes = reorder(all_routes, fsdp_place)
    first_expert = fsdp_place * local_experts
    wanted = first_expert + jnp.arange(local_experts, dtype=jnp.int32)
    named = jnp.any(all_routes[:, None] == wanted[None, :, None, None], axis=2)
    tally = jnp.cumsum(named.astype(jnp.int32), axis=2) - 1
    codes = jnp.where(named, tally, -1)
    lane = jnp.arange(128, dtype=jnp.int32)[None, :] + hidden_units // 128 * 128 - hidden_units
    own = (lane == wanted[:, None]).astype(F32)

    normed_attn = after(normed_attn, (codes, wide_gu, wide_down))
    qkv_lin = dot(normed_attn, full_qkv)
    query_lin = qkv_lin[:, :head_width] + bias_query.astype(F32)
    key_lin = qkv_lin[:, head_width : 2 * head_width] + bias_key.astype(F32)
    value_rows = (
        (qkv_lin[:, 2 * head_width :] + bias_value.astype(F32))
        .astype(BF)
        .reshape(seq_len, local_heads, HEAD)
    )
    query_rot = rotate(query_lin.reshape(seq_len, local_heads, HEAD), cosine, sine_table).astype(BF)
    key_rot = rotate(key_lin.reshape(seq_len, local_heads, HEAD), cosine, sine_table).astype(BF)

    def block_scores(block_index):
        offset = block_index * row_block
        query_block = lax.dynamic_slice_in_dim(query_rot, offset, row_block)
        raw_scores = (
            jnp.einsum("qhd,khd->hqk", query_block, key_rot, preferred_element_type=jnp.float32)
            * score_scale
        )
        seg_block = lax.dynamic_slice_in_dim(segments, offset, row_block)
        pos_block = offset + jnp.arange(row_block, dtype=jnp.int32)
        allowed = (
            (seg_block[:, None] == segments[None, :]) & (position[None, :] <= pos_block[:, None])
        )[None]
        return (query_block, raw_scores, allowed)

    def attend_block(block_index):
        score_parts = block_scores(block_index)
        raw_scores = score_parts[1]
        allowed = score_parts[2]
        row_max = jnp.max(jnp.where(allowed, raw_scores, -jnp.inf), axis=-1, keepdims=True)
        exponent = jnp.exp(jnp.where(allowed, raw_scores - row_max, -jnp.inf))
        row_total = jnp.sum(exponent, axis=-1, keepdims=True)
        probability = (exponent / row_total).astype(jnp.bfloat16)
        attended_block = jnp.einsum(
            "hqk,khd->qhd", probability, value_rows, preferred_element_type=jnp.float32
        ).astype(jnp.bfloat16)
        return (attended_block, (row_max + jnp.log(row_total))[..., 0])

    attended, log_total = lax.map(attend_block, jnp.arange(block_count))
    attended = attended.reshape(seq_len, local_heads * HEAD)
    attn_out = collect(dot(attended, full_out), 2)
    hidden = inputs + live_rows * attn_out
    mlp_rms = rms_scale(hidden)
    gain_two = gain_mlp.astype(F32)
    normed_mlp = (hidden * mlp_rms * gain_two).astype(BF)
    weights = (wide_gu, wide_down, shared_gu, shared_down_rows)
    sizes = (hidden_units, expert_count, share, capacity)
    if own_kernels:
        all_rows = gather_call(normed_mlp, pair_count, True, 3)
        all_rows = all_rows.reshape(fsdp_count, seq_len, width)
        mixer_parts, d_parts, *kept = moe_call(all_rows, all_d_rows, codes, own, weights, sizes)
        d_mlp_own = home(d_parts, 4)
    else:
        seq_rows, seq_d_rows, near_codes = spread(normed_mlp, 3), spread(d_mixer, 4), reorder(codes, fsdp_place)
        mixer_sum = d_sum = jnp.zeros((seq_len, width), F32)
        grads = None
        together = max(1, fsdp_count // 4)
        for start in range(0, fsdp_count, together):
            some = range(start, start + together)
            all_rows = jnp.stack([swap(seq_rows, "fsdp", m) for m in some])
            all_d_rows = jnp.stack([swap(seq_d_rows, "fsdp", m) for m in some])
            mixer_parts, d_parts, *kept = moe_call(
                all_rows, all_d_rows, near_codes[start : start + together], own, weights, sizes
            )
            more = moe_grads(all_rows, all_d_rows, *kept)
            grads = more if grads is None else jax.tree.map(jnp.add, grads, more)
            for n, m in enumerate(some):
                mixer_sum = mixer_sum + swap(mixer_parts[n], "fsdp", m).astype(F32)
                d_sum = d_sum + swap(d_parts[n], "fsdp", m).astype(F32)
            grads, mixer_sum, d_sum, seq_rows = lax.optimization_barrier(
                (grads, mixer_sum, d_sum, seq_rows)
            )
        mixer_out, d_mlp_own = collect(mixer_sum, 7), collect(d_sum, 8)
    grad_gain_two = jnp.sum(d_mlp_own * hidden * mlp_rms, axis=0)
    d_hidden = upstream + norm_back(d_mlp_own, hidden, mlp_rms, gain_two)
    d_attn = spread((live_rows * d_hidden).astype(BF), 5)
    grad_out = dot(attended.T, d_attn)
    d_attended = dot(d_attn, full_out.T).astype(BF).reshape(seq_len, local_heads, HEAD)

    def attend_back(carry_in, block_index):
        key_grad, value_grad = carry_in
        query_block, raw_scores, allowed = block_scores(block_index)
        offset = block_index * row_block
        log_block = lax.dynamic_index_in_dim(log_total, block_index, keepdims=False)
        prob_full = jnp.exp(jnp.where(allowed, raw_scores - log_block[..., None], -jnp.inf))
        prob_low = prob_full.astype(jnp.bfloat16)
        grad_block = lax.dynamic_slice_in_dim(d_attended, offset, row_block)
        d_prob = jnp.einsum(
            "qhd,khd->hqk", grad_block, value_rows, preferred_element_type=jnp.float32
        )
        d_scores = (
            prob_full * (d_prob - jnp.sum(prob_full * d_prob, axis=-1, keepdims=True))
        ).astype(jnp.bfloat16)
        query_grad = (
            jnp.einsum("hqk,khd->qhd", d_scores, key_rot, preferred_element_type=jnp.float32)
            * score_scale
        )
        key_grad = (
            key_grad
            + jnp.einsum("hqk,qhd->khd", d_scores, query_block, preferred_element_type=jnp.float32)
            * score_scale
        )
        value_grad = value_grad + jnp.einsum(
            "hqk,qhd->khd", prob_low, grad_block, preferred_element_type=jnp.float32
        )
        return ((key_grad, value_grad), query_grad)

    zero_grad = jnp.zeros((seq_len, local_heads, HEAD), jnp.float32)
    (key_grad, value_grad), query_grad = lax.scan(
        attend_back, (zero_grad, zero_grad), jnp.arange(block_count)
    )
    query_grad = query_grad.reshape(seq_len, local_heads, HEAD)
    d_query = (
        unrotate(query_grad, cosine, sine_table)
        .reshape(seq_len, local_heads * HEAD)
        .astype(jnp.bfloat16)
    )
    d_key = (
        unrotate(key_grad, cosine, sine_table)
        .reshape(seq_len, local_heads * HEAD)
        .astype(jnp.bfloat16)
    )
    d_value = value_grad.reshape(seq_len, local_heads * HEAD).astype(jnp.bfloat16)
    d_qkv = jnp.concatenate([d_query, d_key, d_value], 1)
    d_normed_attn = dot(d_qkv, full_qkv.T)
    d_attn_own = collect(d_normed_attn, 6)
    grad_qkv = dot(normed_attn.T, d_qkv)
    bias_grads = jnp.sum(d_qkv.astype(F32), axis=0)
    grad_gain_one = jnp.sum(d_attn_own * inputs * attn_rms, axis=0)
    grad_tokens = d_hidden + norm_back(d_attn_own, inputs, attn_rms, gain_one)
    grad_qkv = lax.psum_scatter(
        grad_qkv.astype(BF), "fsdp", scatter_dimension=0, tiled=True
    ).astype(F32)
    grad_w_out = lax.psum_scatter(
        grad_out.astype(BF), "fsdp", scatter_dimension=1, tiled=True
    ).astype(F32)
    if own_kernels:
        mixer_out = home(after(mixer_parts, d_attn_own), 7)
        grads = moe_grads(all_rows, all_d_rows, *kept)
    output = (hidden + live_rows * mixer_out).astype(BF)
    grad_gu, grad_ed, grad_sgu, grad_sdown_t = grads
    grad_sdown_t = grad_sdown_t[:, :share]
    grad_expert_gate = grad_gu[..., :hidden_units]
    grad_expert_up = grad_gu[..., hp : hp + hidden_units]
    grad_expert_down = grad_ed[:, :hidden_units]
    grad_router = jnp.sum(grad_gu[..., hidden_units : hidden_units + expert_count], axis=0)
    grad_mix = grad_sgu[:, share]
    packed_grad = jnp.concatenate(
        [grad_sgu[:, :share], grad_sgu[:, shared_pad : shared_pad + share], grad_sdown_t], 1
    ).astype(BF)
    packed_grad = lax.all_to_all(
        packed_grad.reshape(fsdp_count, -1, 3 * share), "fsdp", split_axis=0, concat_axis=0, tiled=True
    ).transpose(1, 0, 2)
    grad_shared_gate, grad_shared_up, grad_shared_down = (
        packed_grad[:, :, n * share : (n + 1) * share].reshape(-1, fsdp_count * share).astype(F32)
        for n in range(3)
    )
    sum_router, sum_mix, sum_gain_two = lax.psum((grad_router, grad_mix, grad_gain_two), whole_axes)
    sum_gain_one = lax.psum(grad_gain_one, whole_axes)
    own_bias = lax.psum(bias_grads, "fsdp")
    return (
        output,
        grad_tokens,
        sum_gain_one,
        grad_qkv[:, :head_width],
        grad_qkv[:, head_width : 2 * head_width],
        grad_qkv[:, 2 * head_width :],
        own_bias[:head_width],
        own_bias[head_width : 2 * head_width],
        own_bias[2 * head_width :],
        grad_w_out,
        sum_gain_two,
        sum_router,
        sum_mix,
        grad_shared_gate,
        grad_shared_up,
        grad_shared_down.T,
        grad_expert_gate,
        grad_expert_up,
        grad_expert_down,
    )


def solution(mesh):
    return jax.shard_map(
        local,
        mesh=mesh,
        in_specs=(
            P(("fsdp", "sp"), None),
            P("fsdp"),
            P("fsdp", None),
            P(("fsdp", "sp"), None),
            P(),
            P("fsdp", "sp"),
            P("fsdp", "sp"),
            P("fsdp", "sp"),
            P("sp"),
            P("sp"),
            P("sp"),
            P("sp", "fsdp"),
            P(),
            P(),
            P(),
            P("fsdp", "sp"),
            P("fsdp", "sp"),
            P("sp", "fsdp"),
            P("fsdp", None, "sp"),
            P("fsdp", None, "sp"),
            P("fsdp", "sp", None),
        ),
        out_specs=(
            P(("fsdp", "sp"), None),
            P(("fsdp", "sp"), None),
            P(),
            P("fsdp", "sp"),
            P("fsdp", "sp"),
            P("fsdp", "sp"),
            P("sp"),
            P("sp"),
            P("sp"),
            P("sp", "fsdp"),
            P(),
            P(),
            P(),
            P("fsdp", "sp"),
            P("fsdp", "sp"),
            P("sp", "fsdp"),
            P("fsdp", None, "sp"),
            P("fsdp", None, "sp"),
            P("fsdp", "sp", None),
        ),
        check_vma=False,
    )
```

```python
import functools

import jax
import jax.numpy as jnp
from jax import lax
from jax.experimental import pallas as pl
from jax.experimental.pallas import tpu as pltpu
from jax.sharding import PartitionSpec as P

HEAD = 128


EPSILON = 1e-06
ROPE_BASE = 1000000.0


def rms_scale(values):
    return lax.rsqrt(jnp.mean(values * values, axis=-1, keepdims=True) + EPSILON)


def norm_back(grad_rows, values, inverse_rms, gain_vector):
    weighted = grad_rows * gain_vector
    return inverse_rms * (
        weighted
        - values * inverse_rms * inverse_rms * jnp.mean(weighted * values, axis=-1, keepdims=True)
    )


def rope_tables(length, head_width):
    half_size = head_width // 2
    frequency = ROPE_BASE ** (-jnp.arange(half_size, dtype=jnp.float32) * 2.0 / head_width)
    angles = jnp.arange(length, dtype=jnp.float32)[:, None] * frequency[None, :]
    return (jnp.cos(angles)[:, None, :], jnp.sin(angles)[:, None, :])


def rotate(values, cosine, sine_table):
    half_size = values.shape[-1] // 2
    front_half = values[..., :half_size]
    back_half = values[..., half_size:]
    return jnp.concatenate(
        [
            front_half * cosine - back_half * sine_table,
            back_half * cosine + front_half * sine_table,
        ],
        axis=-1,
    )


def unrotate(gradient, cosine, sine_table):
    half_size = gradient.shape[-1] // 2
    front_half = gradient[..., :half_size]
    back_half = gradient[..., half_size:]
    return jnp.concatenate(
        [
            front_half * cosine + back_half * sine_table,
            back_half * cosine - front_half * sine_table,
        ],
        axis=-1,
    )


def silu_slope(activation):
    sigmoid_act = jax.nn.sigmoid(activation)
    return sigmoid_act * (1.0 + activation * (1.0 - sigmoid_act))


BF = jnp.bfloat16
F32 = jnp.float32


def dot(left, right):
    return jnp.dot(left, right, preferred_element_type=F32)


def swap(values, axis_name, mask):
    count = lax.axis_size(axis_name)
    return lax.ppermute(values, axis_name, [(i, i ^ mask) for i in range(count)])


def add_low(left, right):
    return (left.astype(F32) + right.astype(F32)).astype(BF)


def reorder(blocks, place):
    return jnp.stack(
        [lax.dynamic_index_in_dim(blocks, i ^ place, keepdims=False) for i in range(blocks.shape[0])]
    )


def after(value, other):
    return lax.optimization_barrier((value, other))[0]


MESH = pl.DeviceIdType.MESH


def flip(index, mask):
    bit = 1
    while bit <= mask:
        if mask & bit:
            index = index + bit - 2 * bit * lax.rem(lax.div(index, bit), 2)
        bit *= 2
    return index


def sp_bits():
    return ((1, 2), (2, 1))


def greet(barrier_partners):
    barrier = pltpu.get_barrier_semaphore()
    for axis, place in barrier_partners:
        pl.semaphore_signal(barrier, inc=1, device_id={axis: place}, device_id_type=MESH)
    pl.semaphore_wait(barrier, len(barrier_partners))


class Copies:
    def __init__(self, send_sems, recv_sems):
        self.send_sems, self.recv_sems, self.made = send_sems, recv_sems, []

    def start(self, source, target, axis, place):
        number = len(self.made)
        copy = pltpu.make_async_remote_copy(
            src_ref=source,
            dst_ref=target,
            send_sem=self.send_sems.at[number],
            recv_sem=self.recv_sems.at[number],
            device_id={axis: place},
            device_id_type=MESH,
        )
        copy.start()
        self.made.append(copy)
        return copy

    def finish(self):
        for copy in self.made:
            copy.wait_send()


def gather_kernel(count, *refs):
    given, made = refs[:count], refs[count : 2 * count]
    bounce, own_sems, send_sems, recv_sems = refs[2 * count :]
    s = lax.axis_index("sp")
    height = given[0].shape[0]
    middle = height // 2
    greet([("sp", flip(s, 1)), ("sp", flip(s, 2))])
    copies = Copies(send_sems, recv_sems)

    def block(t, j, h):
        start = pl.multiple_of(flip(s, j) * height + h * middle, middle)
        return made[t].at[pl.ds(start, middle)]

    local, near = [], {}
    for t in range(count):
        target = made[t].at[pl.ds(pl.multiple_of(s * height, height), height)]
        pltpu.make_async_copy(given[t], bounce.at[t], own_sems.at[t]).start()
        local.append(pltpu.make_async_copy(bounce.at[t], target, own_sems.at[t]))
        for turn in range(2):
            for h in range(2):
                bit = sp_bits()[h][turn]
                source = given[t].at[pl.ds(h * middle, middle)]
                near[t, h, bit] = copies.start(source, block(t, 0, h), "sp", flip(s, bit))
    for t in range(count):
        pltpu.make_async_copy(given[t], bounce.at[t], own_sems.at[t]).wait()
        local[t].start()
        for h in range(2):
            a, b = sp_bits()[h]
            near[t, h, a].wait_recv()
            near[t, h, 3] = copies.start(block(t, a, h), block(t, a, h), "sp", flip(s, b))
    for t in range(count):
        for h in range(2):
            near[t, h, sp_bits()[h][1]].wait_recv()
            near[t, h, 3].wait_recv()
        local[t].wait()
    copies.finish()


def gather_call(arrays, number):
    height, width = arrays[0].shape
    count, sp_count = len(arrays), lax.axis_size("sp")
    whole = jax.ShapeDtypeStruct((sp_count * height, width), arrays[0].dtype)
    return pl.pallas_call(
        functools.partial(gather_kernel, count),
        out_shape=[whole] * count,
        in_specs=[pl.BlockSpec(memory_space=pl.ANY)] * count,
        out_specs=[pl.BlockSpec(memory_space=pl.ANY)] * count,
        scratch_shapes=[
            pltpu.VMEM((count, height, width), BF),
            pltpu.SemaphoreType.DMA((count,)),
            pltpu.SemaphoreType.DMA((6 * count,)),
            pltpu.SemaphoreType.DMA((6 * count,)),
        ],
        compiler_params=pltpu.CompilerParams(collective_id=number, has_side_effects=True),
    )(*arrays)


def scatter_kernel(
    pair_count, p_ref, q_ref, out_ref, held, loads, came, last, far, load_sems, send_sems, recv_sems
):
    f, s = lax.axis_index("fsdp"), lax.axis_index("sp")
    middle = held.shape[3]
    partners = [("sp", flip(s, 1)), ("sp", flip(s, 2))]
    partners += [("fsdp", flip(f, 2 * k)) for k in range(1, pair_count)]
    greet(partners)
    copies = Copies(send_sems, recv_sems)
    order = list(range(pair_count))[::-1]

    loading = {}

    def load(k):
        for h in range(2):
            rows = pl.ds(h * middle, middle)
            loading[k, h] = [
                pltpu.make_async_copy(p_ref.at[k, :, rows], held.at[k, h], load_sems.at[k % 2, h, 0])
            ]
            if q_ref is not None:
                loading[k, h].append(
                    pltpu.make_async_copy(
                        q_ref.at[k, :, rows], loads.at[k % 2, h], load_sems.at[k % 2, h, 1]
                    )
                )
            for copy in loading[k, h]:
                copy.start()

    def add(target, source):
        def body(n, _):
            part = block_of(n, 16)
            target[part, :] = (target[part, :].astype(F32) + source[part, :].astype(F32)).astype(BF)
            return 0

        lax.fori_loop(0, middle // 16, body, 0)

    near, late, distant = {}, {}, {}

    def first(n):
        k = order[n]
        if n + 1 < pair_count:
            load(order[n + 1])
        for h in range(2):
            for copy in loading[k, h]:
                copy.wait()
            a, b = sp_bits()[h]
            for i, j in ((1, 3), (0, a)):
                piece = held.at[k, h, flip(s, j)]
                if q_ref is not None:
                    add(piece, loads.at[k % 2, h, flip(s, j)])
                near[k, h, i] = copies.start(piece, came.at[k, h, i], "sp", flip(s, a))
        if q_ref is not None:
            for h in range(2):
                a, b = sp_bits()[h]
                for j in (0, b):
                    add(held.at[k, h, flip(s, j)], loads.at[k % 2, h, flip(s, j)])

    def second(n):
        k = order[n]
        for h in range(2):
            a, b = sp_bits()[h]
            near[k, h, 1].wait_recv()
            piece = held.at[k, h, flip(s, b)]
            add(piece, came.at[k, h, 1])
            late[k, h] = copies.start(piece, last.at[k, h], "sp", flip(s, b))
        for h in range(2):
            near[k, h, 0].wait_recv()
            add(held.at[k, h, s], came.at[k, h, 0])

    def third(n):
        k = order[n]
        for h in range(2):
            late[k, h].wait_recv()
            piece = held.at[k, h, s]
            add(piece, last.at[k, h])
            if k:
                distant[k, h] = copies.start(piece, far.at[k - 1, h], "fsdp", flip(f, 2 * k))

    load(order[0])
    for step in range(pair_count + 2):
        if step < pair_count:
            first(step)
        if 0 <= step - 1 < pair_count:
            second(step - 1)
        if 0 <= step - 2 < pair_count:
            third(step - 2)
    for h in range(2):
        for k in range(1, pair_count):
            distant[k, h].wait_recv()

        def total(n, _):
            part = block_of(n, 16)
            value = held[0, h, s, part, :].astype(F32)
            for k in range(1, pair_count):
                value = value + far[k - 1, h, part, :].astype(F32)
            out_ref[pl.ds(pl.multiple_of(h * middle + n * 16, 16), 16), :] = value
            return 0

        lax.fori_loop(0, middle // 16, total, 0)
    copies.finish()


def sum_kernel(pair_count, p_ref, *refs):
    scatter_kernel(pair_count, p_ref, None, *refs)


def scatter_call(number, blocks, more=None):
    pair_count, sp_count, height, width = blocks.shape
    middle = height // 2
    count = 6 * pair_count + 2 * (pair_count - 1)
    given = [blocks] if more is None else [blocks, more]
    used = 2 * pair_count * (sp_count + 3) + (4 * sp_count if more is not None else 0) + 2 * pair_count
    return pl.pallas_call(
        functools.partial(sum_kernel if more is None else scatter_kernel, pair_count),
        out_shape=jax.ShapeDtypeStruct((height, width), F32),
        in_specs=[pl.BlockSpec(memory_space=pl.ANY)] * len(given),
        out_specs=pl.BlockSpec(memory_space=pltpu.VMEM),
        scratch_shapes=[
            pltpu.VMEM((pair_count, 2, sp_count, middle, width), BF),
            pltpu.VMEM((2, 2, sp_count, middle, width) if len(given) > 1 else (2, 2, 1, 16, width), BF),
            pltpu.VMEM((pair_count, 2, 2, middle, width), BF),
            pltpu.VMEM((pair_count, 2, middle, width), BF),
            pltpu.VMEM((max(pair_count - 1, 1), 2, middle if pair_count > 1 else 16, width), BF),
            pltpu.SemaphoreType.DMA((2, 2, 2)),
            pltpu.SemaphoreType.DMA((count,)),
            pltpu.SemaphoreType.DMA((count,)),
        ],
        compiler_params=pltpu.CompilerParams(
            collective_id=number,
            has_side_effects=True,
            vmem_limit_bytes=min(60 * 1024 * 1024, (2 * used * middle + 4 * height) * width + (8 << 20)),
        ),
        cost_estimate=pl.CostEstimate(
            flops=0, bytes_accessed=140_000_000 * pair_count, transcendentals=0
        ),
    )(*given)


def nt_dot(left, right):
    return lax.dot_general(left, right, (((1,), (1,)), ((), ())), preferred_element_type=F32)


def silu_pair(values):
    gate = jax.nn.sigmoid(values)
    return values * gate, gate * (1.0 + values * (1.0 - gate))


def block_of(index, size):
    return pl.ds(pl.multiple_of(index * size, size), size)


def moe_kernel(hidden, expert_count, share, x_ref, dm_ref, *refs):
    ins, (mixer_ref, dout_ref), rest = refs[:7], refs[7:9], refs[9:]
    rows, d_rows, out, d_out = x_ref.at[0], dm_ref.at[0], mixer_ref.at[0], dout_ref.at[0]
    moe_step(hidden, expert_count, share, rows, d_rows, *ins, out, d_out, *rest)


def moe_step(
    hidden,
    expert_count,
    share,
    x_ref,
    dm_ref,
    slot_ref,
    col_ref,
    own_ref,
    wgu_ref,
    wd_ref,
    sgu_ref,
    sd_ref,
    mixer_ref,
    dout_ref,
    rows_ref,
    drows_ref,
    act_ref,
    dgu_ref,
    sact_ref,
    dsgu_ref,
    pick,
    gu,
    y_all,
    dx_all,
    put,
    sgu,
):
    step = pl.program_id(1)
    experts, width, both = wgu_ref.shape
    hp = both // 2
    shared_pad = sd_ref.shape[0]
    capacity = pick.shape[0]
    length = x_ref.shape[0]
    tile = 512
    span = 64
    low = hidden // 128 * 128

    @pl.when(step < experts)
    def _():
        e = step
        slots = lax.broadcasted_iota(jnp.int32, (capacity, length), 0)
        pick[...] = jnp.where(slot_ref[0, pl.ds(e, 1), :] == slots, 1.0, 0.0).astype(BF)

        def take(n, _):
            cols = block_of(n, tile)
            rows_ref[0, 0, :, cols] = dot(pick[...], x_ref[:, cols]).astype(BF)
            drows_ref[0, 0, :, cols] = dot(pick[...], dm_ref[:, cols]).astype(BF)
            return 0

        lax.fori_loop(0, width // tile, take, 0)
        gu[:, : 2 * hp] = dot(rows_ref[0, 0], wgu_ref[e])
        gu[:, 2 * hp :] = nt_dot(drows_ref[0, 0], wd_ref[e])

        def middle(n, _):
            part = block_of(n, span)
            g, u, d = gu[part, :hp], gu[part, hp : 2 * hp], gu[part, 2 * hp :]
            lane = lax.broadcasted_iota(jnp.int32, (span, 128), 1) + low
            inside = (lane >= hidden) & (lane < hidden + expert_count)
            logits = jnp.where(inside, g[:, low : low + 128], -1e30)
            exponent = jnp.exp(logits - jnp.max(logits, axis=-1, keepdims=True))
            prob = exponent / jnp.sum(exponent, axis=-1, keepdims=True)
            own = own_ref[pl.ds(e, 1), :]
            gate = jnp.sum(prob * own, axis=-1, keepdims=True)
            s, slope = silu_pair(g)
            scaled = gate * (s * u)
            act_ref[0, 0, part, :] = scaled.astype(BF)
            pull = jnp.sum(scaled * d, axis=-1, keepdims=True)
            d = d * gate
            dg = d * u * slope
            extra = pull * jnp.where(inside, own - prob, 0.0)
            dgu_ref[0, 0, part, :hp] = dg.astype(BF)
            dgu_ref[0, 0, part, low : low + 128] = (dg[:, low : low + 128] + extra).astype(BF)
            dgu_ref[0, 0, part, hp:] = (d * s).astype(BF)
            return 0

        lax.fori_loop(0, capacity // span, middle, 0)
        place = block_of(e, capacity)

        def back(n, _):
            cols = block_of(n, tile)
            y_all[place, cols] = dot(act_ref[0, 0], wd_ref[e, :, cols]).astype(BF)
            dx_all[place, cols] = nt_dot(dgu_ref[0, 0], wgu_ref[e, cols, :]).astype(BF)
            return 0

        lax.fori_loop(0, width // tile, back, 0)

    @pl.when(step >= experts)
    def _():
        rows = mixer_ref.shape[0]
        here = block_of(step - experts, rows)
        slots = lax.broadcasted_iota(jnp.int32, (rows, capacity), 1)
        for e in range(experts):
            put[:, e * capacity : (e + 1) * capacity] = jnp.where(
                col_ref[0, :, e : e + 1] == slots, 1.0, 0.0
            ).astype(BF)
        sgu[:, : 2 * shared_pad] = dot(x_ref[here, :], sgu_ref[...])
        sgu[:, 2 * shared_pad :] = nt_dot(dm_ref[here, :], sd_ref[...])

        def middle(n, _):
            part = block_of(n, span)
            g, u = sgu[part, :shared_pad], sgu[part, shared_pad : 2 * shared_pad]
            d = sgu[part, 2 * shared_pad :]
            mixing = lax.broadcasted_iota(jnp.int32, (span, shared_pad), 1) == share
            switch = jax.nn.sigmoid(
                jnp.sum(jnp.where(mixing, g, 0.0), axis=-1, keepdims=True)
            )
            s, slope = silu_pair(g)
            scaled = switch * (s * u)
            sact_ref[0, part, :] = scaled.astype(BF)
            pull = jnp.sum(scaled * d, axis=-1, keepdims=True) * (1.0 - switch)
            d = d * switch
            dsgu_ref[0, part, :shared_pad] = jnp.where(mixing, pull, d * u * slope).astype(BF)
            dsgu_ref[0, part, shared_pad:] = (d * s).astype(BF)
            return 0

        lax.fori_loop(0, rows // span, middle, 0)

        def finish(n, _):
            cols = block_of(n, tile)
            mixer_ref[:, cols] = (
                dot(put[...], y_all[:, cols]) + dot(sact_ref[0], sd_ref[:, cols])
            ).astype(BF)
            dout_ref[:, cols] = (
                dot(put[...], dx_all[:, cols]) + nt_dot(dsgu_ref[0], sgu_ref[cols, :])
            ).astype(BF)
            return 0

        lax.fori_loop(0, width // tile, finish, 0)


def moe_gather_kernel(hidden, expert_count, share, pair_count, x_own, dm_seq, dm_far, *refs):
    ins, (x_all, dm_all), outs, crossed, rest = refs[:7], refs[7:9], refs[9:11], refs[11:13], refs[13:-11]
    x_buf, dm_buf, m_buf, d_buf, own_sems, load_sems, far_sems, near_sems, core_sems = refs[-11:-2]
    out_sems, cross_sems = refs[-2:]
    m, step = pl.program_id(0), pl.program_id(1)
    steps = pl.num_programs(1)
    f, s = lax.axis_index("fsdp"), lax.axis_index("sp")
    height = x_own.shape[0]
    middle = height // 2
    alls, bufs = (x_all, dm_all), (x_buf, dm_buf)
    both = (0, 1)

    def rows(place):
        return pl.ds(pl.multiple_of(place * height, height), height)

    def half(t, k, place, h):
        start = pl.multiple_of(place * height + h * middle, middle)
        return alls[t].at[2 * k, pl.ds(start, middle)]

    def remote(source, target, sems, at, axis, place):
        return pltpu.make_async_remote_copy(
            src_ref=source,
            dst_ref=target,
            send_sem=sems.at[(0, *at)],
            recv_sem=sems.at[(1, *at)],
            device_id={axis: place},
            device_id_type=MESH,
        )

    def far(k, t=0):
        source = x_own if t == 0 else dm_seq.at[rows(s)]
        return remote(source, alls[t].at[2 * k, rows(s)], far_sems, (k, t), "fsdp", flip(f, 2 * k))

    early = dm_far.shape[0]

    def near(t, k, h, i):
        a, b = sp_bits()[h]
        source = half(t, k, flip(s, a) if i == 2 else s, h)
        return remote(source, source, near_sems, (k, t, 3 * h + i), "sp", flip(s, a if i == 0 else b))

    def core(t, k, j):
        place = rows(flip(s, j))
        target = alls[t].at[2 * k + 1, place]
        return remote(alls[t].at[2 * k, place], target, core_sems, (k, t, j), "fsdp", flip(f, 1))

    def distant(k):
        far(k).start()
        if k > early:
            far(k, 1).start()

    def first(k, tensors):
        if k:
            far(k).wait_recv()
        if k > early:
            far(k, 1).wait_recv()
        for t in tensors:
            for h in range(2):
                near(t, k, h, 0).start()
        if 2 <= k < pair_count - 1:
            distant(k + 1)

    def direct(k, tensors):
        for t in tensors:
            for h in range(2):
                near(t, k, h, 1).start()
            core(t, k, 0).start()

    def second(k, tensors):
        for t in tensors:
            for h in range(2):
                near(t, k, h, 0).wait_recv()
                near(t, k, h, 2).start()

    def third(k, tensors):
        for t in tensors:
            for h in range(2):
                near(t, k, h, 1).wait_recv()
            core(t, k, 1).start()
            core(t, k, 2).start()

    def fourth(k, tensors):
        for t in tensors:
            for h in range(2):
                near(t, k, h, 2).wait_recv()
            core(t, k, 3).start()

    def load(n, t):
        return pltpu.make_async_copy(alls[t].at[n], bufs[t].at[n % 2], load_sems.at[n % 2, t])

    def at_start():
        partners = [("sp", flip(s, 1)), ("sp", flip(s, 2)), ("fsdp", flip(f, 1))]
        partners += [("fsdp", flip(f, 2 * k)) for k in range(1, pair_count)]
        greet(partners)
        moves = [(x_own, x_buf.at[1, pl.ds(0, height)], x_all.at[0, rows(s)])]
        for k in range(1, early + 1):
            piece = dm_buf.at[1, pl.ds((k - 1) * height, height)]
            moves.append((dm_far.at[k - 1], piece, dm_all.at[2 * k, rows(s)]))
        moves.append((dm_seq, dm_buf.at[0], dm_all.at[0]))
        came = [
            pltpu.make_async_copy(source, stop, own_sems.at[n])
            for n, (source, stop, _) in enumerate(moves)
        ]
        left = [
            pltpu.make_async_copy(stop, target, own_sems.at[n])
            for n, (_, stop, target) in enumerate(moves)
        ]
        for copy in came:
            copy.start()
        for n, copy in enumerate(came):
            copy.wait()
            left[n].start()
        left[0].wait()
        first(0, (0,))
        far(1).start()
        direct(0, (0,))
        for copy in left[1:]:
            copy.wait()
        second(0, (0,))
        distant(2)
        for j in range(4):
            core(1, 0, j).start()
        third(0, (0,))
        fourth(0, (0,))
        load(0, 0).start()

    def whole(n):
        if n % 2:
            for t in both:
                for j in range(4):
                    core(t, n // 2, j).wait_recv()
        for t in both:
            load(n, t).start()

    plan = {0: [at_start]}
    for k in range(1, pair_count):
        base = 8 * (k - 1) + (k > 1)
        last = 8 * k - 1
        places = (base - (k == 2), base + 1 - (k == 2), base + 3, last - 2 + (k > 2), last)
        for event, place in zip((first, direct, second, third, fourth), places, strict=True):
            plan.setdefault(place, []).append(functools.partial(event, k, both))
    for n in range(1, 2 * pair_count):
        plan.setdefault(4 * n - 1, []).append(functools.partial(whole, n))
    now = m * steps + step
    for place, events in sorted(plan.items()):

        @pl.when(now == place)
        def _():
            for event in events:
                event()

    for n in range(2 * pair_count):

        @pl.when(now == n * steps)
        def _():
            for t in both if n else (0,):
                load(n, t).wait()

    token_step = step - ins[4].shape[0]
    even, pair = lax.rem(m, 2) == 0, lax.div(m, 2)
    out_bufs = (m_buf, d_buf)
    tile = m_buf.shape[1]
    tile_slot = lax.rem(token_step + 2, 2)

    def stay(t, k, i):
        target = outs[t].at[k, pl.ds(pl.multiple_of(i * tile, tile), tile)]
        slot = lax.rem(i + 2, 2)
        return pltpu.make_async_copy(out_bufs[t].at[slot], target, out_sems.at[t, slot])

    def leave(t, k, i):
        target = crossed[t].at[k, pl.ds(pl.multiple_of(i * tile, tile), tile)]
        source = out_bufs[t].at[lax.rem(i + 2, 2)]
        return remote(source, target, cross_sems, (t, k, i), "fsdp", flip(f, 1))

    @pl.when((token_step >= 0) & even & (m > 0))
    def _():
        for t in both:
            leave(t, pair - 1, token_step).wait_send()

    @pl.when((token_step >= 0) & (~even))
    def _():
        for t in both:
            stay(t, pair, token_step).wait()

    slot = lax.rem(m, 2)
    tiles = m_buf.at[tile_slot], d_buf.at[tile_slot]
    moe_step(hidden, expert_count, share, x_buf.at[slot], dm_buf.at[slot], *ins, *tiles, *rest)

    @pl.when((token_step >= 0) & even)
    def _():
        for t in both:
            stay(t, pair, token_step).start()

    @pl.when((token_step >= 0) & (~even))
    def _():
        for t in both:
            leave(t, pair, token_step).start()

    @pl.when(now == 2 * pair_count * steps - 1)
    def _():
        for k in range(pair_count):
            if k:
                far(k).wait_send()
            if k > early:
                far(k, 1).wait_send()
            for t in both:
                if k or t == 0:
                    for h in range(2):
                        for i in range(3):
                            near(t, k, h, i).wait_send()
                for j in range(4):
                    core(t, k, j).wait_send()
                for i in range(x_buf.shape[1] // tile):
                    if k == pair_count - 1:
                        leave(t, k, i).wait_send()
                    leave(t, k, i).wait_recv()


def moe_call(rows, d_rows, codes, own, weights, sizes, number=None, far_d_rows=None):
    hidden, expert_count, share, capacity = sizes
    wide_gu, wide_down, shared_gu, shared_down = weights
    seqs, _, length = codes.shape
    width = rows.shape[-1]
    pair_count = seqs // 2
    experts, _, both = wide_gu.shape
    hp = both // 2
    shared_pad = shared_down.shape[0]
    token_rows = min(512, length)
    token_steps = length // token_rows
    last = experts - 1

    def fixed(array):
        return pl.BlockSpec(
            array.shape, lambda s, i: (0,) * array.ndim, pipeline_mode=pl.Buffered(1)
        )

    def token_block(columns):
        return pl.BlockSpec(
            (1, token_rows, columns), lambda s, i: (s, jnp.maximum(i - experts, 0), 0)
        )

    def slot_block(columns):
        return pl.BlockSpec(
            (1, 1, capacity, columns), lambda s, i: (jnp.minimum(i, last), s, 0, 0)
        )

    def token_out(columns):
        return jax.ShapeDtypeStruct((seqs, length, columns), BF)

    def slot_out(columns):
        return jax.ShapeDtypeStruct((experts, seqs, capacity, columns), BF)

    slots = experts * capacity
    flops = seqs * 2 * (
        slots * width * (2 * length + 3 * both) + length * width * (2 * slots + 6 * shared_pad)
    )
    if number is None:
        kernel = functools.partial(moe_kernel, hidden, expert_count, share)
        tokens_spec = pl.BlockSpec((1, length, width), lambda s, i: (s, 0, 0))
        sums, sum_specs = [token_out(width)] * 2, [token_block(width)] * 2
        sems, extra = [], []
    else:
        kernel = functools.partial(moe_gather_kernel, hidden, expert_count, share, pair_count)
        tokens_spec = pl.BlockSpec(memory_space=pl.ANY)
        half = jax.ShapeDtypeStruct((pair_count, length, width), BF)
        sums, sum_specs = [token_out(width)] * 2 + [half] * 4, [tokens_spec] * 6
        extra = [far_d_rows]
        sems = [
            pltpu.VMEM((2, length, width), BF),
            pltpu.VMEM((2, length, width), BF),
            pltpu.VMEM((2, token_rows, width), BF),
            pltpu.VMEM((2, token_rows, width), BF),
            pltpu.SemaphoreType.DMA((1 + pair_count,)),
            pltpu.SemaphoreType.DMA((2, 2)),
            pltpu.SemaphoreType.DMA((2, pair_count, 2)),
            pltpu.SemaphoreType.DMA((2, pair_count, 2, 6)),
            pltpu.SemaphoreType.DMA((2, pair_count, 2, 4)),
            pltpu.SemaphoreType.DMA((2, 2)),
            pltpu.SemaphoreType.DMA((2, 2, pair_count, token_steps)),
        ]
    return pl.pallas_call(
        kernel,
        grid=(seqs, experts + token_steps),
        in_specs=[
            tokens_spec,
            tokens_spec,
            *([tokens_spec] * len(extra)),
            pl.BlockSpec((1, experts, length), lambda s, i: (s, 0, 0)),
            token_block(experts),
            fixed(own),
            fixed(wide_gu),
            fixed(wide_down),
            fixed(shared_gu),
            fixed(shared_down),
        ],
        out_specs=[
            *sum_specs,
            slot_block(width),
            slot_block(width),
            slot_block(hp),
            slot_block(both),
            token_block(shared_pad),
            token_block(2 * shared_pad),
        ],
        out_shape=[
            *sums,
            slot_out(width),
            slot_out(width),
            slot_out(hp),
            slot_out(both),
            token_out(shared_pad),
            token_out(2 * shared_pad),
        ],
        scratch_shapes=[
            pltpu.VMEM((capacity, length), BF),
            pltpu.VMEM((capacity, 3 * hp), F32),
            pltpu.VMEM((slots, width), BF),
            pltpu.VMEM((slots, width), BF),
            pltpu.VMEM((token_rows, slots), BF),
            pltpu.VMEM((token_rows, 3 * shared_pad), F32),
            *sems,
        ],
        compiler_params=pltpu.CompilerParams(
            dimension_semantics=("arbitrary", "arbitrary"),
            vmem_limit_bytes=60 * 1024 * 1024,
            collective_id=number,
            has_side_effects=number is not None,
        ),
        cost_estimate=pl.CostEstimate(
            flops=flops, bytes_accessed=seqs * 64 * length * width, transcendentals=0
        ),
    )(rows, d_rows, *extra, codes, codes.transpose(0, 2, 1), own, *weights)


def shared_grads(rows, d_rows, s_act, d_sgu):
    def tokens_of(array):
        return array.reshape(-1, array.shape[-1])

    return (
        dot(tokens_of(rows).T, tokens_of(d_sgu)),
        dot(tokens_of(d_rows).T, tokens_of(s_act)),
    )


def expert_grads(rows, d_rows, act, d_gu):
    def flat(array):
        return array.reshape(array.shape[0], -1, array.shape[-1])

    grad_gu = jnp.einsum("ecd,ecf->edf", flat(rows), flat(d_gu), preferred_element_type=F32)
    act = after(act, grad_gu)
    grad_ed = jnp.einsum("ecf,ecd->efd", flat(act), flat(d_rows), preferred_element_type=F32)
    return grad_gu, grad_ed


def pad_last(array, size):
    return jnp.pad(array, [(0, 0)] * (array.ndim - 1) + [(0, size - array.shape[-1])])


def round_up(value, unit):
    return -(-value // unit) * unit


def local(
    tokens,
    segments,
    routes,
    cotangent,
    gain_attn,
    w_query,
    w_key,
    w_value,
    bias_query,
    bias_key,
    bias_value,
    w_out,
    gain_mlp,
    router,
    mix_gate,
    shared_gate,
    shared_up,
    shared_down,
    expert_gate,
    expert_up,
    expert_down,
):
    fsdp_count = lax.axis_size("fsdp")
    sp_count = lax.axis_size("sp")
    sp_place = lax.axis_index("sp")
    fsdp_place = lax.axis_index("fsdp")
    pair_count = fsdp_count // 2
    tok_count = tokens.shape[0]
    seq_len = segments.shape[0]
    width = tokens.shape[1]
    top_count = routes.shape[1]
    expert_count = router.shape[1]
    local_experts = expert_gate.shape[0]
    capacity = 3 * seq_len * top_count // (2 * expert_count)
    local_heads = w_query.shape[1] // HEAD
    head_width = w_query.shape[1]
    row_block = min(512, seq_len)
    block_count = seq_len // row_block
    score_scale = HEAD ** (-0.5)
    own_segments = lax.dynamic_slice_in_dim(segments, sp_place * tok_count, tok_count)
    live_rows = (own_segments >= 0).astype(F32)[:, None]
    position = jnp.arange(seq_len, dtype=jnp.int32)
    cosine, sine_table = rope_tables(seq_len, HEAD)
    whole_axes = ("fsdp", "sp")
    own_kernels = sp_count == 4 and pair_count == 4

    def spread(local_rows, number):
        if not own_kernels:
            return lax.all_gather(local_rows, "sp", axis=0, tiled=True)
        return gather_call([local_rows], number)[0]

    def collect(partial_rows, number):
        partial_rows = partial_rows.astype(BF)
        if not own_kernels:
            rows = lax.psum_scatter(partial_rows, "sp", scatter_dimension=0, tiled=True)
            return rows.astype(F32)
        blocks = partial_rows.reshape(1, sp_count, tok_count, width)
        return scatter_call(number, blocks)

    orders = sp_bits()

    def slow_start(parts, crossed):
        shape = (pair_count, sp_count, 2, tok_count // 2, width)
        mine, crossed = parts.reshape(shape), crossed.reshape(shape)

        def pick(h, j):
            place = sp_place ^ j
            return add_low(
                lax.dynamic_index_in_dim(mine, place, 1, False)[:, h],
                lax.dynamic_index_in_dim(crossed, place, 1, False)[:, h],
            )

        sent = [jnp.stack([pick(h, orders[h][0]), pick(h, 3)]) for h in range(2)]
        kept = [jnp.stack([pick(h, 0), pick(h, orders[h][1])]) for h in range(2)]
        return sent, kept

    def slow_first(sent):
        return [swap(sent[h], "sp", orders[h][0]) for h in range(2)]

    def slow_second(kept, came):
        kept = [add_low(kept[h], came[h]) for h in range(2)]
        return [kept[h][0] for h in range(2)], [
            swap(kept[h][1], "sp", orders[h][1]) for h in range(2)
        ]

    def slow_third(kept, came):
        rows = jnp.concatenate([add_low(kept[h], came[h]) for h in range(2)], 1)
        rows = reorder(rows, fsdp_place // 2).reshape(pair_count * tok_count, width)
        cores = [[2 * z + c for z in range(pair_count)] for c in range(2)]
        return lax.psum_scatter(
            rows, "fsdp", scatter_dimension=0, axis_index_groups=cores, tiled=True
        )

    inputs = tokens.astype(F32)
    attn_rms = rms_scale(inputs)
    gain_one = gain_attn.astype(F32)
    normed_attn = (inputs * attn_rms * gain_one).astype(BF)
    upstream = cotangent.astype(F32)
    d_mixer = (live_rows * upstream).astype(BF)
    d_mixer_own = d_mixer
    if own_kernels:
        normed_attn, d_mixer = gather_call([normed_attn, d_mixer], 1)
    else:
        normed_attn, d_mixer = spread(normed_attn, 1), spread(d_mixer, 1)
    full_qkv = lax.all_gather(
        jnp.concatenate([w_query, w_key, w_value], 1), "fsdp", axis=0, tiled=True
    )
    full_out_t = lax.all_gather(after(w_out.T, full_qkv), "fsdp", axis=0, tiled=True)
    share = shared_gate.shape[1] // fsdp_count
    packed = jnp.concatenate(
        [
            shared_gate.reshape(-1, fsdp_count, share),
            shared_up.reshape(-1, fsdp_count, share),
            shared_down.T.reshape(-1, fsdp_count, share),
        ],
        2,
    ).transpose(1, 0, 2)
    packed = lax.all_to_all(
        after(packed, full_qkv), "fsdp", split_axis=0, concat_axis=0, tiled=True
    ).reshape(width, 3 * share)
    hidden_units = expert_gate.shape[2]
    hp = round_up(hidden_units + expert_count, 128)
    shared_pad = round_up(share + 1, 128)
    experts_like = jnp.broadcast_to(router, (local_experts, width, expert_count))
    wide_gu = jnp.concatenate(
        [
            pad_last(jnp.concatenate([expert_gate, experts_like], 2), hp),
            pad_last(expert_up, hp),
        ],
        2,
    )
    wide_down = jnp.pad(expert_down, ((0, 0), (0, hp - hidden_units), (0, 0)))
    all_routes = routes.T[None]
    bit = 1
    while bit < fsdp_count:
        all_routes = jnp.concatenate([all_routes, swap(all_routes, "fsdp", bit)], 0)
        bit *= 2
    first_expert = fsdp_place * local_experts
    wanted = first_expert + jnp.arange(local_experts, dtype=jnp.int32)
    named = jnp.any(all_routes[:, None] == wanted[None, :, None, None], axis=2)
    tally = jnp.cumsum(named.astype(jnp.int32), axis=2) - 1
    codes = jnp.where(named, tally, -1)
    lane = jnp.arange(128, dtype=jnp.int32)[None, :] + hidden_units // 128 * 128 - hidden_units
    own = (lane == wanted[:, None]).astype(F32)

    normed_attn = after(normed_attn, (codes, wide_gu, wide_down))
    qkv_lin = dot(normed_attn, full_qkv)
    query_lin = qkv_lin[:, :head_width] + bias_query.astype(F32)
    key_lin = qkv_lin[:, head_width : 2 * head_width] + bias_key.astype(F32)
    value_rows = (
        (qkv_lin[:, 2 * head_width :] + bias_value.astype(F32))
        .astype(BF)
        .reshape(seq_len, local_heads, HEAD)
    )
    query_rot = rotate(query_lin.reshape(seq_len, local_heads, HEAD), cosine, sine_table).astype(BF)
    query_rot, packed = lax.optimization_barrier((query_rot, packed))
    if own_kernels:
        d_mixer_own = after(d_mixer_own, packed)
        d_mixer_far = jnp.stack([swap(d_mixer_own, "fsdp", 2 * k) for k in range(1, 2)])
    shared_gu = jnp.concatenate(
        [
            pad_last(jnp.concatenate([packed[:, :share], mix_gate[:, None]], 1), shared_pad),
            pad_last(packed[:, share : 2 * share], shared_pad),
        ],
        1,
    )
    shared_down_rows = pad_last(packed[:, 2 * share :], shared_pad).T
    key_rot = rotate(key_lin.reshape(seq_len, local_heads, HEAD), cosine, sine_table).astype(BF)

    def block_scores(block_index):
        offset = block_index * row_block
        query_block = lax.dynamic_slice_in_dim(query_rot, offset, row_block)
        raw_scores = (
            jnp.einsum("qhd,khd->hqk", query_block, key_rot, preferred_element_type=jnp.float32)
            * score_scale
        )
        seg_block = lax.dynamic_slice_in_dim(segments, offset, row_block)
        pos_block = offset + jnp.arange(row_block, dtype=jnp.int32)
        allowed = (
            (seg_block[:, None] == segments[None, :]) & (position[None, :] <= pos_block[:, None])
        )[None]
        return (query_block, raw_scores, allowed)

    def attend_block(block_index):
        score_parts = block_scores(block_index)
        raw_scores = score_parts[1]
        allowed = score_parts[2]
        row_max = jnp.max(jnp.where(allowed, raw_scores, -jnp.inf), axis=-1, keepdims=True)
        exponent = jnp.exp(jnp.where(allowed, raw_scores - row_max, -jnp.inf))
        row_total = jnp.sum(exponent, axis=-1, keepdims=True)
        probability = (exponent / row_total).astype(jnp.bfloat16)
        attended_block = jnp.einsum(
            "hqk,khd->qhd", probability, value_rows, preferred_element_type=jnp.float32
        ).astype(jnp.bfloat16)
        return (attended_block, (row_max + jnp.log(row_total))[..., 0])

    attended, log_total = lax.map(attend_block, jnp.arange(block_count))
    attended = attended.reshape(seq_len, local_heads * HEAD)
    attn_out = collect(nt_dot(attended, full_out_t), 2)
    hidden = inputs + live_rows * attn_out
    mlp_rms = rms_scale(hidden)
    gain_two = gain_mlp.astype(F32)
    normed_mlp = (hidden * mlp_rms * gain_two).astype(BF)
    weights = (wide_gu, wide_down, shared_gu, shared_down_rows)
    sizes = (hidden_units, expert_count, share, capacity)
    if own_kernels:
        all_rows, all_d_rows, mixer_parts, d_parts, mixer_crossed, d_crossed, *kept = moe_call(
            normed_mlp, d_mixer, codes, own, weights, sizes, 3, d_mixer_far
        )
        blocks = (pair_count, sp_count, tok_count, width)
        d_mlp_own = scatter_call(4, d_parts.reshape(blocks), d_crossed.reshape(blocks))
    else:
        seq_rows = spread(normed_mlp, 3)
        mixer_sum = d_sum = jnp.zeros((seq_len, width), F32)
        grads = None
        together = max(1, fsdp_count // 4)
        for start in range(0, fsdp_count, together):
            some = range(start, start + together)
            all_rows = jnp.stack([swap(seq_rows, "fsdp", m) for m in some])
            all_d_rows = jnp.stack([swap(d_mixer, "fsdp", m) for m in some])
            mixer_parts, d_parts, *kept = moe_call(
                all_rows, all_d_rows, codes[start : start + together], own, weights, sizes
            )
            more = expert_grads(*kept[:4]) + shared_grads(all_rows, all_d_rows, *kept[4:])
            grads = more if grads is None else jax.tree.map(jnp.add, grads, more)
            for n, m in enumerate(some):
                mixer_sum = mixer_sum + swap(mixer_parts[n], "fsdp", m).astype(F32)
                d_sum = d_sum + swap(d_parts[n], "fsdp", m).astype(F32)
            grads, mixer_sum, d_sum, seq_rows = lax.optimization_barrier(
                (grads, mixer_sum, d_sum, seq_rows)
            )
        mixer_out, d_mlp_own = collect(mixer_sum, 7), collect(d_sum, 8)
    grad_gain_two = jnp.sum(d_mlp_own * hidden * mlp_rms, axis=0)
    d_hidden = upstream + norm_back(d_mlp_own, hidden, mlp_rms, gain_two)
    d_attn = spread((live_rows * d_hidden).astype(BF), 5)
    if own_kernels:
        slow = slow_start(*after((mixer_parts, mixer_crossed), d_mlp_own))
        d_attn, slow = lax.optimization_barrier((d_attn, slow))
        slow = slow[1], slow_first(slow[0])
        grad_out_t = dot(d_attn.T, attended).astype(BF)
        grad_sgu, grad_sdown = shared_grads(
            all_rows, all_d_rows, *after(kept[4:], (d_attn, grad_out_t))
        )
    else:
        grad_out_t = dot(d_attn.T, attended).astype(BF)
        grad_gu, grad_ed, grad_sgu, grad_sdown = grads
    grad_w_out = lax.psum_scatter(
        grad_out_t, "fsdp", scatter_dimension=0, tiled=True
    ).astype(F32)
    packed_grad = jnp.concatenate(
        [
            grad_sgu[:, :share],
            grad_sgu[:, shared_pad : shared_pad + share],
            grad_sdown[:, :share],
        ],
        1,
    ).astype(BF)
    d_attn, packed_grad = lax.optimization_barrier((d_attn, packed_grad))
    packed_grad = lax.all_to_all(
        packed_grad.reshape(fsdp_count, -1, 3 * share), "fsdp", split_axis=0, concat_axis=0, tiled=True
    ).transpose(1, 0, 2)
    d_attended = dot(d_attn, full_out_t).astype(BF).reshape(seq_len, local_heads, HEAD)

    if own_kernels:
        d_attended, slow = lax.optimization_barrier((d_attended, slow))
        slow = slow_second(*slow)

    def attend_back(carry_in, block_index):
        key_grad, value_grad = carry_in
        query_block, raw_scores, allowed = block_scores(block_index)
        offset = block_index * row_block
        log_block = lax.dynamic_index_in_dim(log_total, block_index, keepdims=False)
        prob_full = jnp.exp(jnp.where(allowed, raw_scores - log_block[..., None], -jnp.inf))
        prob_low = prob_full.astype(jnp.bfloat16)
        grad_block = lax.dynamic_slice_in_dim(d_attended, offset, row_block)
        d_prob = jnp.einsum(
            "qhd,khd->hqk", grad_block, value_rows, preferred_element_type=jnp.float32
        )
        d_scores = (
            prob_full * (d_prob - jnp.sum(prob_full * d_prob, axis=-1, keepdims=True))
        ).astype(jnp.bfloat16)
        query_grad = (
            jnp.einsum("hqk,khd->qhd", d_scores, key_rot, preferred_element_type=jnp.float32)
            * score_scale
        )
        key_grad = (
            key_grad
            + jnp.einsum("hqk,qhd->khd", d_scores, query_block, preferred_element_type=jnp.float32)
            * score_scale
        )
        value_grad = value_grad + jnp.einsum(
            "hqk,qhd->khd", prob_low, grad_block, preferred_element_type=jnp.float32
        )
        return ((key_grad, value_grad), query_grad)

    zero_grad = jnp.zeros((seq_len, local_heads, HEAD), jnp.float32)
    (key_grad, value_grad), query_grad = lax.scan(
        attend_back, (zero_grad, zero_grad), jnp.arange(block_count)
    )
    if own_kernels:
        query_grad, slow, packed_grad, grad_w_out = lax.optimization_barrier(
            (query_grad, slow, packed_grad, grad_w_out)
        )
        mixer_out = slow_third(*slow).astype(F32)
    query_grad = query_grad.reshape(seq_len, local_heads, HEAD)
    d_query = (
        unrotate(query_grad, cosine, sine_table)
        .reshape(seq_len, local_heads * HEAD)
        .astype(jnp.bfloat16)
    )
    d_key = (
        unrotate(key_grad, cosine, sine_table)
        .reshape(seq_len, local_heads * HEAD)
        .astype(jnp.bfloat16)
    )
    d_value = value_grad.reshape(seq_len, local_heads * HEAD).astype(jnp.bfloat16)
    d_qkv = jnp.concatenate([d_query, d_key, d_value], 1)
    grad_qkv = dot(normed_attn.T, d_qkv).astype(BF)
    d_normed_attn = dot(after(d_qkv, grad_qkv), full_qkv.T)
    d_attn_own = collect(d_normed_attn, 6)
    bias_grads = jnp.sum(d_qkv.astype(F32), axis=0)
    grad_gain_one = jnp.sum(d_attn_own * inputs * attn_rms, axis=0)
    grad_tokens = d_hidden + norm_back(d_attn_own, inputs, attn_rms, gain_one)
    grad_qkv = lax.psum_scatter(grad_qkv, "fsdp", scatter_dimension=0, tiled=True).astype(F32)
    if own_kernels:
        grad_gu, grad_ed = expert_grads(*after(kept[:4], d_attn_own))
    output = (hidden + live_rows * mixer_out).astype(BF)
    grad_expert_gate = grad_gu[..., :hidden_units]
    grad_expert_up = grad_gu[..., hp : hp + hidden_units]
    grad_expert_down = grad_ed[:, :hidden_units]
    grad_router = jnp.sum(grad_gu[..., hidden_units : hidden_units + expert_count], axis=0)
    grad_mix = grad_sgu[:, share]
    grad_shared_gate, grad_shared_up, grad_shared_down = (
        packed_grad[:, :, n * share : (n + 1) * share].reshape(-1, fsdp_count * share).astype(F32)
        for n in range(3)
    )
    bias_place = lax.dynamic_update_slice(
        jnp.zeros((3, sp_count * head_width), F32), bias_grads.reshape(3, -1), (0, sp_place * head_width)
    )
    small = jnp.concatenate(
        [jnp.stack([grad_gain_one, grad_gain_two, grad_mix]), bias_place, grad_router.T], 0
    )
    for axis_name in ("sp", "fsdp"):
        bit = 1
        while bit < lax.axis_size(axis_name):
            small = small + swap(small, axis_name, bit)
            bit *= 2
    sum_gain_one, sum_gain_two, sum_mix = small[0], small[1], small[2]
    own_bias = lax.dynamic_slice_in_dim(small[3:6], sp_place * head_width, head_width, 1)
    sum_router = small[6:].T
    return (
        output,
        grad_tokens,
        sum_gain_one,
        grad_qkv[:, :head_width],
        grad_qkv[:, head_width : 2 * head_width],
        grad_qkv[:, 2 * head_width :],
        own_bias[0],
        own_bias[1],
        own_bias[2],
        grad_w_out.T,
        sum_gain_two,
        sum_router,
        sum_mix,
        grad_shared_gate,
        grad_shared_up,
        grad_shared_down.T,
        grad_expert_gate,
        grad_expert_up,
        grad_expert_down,
    )


def solution(mesh):
    return jax.shard_map(
        local,
        mesh=mesh,
        in_specs=(
            P(("fsdp", "sp"), None),
            P("fsdp"),
            P("fsdp", None),
            P(("fsdp", "sp"), None),
            P(),
            P("fsdp", "sp"),
            P("fsdp", "sp"),
            P("fsdp", "sp"),
            P("sp"),
            P("sp"),
            P("sp"),
            P("sp", "fsdp"),
            P(),
            P(),
            P(),
            P("fsdp", "sp"),
            P("fsdp", "sp"),
            P("sp", "fsdp"),
            P("fsdp", None, "sp"),
            P("fsdp", None, "sp"),
            P("fsdp", "sp", None),
        ),
        out_specs=(
            P(("fsdp", "sp"), None),
            P(("fsdp", "sp"), None),
            P(),
            P("fsdp", "sp"),
            P("fsdp", "sp"),
            P("fsdp", "sp"),
            P("sp"),
            P("sp"),
            P("sp"),
            P("sp", "fsdp"),
            P(),
            P(),
            P(),
            P("fsdp", "sp"),
            P("fsdp", "sp"),
            P("sp", "fsdp"),
            P("fsdp", None, "sp"),
            P("fsdp", None, "sp"),
            P("fsdp", "sp", None),
        ),
        check_vma=False,
    )
```

```python
import functools

import jax
import jax.numpy as jnp
from jax import lax
from jax.experimental import pallas as pl
from jax.experimental.pallas import tpu as pltpu
from jax.sharding import PartitionSpec as P

HEAD = 128


EPSILON = 1e-06
ROPE_BASE = 1000000.0


def rms_scale(values):
    return lax.rsqrt(jnp.mean(values * values, axis=-1, keepdims=True) + EPSILON)


def norm_back(grad_rows, values, inverse_rms, gain_vector):
    weighted = grad_rows * gain_vector
    return inverse_rms * (
        weighted
        - values * inverse_rms * inverse_rms * jnp.mean(weighted * values, axis=-1, keepdims=True)
    )


def rope_tables(length, head_width):
    half_size = head_width // 2
    frequency = ROPE_BASE ** (-jnp.arange(half_size, dtype=jnp.float32) * 2.0 / head_width)
    angles = jnp.arange(length, dtype=jnp.float32)[:, None] * frequency[None, :]
    return (jnp.cos(angles)[:, None, :], jnp.sin(angles)[:, None, :])


def rotate(values, cosine, sine_table):
    half_size = values.shape[-1] // 2
    front_half = values[..., :half_size]
    back_half = values[..., half_size:]
    return jnp.concatenate(
        [
            front_half * cosine - back_half * sine_table,
            back_half * cosine + front_half * sine_table,
        ],
        axis=-1,
    )


def unrotate(gradient, cosine, sine_table):
    half_size = gradient.shape[-1] // 2
    front_half = gradient[..., :half_size]
    back_half = gradient[..., half_size:]
    return jnp.concatenate(
        [
            front_half * cosine + back_half * sine_table,
            back_half * cosine - front_half * sine_table,
        ],
        axis=-1,
    )


def silu_slope(activation):
    sigmoid_act = jax.nn.sigmoid(activation)
    return sigmoid_act * (1.0 + activation * (1.0 - sigmoid_act))


BF = jnp.bfloat16
F32 = jnp.float32


def dot(left, right):
    return jnp.dot(left, right, preferred_element_type=F32)


def swap(values, axis_name, mask):
    count = lax.axis_size(axis_name)
    return lax.ppermute(values, axis_name, [(i, i ^ mask) for i in range(count)])


def add_low(left, right):
    return (left.astype(F32) + right.astype(F32)).astype(BF)


def reorder(blocks, place):
    return jnp.stack(
        [lax.dynamic_index_in_dim(blocks, i ^ place, keepdims=False) for i in range(blocks.shape[0])]
    )


def after(value, other):
    return lax.optimization_barrier((value, other))[0]


MESH = pl.DeviceIdType.MESH


def flip(index, mask):
    bit = 1
    while bit <= mask:
        if mask & bit:
            index = index + bit - 2 * bit * lax.rem(lax.div(index, bit), 2)
        bit *= 2
    return index


def sp_bits():
    return ((1, 2), (2, 1))


def greet(barrier_partners):
    barrier = pltpu.get_barrier_semaphore()
    for axis, place in barrier_partners:
        pl.semaphore_signal(barrier, inc=1, device_id={axis: place}, device_id_type=MESH)
    pl.semaphore_wait(barrier, len(barrier_partners))


class Copies:
    def __init__(self, send_sems, recv_sems):
        self.send_sems, self.recv_sems, self.made = send_sems, recv_sems, []

    def start(self, source, target, axis, place):
        number = len(self.made)
        copy = pltpu.make_async_remote_copy(
            src_ref=source,
            dst_ref=target,
            send_sem=self.send_sems.at[number],
            recv_sem=self.recv_sems.at[number],
            device_id={axis: place},
            device_id_type=MESH,
        )
        copy.start()
        self.made.append(copy)
        return copy

    def finish(self):
        for copy in self.made:
            copy.wait_send()


def gather_kernel(count, *refs):
    given, made = refs[:count], refs[count : 2 * count]
    bounce, own_sems, send_sems, recv_sems = refs[2 * count :]
    s = lax.axis_index("sp")
    height = given[0].shape[0]
    middle = height // 2
    greet([("sp", flip(s, 1)), ("sp", flip(s, 2))])
    copies = Copies(send_sems, recv_sems)

    def block(t, j, h):
        start = pl.multiple_of(flip(s, j) * height + h * middle, middle)
        return made[t].at[pl.ds(start, middle)]

    local, near = [], {}
    for t in range(count):
        target = made[t].at[pl.ds(pl.multiple_of(s * height, height), height)]
        pltpu.make_async_copy(given[t], bounce.at[t], own_sems.at[t]).start()
        local.append(pltpu.make_async_copy(bounce.at[t], target, own_sems.at[t]))
        for turn in range(2):
            for h in range(2):
                bit = sp_bits()[h][turn]
                source = given[t].at[pl.ds(h * middle, middle)]
                near[t, h, bit] = copies.start(source, block(t, 0, h), "sp", flip(s, bit))
    for t in range(count):
        pltpu.make_async_copy(given[t], bounce.at[t], own_sems.at[t]).wait()
        local[t].start()
        for h in range(2):
            a, b = sp_bits()[h]
            near[t, h, a].wait_recv()
            near[t, h, 3] = copies.start(block(t, a, h), block(t, a, h), "sp", flip(s, b))
    for t in range(count):
        for h in range(2):
            near[t, h, sp_bits()[h][1]].wait_recv()
            near[t, h, 3].wait_recv()
        local[t].wait()
    copies.finish()


def gather_call(arrays, number):
    height, width = arrays[0].shape
    count, sp_count = len(arrays), lax.axis_size("sp")
    whole = jax.ShapeDtypeStruct((sp_count * height, width), arrays[0].dtype)
    return pl.pallas_call(
        functools.partial(gather_kernel, count),
        out_shape=[whole] * count,
        in_specs=[pl.BlockSpec(memory_space=pl.ANY)] * count,
        out_specs=[pl.BlockSpec(memory_space=pl.ANY)] * count,
        scratch_shapes=[
            pltpu.VMEM((count, height, width), BF),
            pltpu.SemaphoreType.DMA((count,)),
            pltpu.SemaphoreType.DMA((6 * count,)),
            pltpu.SemaphoreType.DMA((6 * count,)),
        ],
        compiler_params=pltpu.CompilerParams(collective_id=number, has_side_effects=True),
    )(*arrays)


def scatter_kernel(
    pair_count, p_ref, q_ref, out_ref, held, loads, came, last, far, load_sems, send_sems, recv_sems
):
    f, s = lax.axis_index("fsdp"), lax.axis_index("sp")
    middle = held.shape[3]
    partners = [("sp", flip(s, 1)), ("sp", flip(s, 2))]
    partners += [("fsdp", flip(f, 2 * k)) for k in range(1, pair_count)]
    greet(partners)
    copies = Copies(send_sems, recv_sems)
    order = list(range(pair_count))[::-1]

    loading = {}

    def load(k):
        for h in range(2):
            rows = pl.ds(h * middle, middle)
            loading[k, h] = [
                pltpu.make_async_copy(p_ref.at[k, :, rows], held.at[k, h], load_sems.at[k % 2, h, 0])
            ]
            if q_ref is not None:
                loading[k, h].append(
                    pltpu.make_async_copy(
                        q_ref.at[k, :, rows], loads.at[k % 2, h], load_sems.at[k % 2, h, 1]
                    )
                )
            for copy in loading[k, h]:
                copy.start()

    def add(target, source):
        def body(n, _):
            part = block_of(n, 16)
            target[part, :] = (target[part, :].astype(F32) + source[part, :].astype(F32)).astype(BF)
            return 0

        lax.fori_loop(0, middle // 16, body, 0)

    near, late, distant = {}, {}, {}

    def first(n):
        k = order[n]
        if n + 1 < pair_count:
            load(order[n + 1])
        for h in range(2):
            for copy in loading[k, h]:
                copy.wait()
            a, b = sp_bits()[h]
            for i, j in ((1, 3), (0, a)):
                piece = held.at[k, h, flip(s, j)]
                if q_ref is not None:
                    add(piece, loads.at[k % 2, h, flip(s, j)])
                near[k, h, i] = copies.start(piece, came.at[k, h, i], "sp", flip(s, a))
        if q_ref is not None:
            for h in range(2):
                a, b = sp_bits()[h]
                for j in (0, b):
                    add(held.at[k, h, flip(s, j)], loads.at[k % 2, h, flip(s, j)])

    def second(n):
        k = order[n]
        for h in range(2):
            a, b = sp_bits()[h]
            near[k, h, 1].wait_recv()
            piece = held.at[k, h, flip(s, b)]
            add(piece, came.at[k, h, 1])
            late[k, h] = copies.start(piece, last.at[k, h], "sp", flip(s, b))
        for h in range(2):
            near[k, h, 0].wait_recv()
            add(held.at[k, h, s], came.at[k, h, 0])

    def third(n):
        k = order[n]
        for h in range(2):
            late[k, h].wait_recv()
            piece = held.at[k, h, s]
            add(piece, last.at[k, h])
            if k:
                distant[k, h] = copies.start(piece, far.at[k - 1, h], "fsdp", flip(f, 2 * k))

    load(order[0])
    for step in range(pair_count + 2):
        if step < pair_count:
            first(step)
        if 0 <= step - 1 < pair_count:
            second(step - 1)
        if 0 <= step - 2 < pair_count:
            third(step - 2)
    for h in range(2):
        for k in range(1, pair_count):
            distant[k, h].wait_recv()

        def total(n, _):
            part = block_of(n, 16)
            value = held[0, h, s, part, :].astype(F32)
            for k in range(1, pair_count):
                value = value + far[k - 1, h, part, :].astype(F32)
            out_ref[pl.ds(pl.multiple_of(h * middle + n * 16, 16), 16), :] = value
            return 0

        lax.fori_loop(0, middle // 16, total, 0)
    copies.finish()


def sum_kernel(pair_count, p_ref, *refs):
    scatter_kernel(pair_count, p_ref, None, *refs)


def scatter_call(number, blocks, more=None):
    pair_count, sp_count, height, width = blocks.shape
    middle = height // 2
    count = 6 * pair_count + 2 * (pair_count - 1)
    given = [blocks] if more is None else [blocks, more]
    used = 2 * pair_count * (sp_count + 3) + (4 * sp_count if more is not None else 0) + 2 * pair_count
    return pl.pallas_call(
        functools.partial(sum_kernel if more is None else scatter_kernel, pair_count),
        out_shape=jax.ShapeDtypeStruct((height, width), F32),
        in_specs=[pl.BlockSpec(memory_space=pl.ANY)] * len(given),
        out_specs=pl.BlockSpec(memory_space=pltpu.VMEM),
        scratch_shapes=[
            pltpu.VMEM((pair_count, 2, sp_count, middle, width), BF),
            pltpu.VMEM((2, 2, sp_count, middle, width) if len(given) > 1 else (2, 2, 1, 16, width), BF),
            pltpu.VMEM((pair_count, 2, 2, middle, width), BF),
            pltpu.VMEM((pair_count, 2, middle, width), BF),
            pltpu.VMEM((max(pair_count - 1, 1), 2, middle if pair_count > 1 else 16, width), BF),
            pltpu.SemaphoreType.DMA((2, 2, 2)),
            pltpu.SemaphoreType.DMA((count,)),
            pltpu.SemaphoreType.DMA((count,)),
        ],
        compiler_params=pltpu.CompilerParams(
            collective_id=number,
            has_side_effects=True,
            vmem_limit_bytes=min(60 * 1024 * 1024, (2 * used * middle + 4 * height) * width + (8 << 20)),
        ),
        cost_estimate=pl.CostEstimate(
            flops=0, bytes_accessed=140_000_000 * pair_count, transcendentals=0
        ),
    )(*given)


def nt_dot(left, right):
    return lax.dot_general(left, right, (((1,), (1,)), ((), ())), preferred_element_type=F32)


def silu_pair(values):
    gate = jax.nn.sigmoid(values)
    return values * gate, gate * (1.0 + values * (1.0 - gate))


def block_of(index, size):
    return pl.ds(pl.multiple_of(index * size, size), size)


def moe_kernel(hidden, expert_count, share, x_ref, dm_ref, *refs):
    ins, (mixer_ref, dout_ref), rest = refs[:7], refs[7:9], refs[9:]
    rows, d_rows, out, d_out = x_ref.at[0], dm_ref.at[0], mixer_ref.at[0], dout_ref.at[0]
    moe_step(hidden, expert_count, share, rows, d_rows, *ins, out, d_out, *rest)


def moe_step(
    hidden,
    expert_count,
    share,
    x_ref,
    dm_ref,
    slot_ref,
    col_ref,
    own_ref,
    wgu_ref,
    wd_ref,
    sgu_ref,
    sd_ref,
    mixer_ref,
    dout_ref,
    rows_ref,
    drows_ref,
    act_ref,
    dgu_ref,
    sact_ref,
    dsgu_ref,
    pick,
    gu,
    y_all,
    dx_all,
    put,
    sgu,
):
    step = pl.program_id(1)
    experts, width, both = wgu_ref.shape
    hp = both // 2
    shared_pad = sd_ref.shape[0]
    capacity = pick.shape[0]
    length = x_ref.shape[0]
    tile = 512
    span = 64
    low = hidden // 128 * 128

    @pl.when(step < experts)
    def _():
        e = step
        slots = lax.broadcasted_iota(jnp.int32, (capacity, length), 0)
        pick[...] = jnp.where(slot_ref[0, pl.ds(e, 1), :] == slots, 1.0, 0.0).astype(BF)

        def take(n, _):
            cols = block_of(n, tile)
            rows_ref[0, 0, :, cols] = dot(pick[...], x_ref[:, cols]).astype(BF)
            drows_ref[0, 0, :, cols] = dot(pick[...], dm_ref[:, cols]).astype(BF)
            return 0

        lax.fori_loop(0, width // tile, take, 0)
        gu[:, : 2 * hp] = dot(rows_ref[0, 0], wgu_ref[e])
        gu[:, 2 * hp :] = nt_dot(drows_ref[0, 0], wd_ref[e])

        def middle(n, _):
            part = block_of(n, span)
            g, u, d = gu[part, :hp], gu[part, hp : 2 * hp], gu[part, 2 * hp :]
            lane = lax.broadcasted_iota(jnp.int32, (span, 128), 1) + low
            inside = (lane >= hidden) & (lane < hidden + expert_count)
            logits = jnp.where(inside, g[:, low : low + 128], -1e30)
            exponent = jnp.exp(logits - jnp.max(logits, axis=-1, keepdims=True))
            prob = exponent / jnp.sum(exponent, axis=-1, keepdims=True)
            own = own_ref[pl.ds(e, 1), :]
            gate = jnp.sum(prob * own, axis=-1, keepdims=True)
            s, slope = silu_pair(g)
            scaled = gate * (s * u)
            act_ref[0, 0, part, :] = scaled.astype(BF)
            pull = jnp.sum(scaled * d, axis=-1, keepdims=True)
            d = d * gate
            dg = d * u * slope
            extra = pull * jnp.where(inside, own - prob, 0.0)
            dgu_ref[0, 0, part, :hp] = dg.astype(BF)
            dgu_ref[0, 0, part, low : low + 128] = (dg[:, low : low + 128] + extra).astype(BF)
            dgu_ref[0, 0, part, hp:] = (d * s).astype(BF)
            return 0

        lax.fori_loop(0, capacity // span, middle, 0)
        place = block_of(e, capacity)

        def back(n, _):
            cols = block_of(n, tile)
            y_all[place, cols] = dot(act_ref[0, 0], wd_ref[e, :, cols]).astype(BF)
            dx_all[place, cols] = nt_dot(dgu_ref[0, 0], wgu_ref[e, cols, :]).astype(BF)
            return 0

        lax.fori_loop(0, width // tile, back, 0)

    @pl.when(step >= experts)
    def _():
        rows = mixer_ref.shape[0]
        here = block_of(step - experts, rows)
        slots = lax.broadcasted_iota(jnp.int32, (rows, capacity), 1)
        for e in range(experts):
            put[:, e * capacity : (e + 1) * capacity] = jnp.where(
                col_ref[0, :, e : e + 1] == slots, 1.0, 0.0
            ).astype(BF)
        sgu[:, : 2 * shared_pad] = dot(x_ref[here, :], sgu_ref[...])
        sgu[:, 2 * shared_pad :] = nt_dot(dm_ref[here, :], sd_ref[...])

        def middle(n, _):
            part = block_of(n, span)
            g, u = sgu[part, :shared_pad], sgu[part, shared_pad : 2 * shared_pad]
            d = sgu[part, 2 * shared_pad :]
            mixing = lax.broadcasted_iota(jnp.int32, (span, shared_pad), 1) == share
            switch = jax.nn.sigmoid(
                jnp.sum(jnp.where(mixing, g, 0.0), axis=-1, keepdims=True)
            )
            s, slope = silu_pair(g)
            scaled = switch * (s * u)
            sact_ref[0, part, :] = scaled.astype(BF)
            pull = jnp.sum(scaled * d, axis=-1, keepdims=True) * (1.0 - switch)
            d = d * switch
            dsgu_ref[0, part, :shared_pad] = jnp.where(mixing, pull, d * u * slope).astype(BF)
            dsgu_ref[0, part, shared_pad:] = (d * s).astype(BF)
            return 0

        lax.fori_loop(0, rows // span, middle, 0)

        def finish(n, _):
            cols = block_of(n, tile)
            mixer_ref[:, cols] = (
                dot(put[...], y_all[:, cols]) + dot(sact_ref[0], sd_ref[:, cols])
            ).astype(BF)
            dout_ref[:, cols] = (
                dot(put[...], dx_all[:, cols]) + nt_dot(dsgu_ref[0], sgu_ref[cols, :])
            ).astype(BF)
            return 0

        lax.fori_loop(0, width // tile, finish, 0)


def moe_gather_kernel(hidden, expert_count, share, pair_count, x_own, dm_seq, dm_far, *refs):
    ins, (x_all, dm_all), outs, crossed, rest = refs[:7], refs[7:9], refs[9:11], refs[11:13], refs[13:-11]
    x_buf, dm_buf, m_buf, d_buf, own_sems, load_sems, far_sems, near_sems, core_sems = refs[-11:-2]
    out_sems, cross_sems = refs[-2:]
    m, step = pl.program_id(0), pl.program_id(1)
    steps = pl.num_programs(1)
    f, s = lax.axis_index("fsdp"), lax.axis_index("sp")
    height = x_own.shape[0]
    middle = height // 2
    alls, bufs = (x_all, dm_all), (x_buf, dm_buf)
    both = (0, 1)

    def rows(place):
        return pl.ds(pl.multiple_of(place * height, height), height)

    def half(t, k, place, h):
        start = pl.multiple_of(place * height + h * middle, middle)
        return alls[t].at[2 * k, pl.ds(start, middle)]

    def remote(source, target, sems, at, axis, place):
        return pltpu.make_async_remote_copy(
            src_ref=source,
            dst_ref=target,
            send_sem=sems.at[(0, *at)],
            recv_sem=sems.at[(1, *at)],
            device_id={axis: place},
            device_id_type=MESH,
        )

    def far(k, t=0):
        source = x_own if t == 0 else dm_seq.at[rows(s)]
        return remote(source, alls[t].at[2 * k, rows(s)], far_sems, (k, t), "fsdp", flip(f, 2 * k))

    early = dm_far.shape[0]

    def near(t, k, h, i):
        a, b = sp_bits()[h]
        source = half(t, k, flip(s, a) if i == 2 else s, h)
        return remote(source, source, near_sems, (k, t, 3 * h + i), "sp", flip(s, a if i == 0 else b))

    def core(t, k, j):
        place = rows(flip(s, j))
        target = alls[t].at[2 * k + 1, place]
        return remote(alls[t].at[2 * k, place], target, core_sems, (k, t, j), "fsdp", flip(f, 1))

    def distant(k):
        far(k).start()
        if k > early:
            far(k, 1).start()

    def first(k, tensors):
        if k:
            far(k).wait_recv()
        if k > early:
            far(k, 1).wait_recv()
        for t in tensors:
            for h in range(2):
                near(t, k, h, 0).start()
        if 2 <= k < pair_count - 1:
            distant(k + 1)

    def direct(k, tensors):
        for t in tensors:
            for h in range(2):
                near(t, k, h, 1).start()
            core(t, k, 0).start()

    def second(k, tensors):
        for t in tensors:
            for h in range(2):
                near(t, k, h, 0).wait_recv()
                near(t, k, h, 2).start()

    def third(k, tensors):
        for t in tensors:
            for h in range(2):
                near(t, k, h, 1).wait_recv()
            core(t, k, 1).start()
            core(t, k, 2).start()

    def fourth(k, tensors):
        for t in tensors:
            for h in range(2):
                near(t, k, h, 2).wait_recv()
            core(t, k, 3).start()

    def load(n, t):
        return pltpu.make_async_copy(alls[t].at[n], bufs[t].at[n % 2], load_sems.at[n % 2, t])

    def at_start():
        partners = [("sp", flip(s, 1)), ("sp", flip(s, 2)), ("fsdp", flip(f, 1))]
        partners += [("fsdp", flip(f, 2 * k)) for k in range(1, pair_count)]
        greet(partners)
        moves = [(x_own, x_buf.at[1, pl.ds(0, height)], x_all.at[0, rows(s)])]
        for k in range(1, early + 1):
            piece = dm_buf.at[1, pl.ds((k - 1) * height, height)]
            moves.append((dm_far.at[k - 1], piece, dm_all.at[2 * k, rows(s)]))
        moves.append((dm_seq, dm_buf.at[0], dm_all.at[0]))
        came = [
            pltpu.make_async_copy(source, stop, own_sems.at[n])
            for n, (source, stop, _) in enumerate(moves)
        ]
        left = [
            pltpu.make_async_copy(stop, target, own_sems.at[n])
            for n, (_, stop, target) in enumerate(moves)
        ]
        for copy in came:
            copy.start()
        for n, copy in enumerate(came):
            copy.wait()
            left[n].start()
        left[0].wait()
        first(0, (0,))
        far(1).start()
        direct(0, (0,))
        for copy in left[1:]:
            copy.wait()
        second(0, (0,))
        distant(2)
        for j in range(4):
            core(1, 0, j).start()
        third(0, (0,))
        fourth(0, (0,))
        load(0, 0).start()

    def whole(n):
        if n % 2:
            for t in both:
                for j in range(4):
                    core(t, n // 2, j).wait_recv()
        for t in both:
            load(n, t).start()

    plan = {0: [at_start]}
    for k in range(1, pair_count):
        base = 8 * (k - 1) + (k > 1)
        last = 8 * k - 1
        places = (base - (k == 2), base + 1 - (k == 2), base + 3, last - 2 + (k > 2), last)
        for event, place in zip((first, direct, second, third, fourth), places, strict=True):
            plan.setdefault(place, []).append(functools.partial(event, k, both))
    for n in range(1, 2 * pair_count):
        plan.setdefault(4 * n - 1, []).append(functools.partial(whole, n))
    now = m * steps + step
    for place, events in sorted(plan.items()):

        @pl.when(now == place)
        def _():
            for event in events:
                event()

    for n in range(2 * pair_count):

        @pl.when(now == n * steps)
        def _():
            for t in both if n else (0,):
                load(n, t).wait()

    token_step = step - ins[4].shape[0]
    even, pair = lax.rem(m, 2) == 0, lax.div(m, 2)
    out_bufs = (m_buf, d_buf)
    tile = m_buf.shape[1]
    tile_slot = lax.rem(token_step + 2, 2)

    def stay(t, k, i):
        target = outs[t].at[k, pl.ds(pl.multiple_of(i * tile, tile), tile)]
        slot = lax.rem(i + 2, 2)
        return pltpu.make_async_copy(out_bufs[t].at[slot], target, out_sems.at[t, slot])

    def leave(t, k, i):
        target = crossed[t].at[k, pl.ds(pl.multiple_of(i * tile, tile), tile)]
        source = out_bufs[t].at[lax.rem(i + 2, 2)]
        return remote(source, target, cross_sems, (t, k, i), "fsdp", flip(f, 1))

    @pl.when((token_step >= 0) & even & (m > 0))
    def _():
        for t in both:
            leave(t, pair - 1, token_step).wait_send()

    @pl.when((token_step >= 0) & (~even))
    def _():
        for t in both:
            stay(t, pair, token_step).wait()

    slot = lax.rem(m, 2)
    tiles = m_buf.at[tile_slot], d_buf.at[tile_slot]
    moe_step(hidden, expert_count, share, x_buf.at[slot], dm_buf.at[slot], *ins, *tiles, *rest)

    @pl.when((token_step >= 0) & even)
    def _():
        for t in both:
            stay(t, pair, token_step).start()

    @pl.when((token_step >= 0) & (~even))
    def _():
        for t in both:
            leave(t, pair, token_step).start()

    @pl.when(now == 2 * pair_count * steps - 1)
    def _():
        for k in range(pair_count):
            if k:
                far(k).wait_send()
            if k > early:
                far(k, 1).wait_send()
            for t in both:
                if k or t == 0:
                    for h in range(2):
                        for i in range(3):
                            near(t, k, h, i).wait_send()
                for j in range(4):
                    core(t, k, j).wait_send()
                for i in range(x_buf.shape[1] // tile):
                    if k == pair_count - 1:
                        leave(t, k, i).wait_send()
                    leave(t, k, i).wait_recv()


def moe_call(rows, d_rows, codes, own, weights, sizes, number=None, far_d_rows=None):
    hidden, expert_count, share, capacity = sizes
    wide_gu, wide_down, shared_gu, shared_down = weights
    seqs, _, length = codes.shape
    width = rows.shape[-1]
    pair_count = seqs // 2
    experts, _, both = wide_gu.shape
    hp = both // 2
    shared_pad = shared_down.shape[0]
    token_rows = min(512, length)
    token_steps = length // token_rows
    last = experts - 1

    def fixed(array):
        return pl.BlockSpec(
            array.shape, lambda s, i: (0,) * array.ndim, pipeline_mode=pl.Buffered(1)
        )

    def token_block(columns):
        return pl.BlockSpec(
            (1, token_rows, columns), lambda s, i: (s, jnp.maximum(i - experts, 0), 0)
        )

    def slot_block(columns):
        return pl.BlockSpec(
            (1, 1, capacity, columns), lambda s, i: (jnp.minimum(i, last), s, 0, 0)
        )

    def token_out(columns):
        return jax.ShapeDtypeStruct((seqs, length, columns), BF)

    def slot_out(columns):
        return jax.ShapeDtypeStruct((experts, seqs, capacity, columns), BF)

    slots = experts * capacity
    flops = seqs * 2 * (
        slots * width * (2 * length + 3 * both) + length * width * (2 * slots + 6 * shared_pad)
    )
    if number is None:
        kernel = functools.partial(moe_kernel, hidden, expert_count, share)
        tokens_spec = pl.BlockSpec((1, length, width), lambda s, i: (s, 0, 0))
        sums, sum_specs = [token_out(width)] * 2, [token_block(width)] * 2
        sems, extra = [], []
    else:
        kernel = functools.partial(moe_gather_kernel, hidden, expert_count, share, pair_count)
        tokens_spec = pl.BlockSpec(memory_space=pl.ANY)
        half = jax.ShapeDtypeStruct((pair_count, length, width), BF)
        sums, sum_specs = [token_out(width)] * 2 + [half] * 4, [tokens_spec] * 6
        extra = [far_d_rows]
        sems = [
            pltpu.VMEM((2, length, width), BF),
            pltpu.VMEM((2, length, width), BF),
            pltpu.VMEM((2, token_rows, width), BF),
            pltpu.VMEM((2, token_rows, width), BF),
            pltpu.SemaphoreType.DMA((1 + pair_count,)),
            pltpu.SemaphoreType.DMA((2, 2)),
            pltpu.SemaphoreType.DMA((2, pair_count, 2)),
            pltpu.SemaphoreType.DMA((2, pair_count, 2, 6)),
            pltpu.SemaphoreType.DMA((2, pair_count, 2, 4)),
            pltpu.SemaphoreType.DMA((2, 2)),
            pltpu.SemaphoreType.DMA((2, 2, pair_count, token_steps)),
        ]
    return pl.pallas_call(
        kernel,
        grid=(seqs, experts + token_steps),
        in_specs=[
            tokens_spec,
            tokens_spec,
            *([tokens_spec] * len(extra)),
            pl.BlockSpec((1, experts, length), lambda s, i: (s, 0, 0)),
            token_block(experts),
            fixed(own),
            fixed(wide_gu),
            fixed(wide_down),
            fixed(shared_gu),
            fixed(shared_down),
        ],
        out_specs=[
            *sum_specs,
            slot_block(width),
            slot_block(width),
            slot_block(hp),
            slot_block(both),
            token_block(shared_pad),
            token_block(2 * shared_pad),
        ],
        out_shape=[
            *sums,
            slot_out(width),
            slot_out(width),
            slot_out(hp),
            slot_out(both),
            token_out(shared_pad),
            token_out(2 * shared_pad),
        ],
        scratch_shapes=[
            pltpu.VMEM((capacity, length), BF),
            pltpu.VMEM((capacity, 3 * hp), F32),
            pltpu.VMEM((slots, width), BF),
            pltpu.VMEM((slots, width), BF),
            pltpu.VMEM((token_rows, slots), BF),
            pltpu.VMEM((token_rows, 3 * shared_pad), F32),
            *sems,
        ],
        compiler_params=pltpu.CompilerParams(
            dimension_semantics=("arbitrary", "arbitrary"),
            vmem_limit_bytes=60 * 1024 * 1024,
            collective_id=number,
            has_side_effects=number is not None,
        ),
        cost_estimate=pl.CostEstimate(
            flops=flops, bytes_accessed=seqs * 64 * length * width, transcendentals=0
        ),
    )(rows, d_rows, *extra, codes, codes.transpose(0, 2, 1), own, *weights)


def shared_grads(rows, d_rows, s_act, d_sgu):
    def tokens_of(array):
        return array.reshape(-1, array.shape[-1])

    return (
        dot(tokens_of(rows).T, tokens_of(d_sgu)),
        dot(tokens_of(d_rows).T, tokens_of(s_act)),
    )


def expert_grads(rows, d_rows, act, d_gu):
    def flat(array):
        return array.reshape(array.shape[0], -1, array.shape[-1])

    grad_gu = jnp.einsum("ecd,ecf->edf", flat(rows), flat(d_gu), preferred_element_type=F32)
    act = after(act, grad_gu)
    grad_ed = jnp.einsum("ecf,ecd->efd", flat(act), flat(d_rows), preferred_element_type=F32)
    return grad_gu, grad_ed


def pad_last(array, size):
    return jnp.pad(array, [(0, 0)] * (array.ndim - 1) + [(0, size - array.shape[-1])])


def round_up(value, unit):
    return -(-value // unit) * unit


def local(
    tokens,
    segments,
    routes,
    cotangent,
    gain_attn,
    w_query,
    w_key,
    w_value,
    bias_query,
    bias_key,
    bias_value,
    w_out,
    gain_mlp,
    router,
    mix_gate,
    shared_gate,
    shared_up,
    shared_down,
    expert_gate,
    expert_up,
    expert_down,
):
    fsdp_count = lax.axis_size("fsdp")
    sp_count = lax.axis_size("sp")
    sp_place = lax.axis_index("sp")
    fsdp_place = lax.axis_index("fsdp")
    pair_count = fsdp_count // 2
    tok_count = tokens.shape[0]
    seq_len = segments.shape[0]
    width = tokens.shape[1]
    top_count = routes.shape[1]
    expert_count = router.shape[1]
    local_experts = expert_gate.shape[0]
    capacity = 3 * seq_len * top_count // (2 * expert_count)
    local_heads = w_query.shape[1] // HEAD
    head_width = w_query.shape[1]
    row_block = min(512, seq_len)
    block_count = seq_len // row_block
    score_scale = HEAD ** (-0.5)
    own_segments = lax.dynamic_slice_in_dim(segments, sp_place * tok_count, tok_count)
    live_rows = (own_segments >= 0).astype(F32)[:, None]
    position = jnp.arange(seq_len, dtype=jnp.int32)
    cosine, sine_table = rope_tables(seq_len, HEAD)
    whole_axes = ("fsdp", "sp")
    own_kernels = sp_count == 4 and pair_count == 4

    def spread(local_rows, number):
        if not own_kernels:
            return lax.all_gather(local_rows, "sp", axis=0, tiled=True)
        return gather_call([local_rows], number)[0]

    def collect(partial_rows, number):
        partial_rows = partial_rows.astype(BF)
        if not own_kernels:
            rows = lax.psum_scatter(partial_rows, "sp", scatter_dimension=0, tiled=True)
            return rows.astype(F32)
        blocks = partial_rows.reshape(1, sp_count, tok_count, width)
        return scatter_call(number, blocks)

    orders = sp_bits()

    def slow_start(parts, crossed):
        shape = (pair_count, sp_count, 2, tok_count // 2, width)
        mine, crossed = parts.reshape(shape), crossed.reshape(shape)

        def pick(h, j):
            place = sp_place ^ j
            return add_low(
                lax.dynamic_index_in_dim(mine, place, 1, False)[:, h],
                lax.dynamic_index_in_dim(crossed, place, 1, False)[:, h],
            )

        sent = [jnp.stack([pick(h, orders[h][0]), pick(h, 3)]) for h in range(2)]
        kept = [jnp.stack([pick(h, 0), pick(h, orders[h][1])]) for h in range(2)]
        return sent, kept

    def slow_first(sent):
        return [swap(sent[h], "sp", orders[h][0]) for h in range(2)]

    def slow_second(kept, came):
        kept = [add_low(kept[h], came[h]) for h in range(2)]
        return [kept[h][0] for h in range(2)], [
            swap(kept[h][1], "sp", orders[h][1]) for h in range(2)
        ]

    def slow_third(kept, came):
        rows = jnp.concatenate([add_low(kept[h], came[h]) for h in range(2)], 1)
        rows = reorder(rows, fsdp_place // 2).reshape(pair_count * tok_count, width)
        cores = [[2 * z + c for z in range(pair_count)] for c in range(2)]
        return lax.psum_scatter(
            rows, "fsdp", scatter_dimension=0, axis_index_groups=cores, tiled=True
        )

    inputs = tokens.astype(F32)
    attn_rms = rms_scale(inputs)
    gain_one = gain_attn.astype(F32)
    normed_attn = (inputs * attn_rms * gain_one).astype(BF)
    upstream = cotangent.astype(F32)
    d_mixer = (live_rows * upstream).astype(BF)
    normed_attn = spread(normed_attn, 1)
    full_qkv = lax.all_gather(
        jnp.concatenate([w_query, w_key, w_value], 1), "fsdp", axis=0, tiled=True
    )
    d_mixer_own = after(d_mixer, (full_qkv, normed_attn))
    d_mixer = lax.all_gather(d_mixer_own, "sp", axis=0, tiled=True)
    full_out_t = lax.all_gather(after(w_out.T, d_mixer), "fsdp", axis=0, tiled=True)
    share = shared_gate.shape[1] // fsdp_count
    packed = jnp.concatenate(
        [
            shared_gate.reshape(-1, fsdp_count, share),
            shared_up.reshape(-1, fsdp_count, share),
            shared_down.T.reshape(-1, fsdp_count, share),
        ],
        2,
    ).transpose(1, 0, 2)
    packed = lax.all_to_all(
        after(packed, full_qkv), "fsdp", split_axis=0, concat_axis=0, tiled=True
    ).reshape(width, 3 * share)
    hidden_units = expert_gate.shape[2]
    hp = round_up(hidden_units + expert_count, 128)
    shared_pad = round_up(share + 1, 128)
    experts_like = jnp.broadcast_to(router, (local_experts, width, expert_count))
    wide_gu = jnp.concatenate(
        [
            pad_last(jnp.concatenate([expert_gate, experts_like], 2), hp),
            pad_last(expert_up, hp),
        ],
        2,
    )
    wide_down = jnp.pad(expert_down, ((0, 0), (0, hp - hidden_units), (0, 0)))
    all_routes = routes.T[None]
    bit = 1
    while bit < fsdp_count:
        all_routes = jnp.concatenate([all_routes, swap(all_routes, "fsdp", bit)], 0)
        bit *= 2
    first_expert = fsdp_place * local_experts
    wanted = first_expert + jnp.arange(local_experts, dtype=jnp.int32)
    named = jnp.any(all_routes[:, None] == wanted[None, :, None, None], axis=2)
    tally = jnp.cumsum(named.astype(jnp.int32), axis=2) - 1
    codes = jnp.where(named, tally, -1)
    lane = jnp.arange(128, dtype=jnp.int32)[None, :] + hidden_units // 128 * 128 - hidden_units
    own = (lane == wanted[:, None]).astype(F32)

    normed_attn = after(normed_attn, (codes, wide_gu, wide_down))
    qkv_lin = dot(normed_attn, full_qkv)
    query_lin = qkv_lin[:, :head_width] + bias_query.astype(F32)
    key_lin = qkv_lin[:, head_width : 2 * head_width] + bias_key.astype(F32)
    value_rows = (
        (qkv_lin[:, 2 * head_width :] + bias_value.astype(F32))
        .astype(BF)
        .reshape(seq_len, local_heads, HEAD)
    )
    query_rot = rotate(query_lin.reshape(seq_len, local_heads, HEAD), cosine, sine_table).astype(BF)
    query_rot, packed = lax.optimization_barrier((query_rot, packed))
    if own_kernels:
        d_mixer_own = after(d_mixer_own, packed)
        d_mixer_far = jnp.stack([swap(d_mixer_own, "fsdp", 2 * k) for k in range(1, 2)])
    shared_gu = jnp.concatenate(
        [
            pad_last(jnp.concatenate([packed[:, :share], mix_gate[:, None]], 1), shared_pad),
            pad_last(packed[:, share : 2 * share], shared_pad),
        ],
        1,
    )
    shared_down_rows = pad_last(packed[:, 2 * share :], shared_pad).T
    key_rot = rotate(key_lin.reshape(seq_len, local_heads, HEAD), cosine, sine_table).astype(BF)

    def block_scores(block_index):
        start, stop = block_index * row_block, (block_index + 1) * row_block
        query_block = query_rot[start:stop]
        raw_scores = (
            jnp.einsum(
                "qhd,khd->hqk", query_block, key_rot[:stop], preferred_element_type=jnp.float32
            )
            * score_scale
        )
        allowed = (
            (segments[start:stop, None] == segments[None, :stop])
            & (position[None, :stop] <= position[start:stop, None])
        )[None]
        return (query_block, raw_scores, allowed)

    def attend_block(block_index):
        query_block, raw_scores, allowed = block_scores(block_index)
        row_max = jnp.max(jnp.where(allowed, raw_scores, -jnp.inf), axis=-1, keepdims=True)
        exponent = jnp.exp(jnp.where(allowed, raw_scores - row_max, -jnp.inf))
        row_total = jnp.sum(exponent, axis=-1, keepdims=True)
        probability = (exponent / row_total).astype(BF)
        attended_block = jnp.einsum(
            "hqk,khd->qhd",
            probability,
            value_rows[: raw_scores.shape[2]],
            preferred_element_type=jnp.float32,
        ).astype(BF)
        return (attended_block, row_max + jnp.log(row_total))

    blocks = [attend_block(n) for n in range(block_count)]
    log_total = [block[1] for block in blocks]
    attended = jnp.concatenate([block[0] for block in blocks], 0)
    attended = attended.reshape(seq_len, local_heads * HEAD)
    attn_out = collect(nt_dot(attended, full_out_t), 2)
    hidden = inputs + live_rows * attn_out
    mlp_rms = rms_scale(hidden)
    gain_two = gain_mlp.astype(F32)
    normed_mlp = (hidden * mlp_rms * gain_two).astype(BF)
    weights = (wide_gu, wide_down, shared_gu, shared_down_rows)
    sizes = (hidden_units, expert_count, share, capacity)
    if own_kernels:
        all_rows, all_d_rows, mixer_parts, d_parts, mixer_crossed, d_crossed, *kept = moe_call(
            normed_mlp, d_mixer, codes, own, weights, sizes, 3, d_mixer_far
        )
        blocks = (pair_count, sp_count, tok_count, width)
        d_mlp_own = scatter_call(4, d_parts.reshape(blocks), d_crossed.reshape(blocks))
    else:
        seq_rows = spread(normed_mlp, 3)
        mixer_sum = d_sum = jnp.zeros((seq_len, width), F32)
        grads = None
        together = max(1, fsdp_count // 4)
        for start in range(0, fsdp_count, together):
            some = range(start, start + together)
            all_rows = jnp.stack([swap(seq_rows, "fsdp", m) for m in some])
            all_d_rows = jnp.stack([swap(d_mixer, "fsdp", m) for m in some])
            mixer_parts, d_parts, *kept = moe_call(
                all_rows, all_d_rows, codes[start : start + together], own, weights, sizes
            )
            more = expert_grads(*kept[:4]) + shared_grads(all_rows, all_d_rows, *kept[4:])
            grads = more if grads is None else jax.tree.map(jnp.add, grads, more)
            for n, m in enumerate(some):
                mixer_sum = mixer_sum + swap(mixer_parts[n], "fsdp", m).astype(F32)
                d_sum = d_sum + swap(d_parts[n], "fsdp", m).astype(F32)
            grads, mixer_sum, d_sum, seq_rows = lax.optimization_barrier(
                (grads, mixer_sum, d_sum, seq_rows)
            )
        mixer_out, d_mlp_own = collect(mixer_sum, 7), collect(d_sum, 8)
    grad_gain_two = jnp.sum(d_mlp_own * hidden * mlp_rms, axis=0)
    d_hidden = upstream + norm_back(d_mlp_own, hidden, mlp_rms, gain_two)
    d_attn = spread((live_rows * d_hidden).astype(BF), 5)
    if own_kernels:
        slow = slow_start(*after((mixer_parts, mixer_crossed), d_mlp_own))
        d_attn, slow = lax.optimization_barrier((d_attn, slow))
        slow = slow[1], slow_first(slow[0])
        grad_out_t = dot(d_attn.T, attended).astype(BF)
        grad_sgu, grad_sdown = shared_grads(
            all_rows, all_d_rows, *after(kept[4:], (d_attn, grad_out_t))
        )
    else:
        grad_out_t = dot(d_attn.T, attended).astype(BF)
        grad_gu, grad_ed, grad_sgu, grad_sdown = grads
    grad_w_out = lax.psum_scatter(
        grad_out_t, "fsdp", scatter_dimension=0, tiled=True
    ).astype(F32)
    packed_grad = jnp.concatenate(
        [
            grad_sgu[:, :share],
            grad_sgu[:, shared_pad : shared_pad + share],
            grad_sdown[:, :share],
        ],
        1,
    ).astype(BF)
    d_attn, packed_grad = lax.optimization_barrier((d_attn, packed_grad))
    packed_grad = lax.all_to_all(
        packed_grad.reshape(fsdp_count, -1, 3 * share), "fsdp", split_axis=0, concat_axis=0, tiled=True
    ).transpose(1, 0, 2)
    d_attended = dot(d_attn, full_out_t).astype(BF).reshape(seq_len, local_heads, HEAD)

    if own_kernels:
        d_attended, slow = lax.optimization_barrier((d_attended, slow))
        slow = slow_second(*slow)

    def attend_back(block_index):
        query_block, raw_scores, allowed = block_scores(block_index)
        start, stop = block_index * row_block, (block_index + 1) * row_block
        prob_full = jnp.exp(jnp.where(allowed, raw_scores - log_total[block_index], -jnp.inf))
        prob_low = prob_full.astype(BF)
        grad_block = d_attended[start:stop]
        d_prob = jnp.einsum(
            "qhd,khd->hqk", grad_block, value_rows[:stop], preferred_element_type=jnp.float32
        )
        d_scores = (
            prob_full * (d_prob - jnp.sum(prob_full * d_prob, axis=-1, keepdims=True))
        ).astype(BF)
        query_grad = (
            jnp.einsum("hqk,khd->qhd", d_scores, key_rot[:stop], preferred_element_type=jnp.float32)
            * score_scale
        )
        key_grad = (
            jnp.einsum("hqk,qhd->khd", d_scores, query_block, preferred_element_type=jnp.float32)
            * score_scale
        )
        value_grad = jnp.einsum(
            "hqk,qhd->khd", prob_low, grad_block, preferred_element_type=jnp.float32
        )
        return query_grad, key_grad, value_grad

    query_grads = []
    for block_index in range(block_count)[::-1]:
        query_part, key_part, value_part = attend_back(block_index)
        query_grads.insert(0, query_part)
        if block_index == block_count - 1:
            key_grad, value_grad = key_part, value_part
        else:
            stop = (block_index + 1) * row_block
            key_grad = key_grad.at[:stop].add(key_part)
            value_grad = value_grad.at[:stop].add(value_part)
    query_grad = jnp.concatenate(query_grads, 0)
    if own_kernels:
        query_grad, slow, packed_grad, grad_w_out = lax.optimization_barrier(
            (query_grad, slow, packed_grad, grad_w_out)
        )
        mixer_out = slow_third(*slow).astype(F32)
    query_grad = query_grad.reshape(seq_len, local_heads, HEAD)
    d_query = (
        unrotate(query_grad, cosine, sine_table)
        .reshape(seq_len, local_heads * HEAD)
        .astype(jnp.bfloat16)
    )
    d_key = (
        unrotate(key_grad, cosine, sine_table)
        .reshape(seq_len, local_heads * HEAD)
        .astype(jnp.bfloat16)
    )
    d_value = value_grad.reshape(seq_len, local_heads * HEAD).astype(jnp.bfloat16)
    d_qkv = jnp.concatenate([d_query, d_key, d_value], 1)
    grad_qkv = dot(normed_attn.T, d_qkv).astype(BF)
    d_normed_attn = dot(after(d_qkv, grad_qkv), full_qkv.T)
    d_attn_own = collect(d_normed_attn, 6)
    bias_grads = jnp.sum(d_qkv.astype(F32), axis=0)
    grad_gain_one = jnp.sum(d_attn_own * inputs * attn_rms, axis=0)
    grad_tokens = d_hidden + norm_back(d_attn_own, inputs, attn_rms, gain_one)
    grad_qkv = lax.psum_scatter(grad_qkv, "fsdp", scatter_dimension=0, tiled=True).astype(F32)
    if own_kernels:
        grad_gu, grad_ed = expert_grads(*after(kept[:4], d_attn_own))
    output = (hidden + live_rows * mixer_out).astype(BF)
    grad_expert_gate = grad_gu[..., :hidden_units]
    grad_expert_up = grad_gu[..., hp : hp + hidden_units]
    grad_expert_down = grad_ed[:, :hidden_units]
    grad_router = jnp.sum(grad_gu[..., hidden_units : hidden_units + expert_count], axis=0)
    grad_mix = grad_sgu[:, share]
    grad_shared_gate, grad_shared_up, grad_shared_down = (
        packed_grad[:, :, n * share : (n + 1) * share].reshape(-1, fsdp_count * share).astype(F32)
        for n in range(3)
    )
    bias_place = lax.dynamic_update_slice(
        jnp.zeros((3, sp_count * head_width), F32), bias_grads.reshape(3, -1), (0, sp_place * head_width)
    )
    small = jnp.concatenate(
        [jnp.stack([grad_gain_one, grad_gain_two, grad_mix]), bias_place, grad_router.T], 0
    )
    for axis_name in ("sp", "fsdp"):
        bit = 1
        while bit < lax.axis_size(axis_name):
            small = small + swap(small, axis_name, bit)
            bit *= 2
    sum_gain_one, sum_gain_two, sum_mix = small[0], small[1], small[2]
    own_bias = lax.dynamic_slice_in_dim(small[3:6], sp_place * head_width, head_width, 1)
    sum_router = small[6:].T
    return (
        output,
        grad_tokens,
        sum_gain_one,
        grad_qkv[:, :head_width],
        grad_qkv[:, head_width : 2 * head_width],
        grad_qkv[:, 2 * head_width :],
        own_bias[0],
        own_bias[1],
        own_bias[2],
        grad_w_out.T,
        sum_gain_two,
        sum_router,
        sum_mix,
        grad_shared_gate,
        grad_shared_up,
        grad_shared_down.T,
        grad_expert_gate,
        grad_expert_up,
        grad_expert_down,
    )


def solution(mesh):
    return jax.shard_map(
        local,
        mesh=mesh,
        in_specs=(
            P(("fsdp", "sp"), None),
            P("fsdp"),
            P("fsdp", None),
            P(("fsdp", "sp"), None),
            P(),
            P("fsdp", "sp"),
            P("fsdp", "sp"),
            P("fsdp", "sp"),
            P("sp"),
            P("sp"),
            P("sp"),
            P("sp", "fsdp"),
            P(),
            P(),
            P(),
            P("fsdp", "sp"),
            P("fsdp", "sp"),
            P("sp", "fsdp"),
            P("fsdp", None, "sp"),
            P("fsdp", None, "sp"),
            P("fsdp", "sp", None),
        ),
        out_specs=(
            P(("fsdp", "sp"), None),
            P(("fsdp", "sp"), None),
            P(),
            P("fsdp", "sp"),
            P("fsdp", "sp"),
            P("fsdp", "sp"),
            P("sp"),
            P("sp"),
            P("sp"),
            P("sp", "fsdp"),
            P(),
            P(),
            P(),
            P("fsdp", "sp"),
            P("fsdp", "sp"),
            P("sp", "fsdp"),
            P("fsdp", None, "sp"),
            P("fsdp", None, "sp"),
            P("fsdp", "sp", None),
        ),
        check_vma=False,
    )
```

```python
import functools

import jax
import jax.numpy as jnp
from jax import lax
from jax.experimental import pallas as pl
from jax.experimental.pallas import tpu as pltpu
from jax.sharding import PartitionSpec as P

HEAD = 128


EPSILON = 1e-06
ROPE_BASE = 1000000.0


def rms_scale(values):
    return lax.rsqrt(jnp.mean(values * values, axis=-1, keepdims=True) + EPSILON)


def norm_back(grad_rows, values, inverse_rms, gain_vector):
    weighted = grad_rows * gain_vector
    return inverse_rms * (
        weighted
        - values * inverse_rms * inverse_rms * jnp.mean(weighted * values, axis=-1, keepdims=True)
    )


def rope_tables(length, head_width):
    half_size = head_width // 2
    frequency = ROPE_BASE ** (-jnp.arange(half_size, dtype=jnp.float32) * 2.0 / head_width)
    angles = jnp.arange(length, dtype=jnp.float32)[:, None] * frequency[None, :]
    return (jnp.cos(angles)[:, None, :], jnp.sin(angles)[:, None, :])


def rotate(values, cosine, sine_table):
    half_size = values.shape[-1] // 2
    front_half = values[..., :half_size]
    back_half = values[..., half_size:]
    return jnp.concatenate(
        [
            front_half * cosine - back_half * sine_table,
            back_half * cosine + front_half * sine_table,
        ],
        axis=-1,
    )


def unrotate(gradient, cosine, sine_table):
    half_size = gradient.shape[-1] // 2
    front_half = gradient[..., :half_size]
    back_half = gradient[..., half_size:]
    return jnp.concatenate(
        [
            front_half * cosine + back_half * sine_table,
            back_half * cosine - front_half * sine_table,
        ],
        axis=-1,
    )


def silu_slope(activation):
    sigmoid_act = jax.nn.sigmoid(activation)
    return sigmoid_act * (1.0 + activation * (1.0 - sigmoid_act))


BF = jnp.bfloat16
F32 = jnp.float32


def dot(left, right):
    return jnp.dot(left, right, preferred_element_type=F32)


def swap(values, axis_name, mask):
    count = lax.axis_size(axis_name)
    return lax.ppermute(values, axis_name, [(i, i ^ mask) for i in range(count)])


def add_low(left, right):
    return (left.astype(F32) + right.astype(F32)).astype(BF)


def reorder(blocks, place):
    return jnp.stack(
        [lax.dynamic_index_in_dim(blocks, i ^ place, keepdims=False) for i in range(blocks.shape[0])]
    )


def after(value, other):
    return lax.optimization_barrier((value, other))[0]


MESH = pl.DeviceIdType.MESH


def flip(index, mask):
    bit = 1
    while bit <= mask:
        if mask & bit:
            index = index + bit - 2 * bit * lax.rem(lax.div(index, bit), 2)
        bit *= 2
    return index


def sp_bits():
    return ((1, 2), (2, 1))


def greet(barrier_partners):
    barrier = pltpu.get_barrier_semaphore()
    for axis, place in barrier_partners:
        pl.semaphore_signal(barrier, inc=1, device_id={axis: place}, device_id_type=MESH)
    pl.semaphore_wait(barrier, len(barrier_partners))


class Copies:
    def __init__(self, send_sems, recv_sems):
        self.send_sems, self.recv_sems, self.made = send_sems, recv_sems, []

    def start(self, source, target, axis, place):
        number = len(self.made)
        copy = pltpu.make_async_remote_copy(
            src_ref=source,
            dst_ref=target,
            send_sem=self.send_sems.at[number],
            recv_sem=self.recv_sems.at[number],
            device_id={axis: place},
            device_id_type=MESH,
        )
        copy.start()
        self.made.append(copy)
        return copy

    def finish(self):
        for copy in self.made:
            copy.wait_send()


def gather_kernel(count, *refs):
    given, made = refs[:count], refs[count : 2 * count]
    bounce, own_sems, send_sems, recv_sems = refs[2 * count :]
    s = lax.axis_index("sp")
    height = given[0].shape[0]
    middle = height // 2
    greet([("sp", flip(s, 1)), ("sp", flip(s, 2))])
    copies = Copies(send_sems, recv_sems)

    def block(t, j, h):
        start = pl.multiple_of(flip(s, j) * height + h * middle, middle)
        return made[t].at[pl.ds(start, middle)]

    local, near = [], {}
    for t in range(count):
        target = made[t].at[pl.ds(pl.multiple_of(s * height, height), height)]
        pltpu.make_async_copy(given[t], bounce.at[t], own_sems.at[t]).start()
        local.append(pltpu.make_async_copy(bounce.at[t], target, own_sems.at[t]))
        for turn in range(2):
            for h in range(2):
                bit = sp_bits()[h][turn]
                source = given[t].at[pl.ds(h * middle, middle)]
                near[t, h, bit] = copies.start(source, block(t, 0, h), "sp", flip(s, bit))
    for t in range(count):
        pltpu.make_async_copy(given[t], bounce.at[t], own_sems.at[t]).wait()
        local[t].start()
        for h in range(2):
            a, b = sp_bits()[h]
            near[t, h, a].wait_recv()
            near[t, h, 3] = copies.start(block(t, a, h), block(t, a, h), "sp", flip(s, b))
    for t in range(count):
        for h in range(2):
            near[t, h, sp_bits()[h][1]].wait_recv()
            near[t, h, 3].wait_recv()
        local[t].wait()
    copies.finish()


def gather_call(arrays, number):
    height, width = arrays[0].shape
    count, sp_count = len(arrays), lax.axis_size("sp")
    whole = jax.ShapeDtypeStruct((sp_count * height, width), arrays[0].dtype)
    return pl.pallas_call(
        functools.partial(gather_kernel, count),
        out_shape=[whole] * count,
        in_specs=[pl.BlockSpec(memory_space=pl.ANY)] * count,
        out_specs=[pl.BlockSpec(memory_space=pl.ANY)] * count,
        scratch_shapes=[
            pltpu.VMEM((count, height, width), BF),
            pltpu.SemaphoreType.DMA((count,)),
            pltpu.SemaphoreType.DMA((6 * count,)),
            pltpu.SemaphoreType.DMA((6 * count,)),
        ],
        compiler_params=pltpu.CompilerParams(collective_id=number, has_side_effects=True),
    )(*arrays)


def scatter_kernel(
    pair_count, p_ref, q_ref, out_ref, held, loads, came, last, far, load_sems, send_sems, recv_sems
):
    f, s = lax.axis_index("fsdp"), lax.axis_index("sp")
    middle = held.shape[3]
    partners = [("sp", flip(s, 1)), ("sp", flip(s, 2))]
    partners += [("fsdp", flip(f, 2 * k)) for k in range(1, pair_count)]
    greet(partners)
    copies = Copies(send_sems, recv_sems)
    order = list(range(pair_count))[::-1]

    loading = {}

    def load(k):
        for h in range(2):
            rows = pl.ds(h * middle, middle)
            loading[k, h] = [
                pltpu.make_async_copy(p_ref.at[k, :, rows], held.at[k, h], load_sems.at[k % 2, h, 0])
            ]
            if q_ref is not None:
                loading[k, h].append(
                    pltpu.make_async_copy(
                        q_ref.at[k, :, rows], loads.at[k % 2, h], load_sems.at[k % 2, h, 1]
                    )
                )
            for copy in loading[k, h]:
                copy.start()

    def add(target, source):
        def body(n, _):
            part = block_of(n, 16)
            target[part, :] = (target[part, :].astype(F32) + source[part, :].astype(F32)).astype(BF)
            return 0

        lax.fori_loop(0, middle // 16, body, 0)

    near, late, distant = {}, {}, {}

    def first(n):
        k = order[n]
        if n + 1 < pair_count:
            load(order[n + 1])
        for h in range(2):
            for copy in loading[k, h]:
                copy.wait()
            a, b = sp_bits()[h]
            for i, j in ((1, 3), (0, a)):
                piece = held.at[k, h, flip(s, j)]
                if q_ref is not None:
                    add(piece, loads.at[k % 2, h, flip(s, j)])
                near[k, h, i] = copies.start(piece, came.at[k, h, i], "sp", flip(s, a))
        if q_ref is not None:
            for h in range(2):
                a, b = sp_bits()[h]
                for j in (0, b):
                    add(held.at[k, h, flip(s, j)], loads.at[k % 2, h, flip(s, j)])

    def second(n):
        k = order[n]
        for h in range(2):
            a, b = sp_bits()[h]
            near[k, h, 1].wait_recv()
            piece = held.at[k, h, flip(s, b)]
            add(piece, came.at[k, h, 1])
            late[k, h] = copies.start(piece, last.at[k, h], "sp", flip(s, b))
        for h in range(2):
            near[k, h, 0].wait_recv()
            add(held.at[k, h, s], came.at[k, h, 0])

    def third(n):
        k = order[n]
        for h in range(2):
            late[k, h].wait_recv()
            piece = held.at[k, h, s]
            add(piece, last.at[k, h])
            if k:
                distant[k, h] = copies.start(piece, far.at[k - 1, h], "fsdp", flip(f, 2 * k))

    load(order[0])
    for step in range(pair_count + 2):
        if step < pair_count:
            first(step)
        if 0 <= step - 1 < pair_count:
            second(step - 1)
        if 0 <= step - 2 < pair_count:
            third(step - 2)
    for h in range(2):
        for k in range(1, pair_count):
            distant[k, h].wait_recv()

        def total(n, _):
            part = block_of(n, 16)
            value = held[0, h, s, part, :].astype(F32)
            for k in range(1, pair_count):
                value = value + far[k - 1, h, part, :].astype(F32)
            out_ref[pl.ds(pl.multiple_of(h * middle + n * 16, 16), 16), :] = value
            return 0

        lax.fori_loop(0, middle // 16, total, 0)
    copies.finish()


def sum_kernel(pair_count, p_ref, *refs):
    scatter_kernel(pair_count, p_ref, None, *refs)


def scatter_call(number, blocks, more=None):
    pair_count, sp_count, height, width = blocks.shape
    middle = height // 2
    count = 6 * pair_count + 2 * (pair_count - 1)
    given = [blocks] if more is None else [blocks, more]
    used = 2 * pair_count * (sp_count + 3) + (4 * sp_count if more is not None else 0) + 2 * pair_count
    return pl.pallas_call(
        functools.partial(sum_kernel if more is None else scatter_kernel, pair_count),
        out_shape=jax.ShapeDtypeStruct((height, width), F32),
        in_specs=[pl.BlockSpec(memory_space=pl.ANY)] * len(given),
        out_specs=pl.BlockSpec(memory_space=pltpu.VMEM),
        scratch_shapes=[
            pltpu.VMEM((pair_count, 2, sp_count, middle, width), BF),
            pltpu.VMEM((2, 2, sp_count, middle, width) if len(given) > 1 else (2, 2, 1, 16, width), BF),
            pltpu.VMEM((pair_count, 2, 2, middle, width), BF),
            pltpu.VMEM((pair_count, 2, middle, width), BF),
            pltpu.VMEM((max(pair_count - 1, 1), 2, middle if pair_count > 1 else 16, width), BF),
            pltpu.SemaphoreType.DMA((2, 2, 2)),
            pltpu.SemaphoreType.DMA((count,)),
            pltpu.SemaphoreType.DMA((count,)),
        ],
        compiler_params=pltpu.CompilerParams(
            collective_id=number,
            has_side_effects=True,
            vmem_limit_bytes=min(60 * 1024 * 1024, (2 * used * middle + 4 * height) * width + (8 << 20)),
        ),
        cost_estimate=pl.CostEstimate(
            flops=0, bytes_accessed=140_000_000 * pair_count, transcendentals=0
        ),
    )(*given)


def nt_dot(left, right):
    return lax.dot_general(left, right, (((1,), (1,)), ((), ())), preferred_element_type=F32)


def silu_pair(values):
    gate = jax.nn.sigmoid(values)
    return values * gate, gate * (1.0 + values * (1.0 - gate))


def block_of(index, size):
    return pl.ds(pl.multiple_of(index * size, size), size)


def moe_kernel(hidden, expert_count, share, x_ref, dm_ref, *refs):
    ins, (mixer_ref, dout_ref), rest = refs[:7], refs[7:9], refs[9:]
    rows, d_rows, out, d_out = x_ref.at[0], dm_ref.at[0], mixer_ref.at[0], dout_ref.at[0]
    moe_step(hidden, expert_count, share, rows, d_rows, *ins, out, d_out, *rest)


def moe_step(
    hidden,
    expert_count,
    share,
    x_ref,
    dm_ref,
    slot_ref,
    col_ref,
    own_ref,
    wgu_ref,
    wd_ref,
    sgu_ref,
    sd_ref,
    mixer_ref,
    dout_ref,
    rows_ref,
    drows_ref,
    act_ref,
    dgu_ref,
    sact_ref,
    dsgu_ref,
    pick,
    gu,
    y_all,
    dx_all,
    put,
    sgu,
):
    step = pl.program_id(1)
    experts, width, both = wgu_ref.shape
    hp = both // 2
    shared_pad = sd_ref.shape[0]
    capacity = pick.shape[0]
    length = x_ref.shape[0]
    tile = 512
    span = 64
    low = hidden // 128 * 128

    @pl.when(step < experts)
    def _():
        e = step
        slots = lax.broadcasted_iota(jnp.int32, (capacity, length), 0)
        pick[...] = jnp.where(slot_ref[0, pl.ds(e, 1), :] == slots, 1.0, 0.0).astype(BF)

        def take(n, _):
            cols = block_of(n, tile)
            rows_ref[0, 0, :, cols] = dot(pick[...], x_ref[:, cols]).astype(BF)
            drows_ref[0, 0, :, cols] = dot(pick[...], dm_ref[:, cols]).astype(BF)
            return 0

        lax.fori_loop(0, width // tile, take, 0)
        gu[:, : 2 * hp] = dot(rows_ref[0, 0], wgu_ref[e])
        gu[:, 2 * hp :] = nt_dot(drows_ref[0, 0], wd_ref[e])

        def middle(n, _):
            part = block_of(n, span)
            g, u, d = gu[part, :hp], gu[part, hp : 2 * hp], gu[part, 2 * hp :]
            lane = lax.broadcasted_iota(jnp.int32, (span, 128), 1) + low
            inside = (lane >= hidden) & (lane < hidden + expert_count)
            logits = jnp.where(inside, g[:, low : low + 128], -1e30)
            exponent = jnp.exp(logits - jnp.max(logits, axis=-1, keepdims=True))
            prob = exponent / jnp.sum(exponent, axis=-1, keepdims=True)
            own = own_ref[pl.ds(e, 1), :]
            gate = jnp.sum(prob * own, axis=-1, keepdims=True)
            s, slope = silu_pair(g)
            scaled = gate * (s * u)
            act_ref[0, 0, part, :] = scaled.astype(BF)
            pull = jnp.sum(scaled * d, axis=-1, keepdims=True)
            d = d * gate
            dg = d * u * slope
            extra = pull * jnp.where(inside, own - prob, 0.0)
            dgu_ref[0, 0, part, :hp] = dg.astype(BF)
            dgu_ref[0, 0, part, low : low + 128] = (dg[:, low : low + 128] + extra).astype(BF)
            dgu_ref[0, 0, part, hp:] = (d * s).astype(BF)
            return 0

        lax.fori_loop(0, capacity // span, middle, 0)
        place = block_of(e, capacity)

        def back(n, _):
            cols = block_of(n, tile)
            y_all[place, cols] = dot(act_ref[0, 0], wd_ref[e, :, cols]).astype(BF)
            dx_all[place, cols] = nt_dot(dgu_ref[0, 0], wgu_ref[e, cols, :]).astype(BF)
            return 0

        lax.fori_loop(0, width // tile, back, 0)

    @pl.when(step >= experts)
    def _():
        rows = mixer_ref.shape[0]
        here = block_of(step - experts, rows)
        slots = lax.broadcasted_iota(jnp.int32, (rows, capacity), 1)
        for e in range(experts):
            put[:, e * capacity : (e + 1) * capacity] = jnp.where(
                col_ref[0, :, e : e + 1] == slots, 1.0, 0.0
            ).astype(BF)
        sgu[:, : 2 * shared_pad] = dot(x_ref[here, :], sgu_ref[...])
        sgu[:, 2 * shared_pad :] = nt_dot(dm_ref[here, :], sd_ref[...])

        def middle(n, _):
            part = block_of(n, span)
            g, u = sgu[part, :shared_pad], sgu[part, shared_pad : 2 * shared_pad]
            d = sgu[part, 2 * shared_pad :]
            mixing = lax.broadcasted_iota(jnp.int32, (span, shared_pad), 1) == share
            switch = jax.nn.sigmoid(
                jnp.sum(jnp.where(mixing, g, 0.0), axis=-1, keepdims=True)
            )
            s, slope = silu_pair(g)
            scaled = switch * (s * u)
            sact_ref[0, part, :] = scaled.astype(BF)
            pull = jnp.sum(scaled * d, axis=-1, keepdims=True) * (1.0 - switch)
            d = d * switch
            dsgu_ref[0, part, :shared_pad] = jnp.where(mixing, pull, d * u * slope).astype(BF)
            dsgu_ref[0, part, shared_pad:] = (d * s).astype(BF)
            return 0

        lax.fori_loop(0, rows // span, middle, 0)

        def finish(n, _):
            cols = block_of(n, tile)
            mixer_ref[:, cols] = (
                dot(put[...], y_all[:, cols]) + dot(sact_ref[0], sd_ref[:, cols])
            ).astype(BF)
            dout_ref[:, cols] = (
                dot(put[...], dx_all[:, cols]) + nt_dot(dsgu_ref[0], sgu_ref[cols, :])
            ).astype(BF)
            return 0

        lax.fori_loop(0, width // tile, finish, 0)


def moe_gather_kernel(hidden, expert_count, share, pair_count, x_own, dm_seq, dm_far, *refs):
    ins, (x_all, dm_all), outs, crossed, rest = refs[:7], refs[7:9], refs[9:11], refs[11:13], refs[13:-11]
    x_buf, dm_buf, m_buf, d_buf, own_sems, load_sems, far_sems, near_sems, core_sems = refs[-11:-2]
    out_sems, cross_sems = refs[-2:]
    m, step = pl.program_id(0), pl.program_id(1)
    steps = pl.num_programs(1)
    f, s = lax.axis_index("fsdp"), lax.axis_index("sp")
    height = x_own.shape[0]
    middle = height // 2
    alls, bufs = (x_all, dm_all), (x_buf, dm_buf)
    both = (0, 1)

    def rows(place):
        return pl.ds(pl.multiple_of(place * height, height), height)

    def half(t, k, place, h):
        start = pl.multiple_of(place * height + h * middle, middle)
        return alls[t].at[2 * k, pl.ds(start, middle)]

    def remote(source, target, sems, at, axis, place):
        return pltpu.make_async_remote_copy(
            src_ref=source,
            dst_ref=target,
            send_sem=sems.at[(0, *at)],
            recv_sem=sems.at[(1, *at)],
            device_id={axis: place},
            device_id_type=MESH,
        )

    def far(k, t=0):
        source = x_own if t == 0 else dm_seq.at[rows(s)]
        return remote(source, alls[t].at[2 * k, rows(s)], far_sems, (k, t), "fsdp", flip(f, 2 * k))

    early = dm_far.shape[0]

    def near(t, k, h, i):
        a, b = sp_bits()[h]
        source = half(t, k, flip(s, a) if i == 2 else s, h)
        return remote(source, source, near_sems, (k, t, 3 * h + i), "sp", flip(s, a if i == 0 else b))

    def core(t, k, j):
        place = rows(flip(s, j))
        target = alls[t].at[2 * k + 1, place]
        return remote(alls[t].at[2 * k, place], target, core_sems, (k, t, j), "fsdp", flip(f, 1))

    def distant(k):
        far(k).start()
        if k > early:
            far(k, 1).start()

    def first(k, tensors):
        if k:
            far(k).wait_recv()
        if k > early:
            far(k, 1).wait_recv()
        for t in tensors:
            for h in range(2):
                near(t, k, h, 0).start()
        if 2 <= k < pair_count - 1:
            distant(k + 1)

    def direct(k, tensors):
        for t in tensors:
            for h in range(2):
                near(t, k, h, 1).start()
            core(t, k, 0).start()

    def second(k, tensors):
        for t in tensors:
            for h in range(2):
                near(t, k, h, 0).wait_recv()
                near(t, k, h, 2).start()

    def third(k, tensors):
        for t in tensors:
            for h in range(2):
                near(t, k, h, 1).wait_recv()
            core(t, k, 1).start()
            core(t, k, 2).start()

    def fourth(k, tensors):
        for t in tensors:
            for h in range(2):
                near(t, k, h, 2).wait_recv()
            core(t, k, 3).start()

    def load(n, t):
        return pltpu.make_async_copy(alls[t].at[n], bufs[t].at[n % 2], load_sems.at[n % 2, t])

    def at_start():
        partners = [("sp", flip(s, 1)), ("sp", flip(s, 2)), ("fsdp", flip(f, 1))]
        partners += [("fsdp", flip(f, 2 * k)) for k in range(1, pair_count)]
        greet(partners)
        moves = [(x_own, x_buf.at[1, pl.ds(0, height)], x_all.at[0, rows(s)])]
        for k in range(1, early + 1):
            piece = dm_buf.at[1, pl.ds((k - 1) * height, height)]
            moves.append((dm_far.at[k - 1], piece, dm_all.at[2 * k, rows(s)]))
        moves.append((dm_seq, dm_buf.at[0], dm_all.at[0]))
        came = [
            pltpu.make_async_copy(source, stop, own_sems.at[n])
            for n, (source, stop, _) in enumerate(moves)
        ]
        left = [
            pltpu.make_async_copy(stop, target, own_sems.at[n])
            for n, (_, stop, target) in enumerate(moves)
        ]
        for copy in came:
            copy.start()
        for n, copy in enumerate(came):
            copy.wait()
            left[n].start()
        left[0].wait()
        first(0, (0,))
        far(1).start()
        direct(0, (0,))
        for copy in left[1:]:
            copy.wait()
        second(0, (0,))
        distant(2)
        for j in range(4):
            core(1, 0, j).start()
        third(0, (0,))
        fourth(0, (0,))
        load(0, 0).start()

    def whole(n):
        if n % 2:
            for t in both:
                for j in range(4):
                    core(t, n // 2, j).wait_recv()
        for t in both:
            load(n, t).start()

    plan = {0: [at_start]}
    for k in range(1, pair_count):
        base = 8 * (k - 1) + (k > 1)
        last = 8 * k - 1
        places = (base - (k == 2), base + 1 - (k == 2), base + 3, last - 2 + (k > 2), last)
        for event, place in zip((first, direct, second, third, fourth), places, strict=True):
            plan.setdefault(place, []).append(functools.partial(event, k, both))
    for n in range(1, 2 * pair_count):
        plan.setdefault(4 * n - 1, []).append(functools.partial(whole, n))
    now = m * steps + step
    for place, events in sorted(plan.items()):

        @pl.when(now == place)
        def _():
            for event in events:
                event()

    for n in range(2 * pair_count):

        @pl.when(now == n * steps)
        def _():
            for t in both if n else (0,):
                load(n, t).wait()

    token_step = step - ins[4].shape[0]
    even, pair = lax.rem(m, 2) == 0, lax.div(m, 2)
    out_bufs = (m_buf, d_buf)
    tile = m_buf.shape[1]
    tile_slot = lax.rem(token_step + 2, 2)

    def stay(t, k, i):
        target = outs[t].at[k, pl.ds(pl.multiple_of(i * tile, tile), tile)]
        slot = lax.rem(i + 2, 2)
        return pltpu.make_async_copy(out_bufs[t].at[slot], target, out_sems.at[t, slot])

    def leave(t, k, i):
        target = crossed[t].at[k, pl.ds(pl.multiple_of(i * tile, tile), tile)]
        source = out_bufs[t].at[lax.rem(i + 2, 2)]
        return remote(source, target, cross_sems, (t, k, i), "fsdp", flip(f, 1))

    @pl.when((token_step >= 0) & even & (m > 0))
    def _():
        for t in both:
            leave(t, pair - 1, token_step).wait_send()

    @pl.when((token_step >= 0) & (~even))
    def _():
        for t in both:
            stay(t, pair, token_step).wait()

    slot = lax.rem(m, 2)
    tiles = m_buf.at[tile_slot], d_buf.at[tile_slot]
    moe_step(hidden, expert_count, share, x_buf.at[slot], dm_buf.at[slot], *ins, *tiles, *rest)

    @pl.when((token_step >= 0) & even)
    def _():
        for t in both:
            stay(t, pair, token_step).start()

    @pl.when((token_step >= 0) & (~even))
    def _():
        for t in both:
            leave(t, pair, token_step).start()

    @pl.when(now == 2 * pair_count * steps - 1)
    def _():
        for k in range(pair_count):
            if k:
                far(k).wait_send()
            if k > early:
                far(k, 1).wait_send()
            for t in both:
                if k or t == 0:
                    for h in range(2):
                        for i in range(3):
                            near(t, k, h, i).wait_send()
                for j in range(4):
                    core(t, k, j).wait_send()
                for i in range(x_buf.shape[1] // tile):
                    if k == pair_count - 1:
                        leave(t, k, i).wait_send()
                    leave(t, k, i).wait_recv()


def moe_call(rows, d_rows, codes, own, weights, sizes, number=None, far_d_rows=None):
    hidden, expert_count, share, capacity = sizes
    wide_gu, wide_down, shared_gu, shared_down = weights
    seqs, _, length = codes.shape
    width = rows.shape[-1]
    pair_count = seqs // 2
    experts, _, both = wide_gu.shape
    hp = both // 2
    shared_pad = shared_down.shape[0]
    token_rows = min(512, length)
    token_steps = length // token_rows
    last = experts - 1

    def fixed(array):
        return pl.BlockSpec(
            array.shape, lambda s, i: (0,) * array.ndim, pipeline_mode=pl.Buffered(1)
        )

    def token_block(columns):
        return pl.BlockSpec(
            (1, token_rows, columns), lambda s, i: (s, jnp.maximum(i - experts, 0), 0)
        )

    def slot_block(columns):
        return pl.BlockSpec(
            (1, 1, capacity, columns), lambda s, i: (jnp.minimum(i, last), s, 0, 0)
        )

    def token_out(columns):
        return jax.ShapeDtypeStruct((seqs, length, columns), BF)

    def slot_out(columns):
        return jax.ShapeDtypeStruct((experts, seqs, capacity, columns), BF)

    slots = experts * capacity
    flops = seqs * 2 * (
        slots * width * (2 * length + 3 * both) + length * width * (2 * slots + 6 * shared_pad)
    )
    if number is None:
        kernel = functools.partial(moe_kernel, hidden, expert_count, share)
        tokens_spec = pl.BlockSpec((1, length, width), lambda s, i: (s, 0, 0))
        sums, sum_specs = [token_out(width)] * 2, [token_block(width)] * 2
        sems, extra = [], []
    else:
        kernel = functools.partial(moe_gather_kernel, hidden, expert_count, share, pair_count)
        tokens_spec = pl.BlockSpec(memory_space=pl.ANY)
        half = jax.ShapeDtypeStruct((pair_count, length, width), BF)
        sums, sum_specs = [token_out(width)] * 2 + [half] * 4, [tokens_spec] * 6
        extra = [far_d_rows]
        sems = [
            pltpu.VMEM((2, length, width), BF),
            pltpu.VMEM((2, length, width), BF),
            pltpu.VMEM((2, token_rows, width), BF),
            pltpu.VMEM((2, token_rows, width), BF),
            pltpu.SemaphoreType.DMA((1 + pair_count,)),
            pltpu.SemaphoreType.DMA((2, 2)),
            pltpu.SemaphoreType.DMA((2, pair_count, 2)),
            pltpu.SemaphoreType.DMA((2, pair_count, 2, 6)),
            pltpu.SemaphoreType.DMA((2, pair_count, 2, 4)),
            pltpu.SemaphoreType.DMA((2, 2)),
            pltpu.SemaphoreType.DMA((2, 2, pair_count, token_steps)),
        ]
    return pl.pallas_call(
        kernel,
        grid=(seqs, experts + token_steps),
        in_specs=[
            tokens_spec,
            tokens_spec,
            *([tokens_spec] * len(extra)),
            pl.BlockSpec((1, experts, length), lambda s, i: (s, 0, 0)),
            token_block(experts),
            fixed(own),
            fixed(wide_gu),
            fixed(wide_down),
            fixed(shared_gu),
            fixed(shared_down),
        ],
        out_specs=[
            *sum_specs,
            slot_block(width),
            slot_block(width),
            slot_block(hp),
            slot_block(both),
            token_block(shared_pad),
            token_block(2 * shared_pad),
        ],
        out_shape=[
            *sums,
            slot_out(width),
            slot_out(width),
            slot_out(hp),
            slot_out(both),
            token_out(shared_pad),
            token_out(2 * shared_pad),
        ],
        scratch_shapes=[
            pltpu.VMEM((capacity, length), BF),
            pltpu.VMEM((capacity, 3 * hp), F32),
            pltpu.VMEM((slots, width), BF),
            pltpu.VMEM((slots, width), BF),
            pltpu.VMEM((token_rows, slots), BF),
            pltpu.VMEM((token_rows, 3 * shared_pad), F32),
            *sems,
        ],
        compiler_params=pltpu.CompilerParams(
            dimension_semantics=("arbitrary", "arbitrary"),
            vmem_limit_bytes=60 * 1024 * 1024,
            collective_id=number,
            has_side_effects=number is not None,
        ),
        cost_estimate=pl.CostEstimate(
            flops=flops, bytes_accessed=seqs * 64 * length * width, transcendentals=0
        ),
    )(rows, d_rows, *extra, codes, codes.transpose(0, 2, 1), own, *weights)


def shared_grads(rows, d_rows, s_act, d_sgu):
    def tokens_of(array):
        return array.reshape(-1, array.shape[-1])

    return (
        dot(tokens_of(rows).T, tokens_of(d_sgu)),
        dot(tokens_of(d_rows).T, tokens_of(s_act)),
    )


def expert_grads(rows, d_rows, act, d_gu):
    def flat(array):
        return array.reshape(array.shape[0], -1, array.shape[-1])

    grad_gu = jnp.einsum("ecd,ecf->edf", flat(rows), flat(d_gu), preferred_element_type=F32)
    act = after(act, grad_gu)
    grad_ed = jnp.einsum("ecf,ecd->efd", flat(act), flat(d_rows), preferred_element_type=F32)
    return grad_gu, grad_ed


def pad_last(array, size):
    return jnp.pad(array, [(0, 0)] * (array.ndim - 1) + [(0, size - array.shape[-1])])


def round_up(value, unit):
    return -(-value // unit) * unit


def local(
    tokens,
    segments,
    routes,
    cotangent,
    gain_attn,
    w_query,
    w_key,
    w_value,
    bias_query,
    bias_key,
    bias_value,
    w_out,
    gain_mlp,
    router,
    mix_gate,
    shared_gate,
    shared_up,
    shared_down,
    expert_gate,
    expert_up,
    expert_down,
):
    fsdp_count = lax.axis_size("fsdp")
    sp_count = lax.axis_size("sp")
    sp_place = lax.axis_index("sp")
    fsdp_place = lax.axis_index("fsdp")
    pair_count = fsdp_count // 2
    tok_count = tokens.shape[0]
    seq_len = segments.shape[0]
    width = tokens.shape[1]
    top_count = routes.shape[1]
    expert_count = router.shape[1]
    local_experts = expert_gate.shape[0]
    capacity = 3 * seq_len * top_count // (2 * expert_count)
    local_heads = w_query.shape[1] // HEAD
    head_width = w_query.shape[1]
    row_block = min(256, seq_len)
    block_count = seq_len // row_block
    score_scale = HEAD ** (-0.5)
    own_segments = lax.dynamic_slice_in_dim(segments, sp_place * tok_count, tok_count)
    live_rows = (own_segments >= 0).astype(F32)[:, None]
    position = jnp.arange(seq_len, dtype=jnp.int32)
    cosine, sine_table = rope_tables(seq_len, HEAD)
    whole_axes = ("fsdp", "sp")
    own_kernels = sp_count == 4 and pair_count == 4

    def spread(local_rows, number):
        if not own_kernels:
            return lax.all_gather(local_rows, "sp", axis=0, tiled=True)
        return gather_call([local_rows], number)[0]

    def collect(partial_rows, number):
        partial_rows = partial_rows.astype(BF)
        if not own_kernels:
            rows = lax.psum_scatter(partial_rows, "sp", scatter_dimension=0, tiled=True)
            return rows.astype(F32)
        blocks = partial_rows.reshape(1, sp_count, tok_count, width)
        return scatter_call(number, blocks)

    orders = sp_bits()

    def slow_start(parts, crossed):
        shape = (pair_count, sp_count, 2, tok_count // 2, width)
        mine, crossed = parts.reshape(shape), crossed.reshape(shape)

        def pick(h, j):
            place = sp_place ^ j
            return add_low(
                lax.dynamic_index_in_dim(mine, place, 1, False)[:, h],
                lax.dynamic_index_in_dim(crossed, place, 1, False)[:, h],
            )

        sent = [jnp.stack([pick(h, orders[h][0]), pick(h, 3)]) for h in range(2)]
        kept = [jnp.stack([pick(h, 0), pick(h, orders[h][1])]) for h in range(2)]
        return sent, kept

    def slow_first(sent):
        return [swap(sent[h], "sp", orders[h][0]) for h in range(2)]

    def slow_second(kept, came):
        kept = [add_low(kept[h], came[h]) for h in range(2)]
        return [kept[h][0] for h in range(2)], [
            swap(kept[h][1], "sp", orders[h][1]) for h in range(2)
        ]

    def slow_third(kept, came):
        rows = jnp.concatenate([add_low(kept[h], came[h]) for h in range(2)], 1)
        rows = reorder(rows, fsdp_place // 2).reshape(pair_count * tok_count, width)
        cores = [[2 * z + c for z in range(pair_count)] for c in range(2)]
        return lax.psum_scatter(
            rows, "fsdp", scatter_dimension=0, axis_index_groups=cores, tiled=True
        )

    inputs = tokens.astype(F32)
    attn_rms = rms_scale(inputs)
    gain_one = gain_attn.astype(F32)
    normed_attn = (inputs * attn_rms * gain_one).astype(BF)
    upstream = cotangent.astype(F32)
    d_mixer = (live_rows * upstream).astype(BF)
    normed_attn = spread(normed_attn, 1)
    full_qkv = lax.all_gather(
        jnp.concatenate([w_query, w_key, w_value], 1), "fsdp", axis=0, tiled=True
    )
    d_mixer_own = after(d_mixer, (full_qkv, normed_attn))
    d_mixer = lax.all_gather(d_mixer_own, "sp", axis=0, tiled=True)
    full_out_t = lax.all_gather(after(w_out.T, d_mixer), "fsdp", axis=0, tiled=True)
    share = shared_gate.shape[1] // fsdp_count
    packed = jnp.concatenate(
        [
            shared_gate.reshape(-1, fsdp_count, share),
            shared_up.reshape(-1, fsdp_count, share),
            shared_down.T.reshape(-1, fsdp_count, share),
        ],
        2,
    ).transpose(1, 0, 2)
    packed = lax.all_to_all(
        after(packed, full_qkv), "fsdp", split_axis=0, concat_axis=0, tiled=True
    ).reshape(width, 3 * share)
    hidden_units = expert_gate.shape[2]
    hp = round_up(hidden_units + expert_count, 128)
    shared_pad = round_up(share + 1, 128)
    experts_like = jnp.broadcast_to(router, (local_experts, width, expert_count))
    wide_gu = jnp.concatenate(
        [
            pad_last(jnp.concatenate([expert_gate, experts_like], 2), hp),
            pad_last(expert_up, hp),
        ],
        2,
    )
    wide_down = jnp.pad(expert_down, ((0, 0), (0, hp - hidden_units), (0, 0)))
    all_routes = routes.T[None]
    bit = 1
    while bit < fsdp_count:
        all_routes = jnp.concatenate([all_routes, swap(all_routes, "fsdp", bit)], 0)
        bit *= 2
    first_expert = fsdp_place * local_experts
    wanted = first_expert + jnp.arange(local_experts, dtype=jnp.int32)
    named = jnp.any(all_routes[:, None] == wanted[None, :, None, None], axis=2)
    tally = jnp.cumsum(named.astype(jnp.int32), axis=2) - 1
    codes = jnp.where(named, tally, -1)
    lane = jnp.arange(128, dtype=jnp.int32)[None, :] + hidden_units // 128 * 128 - hidden_units
    own = (lane == wanted[:, None]).astype(F32)

    normed_attn = after(normed_attn, (codes, wide_gu, wide_down))
    qkv_lin = dot(normed_attn, full_qkv)
    query_lin = qkv_lin[:, :head_width] + bias_query.astype(F32)
    key_lin = qkv_lin[:, head_width : 2 * head_width] + bias_key.astype(F32)
    value_rows = (
        (qkv_lin[:, 2 * head_width :] + bias_value.astype(F32))
        .astype(BF)
        .reshape(seq_len, local_heads, HEAD)
    )
    query_rot = rotate(query_lin.reshape(seq_len, local_heads, HEAD), cosine, sine_table).astype(BF)
    query_rot, packed = lax.optimization_barrier((query_rot, packed))
    if own_kernels:
        d_mixer_own = after(d_mixer_own, packed)
        d_mixer_far = jnp.stack([swap(d_mixer_own, "fsdp", 2 * k) for k in range(1, 2)])
    shared_gu = jnp.concatenate(
        [
            pad_last(jnp.concatenate([packed[:, :share], mix_gate[:, None]], 1), shared_pad),
            pad_last(packed[:, share : 2 * share], shared_pad),
        ],
        1,
    )
    shared_down_rows = pad_last(packed[:, 2 * share :], shared_pad).T
    key_rot = rotate(key_lin.reshape(seq_len, local_heads, HEAD), cosine, sine_table).astype(BF)

    def block_scores(block_index):
        start, stop = block_index * row_block, (block_index + 1) * row_block
        query_block = query_rot[start:stop]
        raw_scores = (
            jnp.einsum(
                "qhd,khd->hqk", query_block, key_rot[:stop], preferred_element_type=jnp.float32
            )
            * score_scale
        )
        allowed = (
            (segments[start:stop, None] == segments[None, :stop])
            & (position[None, :stop] <= position[start:stop, None])
        )[None]
        return (query_block, raw_scores, allowed)

    def attend_block(block_index):
        query_block, raw_scores, allowed = block_scores(block_index)
        row_max = jnp.max(jnp.where(allowed, raw_scores, -jnp.inf), axis=-1, keepdims=True)
        exponent = jnp.exp(jnp.where(allowed, raw_scores - row_max, -jnp.inf))
        row_total = jnp.sum(exponent, axis=-1, keepdims=True)
        probability = (exponent / row_total).astype(BF)
        attended_block = jnp.einsum(
            "hqk,khd->qhd",
            probability,
            value_rows[: raw_scores.shape[2]],
            preferred_element_type=jnp.float32,
        ).astype(BF)
        return (attended_block, row_max + jnp.log(row_total))

    blocks = [attend_block(n) for n in range(block_count)]
    log_total = [block[1] for block in blocks]
    attended = jnp.concatenate([block[0] for block in blocks], 0)
    attended = attended.reshape(seq_len, local_heads * HEAD)
    attn_out = collect(nt_dot(attended, full_out_t), 2)
    hidden = inputs + live_rows * attn_out
    mlp_rms = rms_scale(hidden)
    gain_two = gain_mlp.astype(F32)
    normed_mlp = (hidden * mlp_rms * gain_two).astype(BF)
    weights = (wide_gu, wide_down, shared_gu, shared_down_rows)
    sizes = (hidden_units, expert_count, share, capacity)
    if own_kernels:
        all_rows, all_d_rows, mixer_parts, d_parts, mixer_crossed, d_crossed, *kept = moe_call(
            normed_mlp, d_mixer, codes, own, weights, sizes, 3, d_mixer_far
        )
        blocks = (pair_count, sp_count, tok_count, width)
        d_mlp_own = scatter_call(4, d_parts.reshape(blocks), d_crossed.reshape(blocks))
    else:
        seq_rows = spread(normed_mlp, 3)
        mixer_sum = d_sum = jnp.zeros((seq_len, width), F32)
        grads = None
        together = max(1, fsdp_count // 4)
        for start in range(0, fsdp_count, together):
            some = range(start, start + together)
            all_rows = jnp.stack([swap(seq_rows, "fsdp", m) for m in some])
            all_d_rows = jnp.stack([swap(d_mixer, "fsdp", m) for m in some])
            mixer_parts, d_parts, *kept = moe_call(
                all_rows, all_d_rows, codes[start : start + together], own, weights, sizes
            )
            more = expert_grads(*kept[:4]) + shared_grads(all_rows, all_d_rows, *kept[4:])
            grads = more if grads is None else jax.tree.map(jnp.add, grads, more)
            for n, m in enumerate(some):
                mixer_sum = mixer_sum + swap(mixer_parts[n], "fsdp", m).astype(F32)
                d_sum = d_sum + swap(d_parts[n], "fsdp", m).astype(F32)
            grads, mixer_sum, d_sum, seq_rows = lax.optimization_barrier(
                (grads, mixer_sum, d_sum, seq_rows)
            )
        mixer_out, d_mlp_own = collect(mixer_sum, 7), collect(d_sum, 8)
    grad_gain_two = jnp.sum(d_mlp_own * hidden * mlp_rms, axis=0)
    d_hidden = upstream + norm_back(d_mlp_own, hidden, mlp_rms, gain_two)
    d_attn = spread((live_rows * d_hidden).astype(BF), 5)
    if own_kernels:
        slow = slow_start(*after((mixer_parts, mixer_crossed), d_mlp_own))
        d_attn, slow = lax.optimization_barrier((d_attn, slow))
        slow = slow[1], slow_first(slow[0])
        grad_out_t = dot(d_attn.T, attended).astype(BF)
        grad_sgu, grad_sdown = shared_grads(
            all_rows, all_d_rows, *after(kept[4:], (d_attn, grad_out_t))
        )
    else:
        grad_out_t = dot(d_attn.T, attended).astype(BF)
        grad_gu, grad_ed, grad_sgu, grad_sdown = grads
    grad_w_out = lax.psum_scatter(
        grad_out_t, "fsdp", scatter_dimension=0, tiled=True
    ).astype(F32)
    packed_grad = jnp.concatenate(
        [
            grad_sgu[:, :share],
            grad_sgu[:, shared_pad : shared_pad + share],
            grad_sdown[:, :share],
        ],
        1,
    ).astype(BF)
    d_attn, packed_grad = lax.optimization_barrier((d_attn, packed_grad))
    packed_grad = lax.all_to_all(
        packed_grad.reshape(fsdp_count, -1, 3 * share), "fsdp", split_axis=0, concat_axis=0, tiled=True
    ).transpose(1, 0, 2)
    d_attended = dot(d_attn, full_out_t).astype(BF).reshape(seq_len, local_heads, HEAD)

    if own_kernels:
        d_attended, slow = lax.optimization_barrier((d_attended, slow))
        slow = slow_second(*slow)

    def attend_back(block_index):
        query_block, raw_scores, allowed = block_scores(block_index)
        start, stop = block_index * row_block, (block_index + 1) * row_block
        prob_full = jnp.exp(jnp.where(allowed, raw_scores - log_total[block_index], -jnp.inf))
        prob_low = prob_full.astype(BF)
        grad_block = d_attended[start:stop]
        d_prob = jnp.einsum(
            "qhd,khd->hqk", grad_block, value_rows[:stop], preferred_element_type=jnp.float32
        )
        d_scores = (
            prob_full * (d_prob - jnp.sum(prob_full * d_prob, axis=-1, keepdims=True))
        ).astype(BF)
        query_grad = (
            jnp.einsum("hqk,khd->qhd", d_scores, key_rot[:stop], preferred_element_type=jnp.float32)
            * score_scale
        )
        key_grad = (
            jnp.einsum("hqk,qhd->khd", d_scores, query_block, preferred_element_type=jnp.float32)
            * score_scale
        )
        value_grad = jnp.einsum(
            "hqk,qhd->khd", prob_low, grad_block, preferred_element_type=jnp.float32
        )
        return query_grad, key_grad, value_grad

    query_grads = []
    for block_index in range(block_count)[::-1]:
        query_part, key_part, value_part = attend_back(block_index)
        query_grads.insert(0, query_part)
        if block_index == block_count - 1:
            key_grad, value_grad = key_part, value_part
        else:
            stop = (block_index + 1) * row_block
            key_grad = key_grad.at[:stop].add(key_part)
            value_grad = value_grad.at[:stop].add(value_part)
    query_grad = jnp.concatenate(query_grads, 0)
    if own_kernels:
        query_grad, slow, packed_grad, grad_w_out = lax.optimization_barrier(
            (query_grad, slow, packed_grad, grad_w_out)
        )
        mixer_out = slow_third(*slow).astype(F32)
    query_grad = query_grad.reshape(seq_len, local_heads, HEAD)
    d_query = (
        unrotate(query_grad, cosine, sine_table)
        .reshape(seq_len, local_heads * HEAD)
        .astype(jnp.bfloat16)
    )
    d_key = (
        unrotate(key_grad, cosine, sine_table)
        .reshape(seq_len, local_heads * HEAD)
        .astype(jnp.bfloat16)
    )
    d_value = value_grad.reshape(seq_len, local_heads * HEAD).astype(jnp.bfloat16)
    d_qkv = jnp.concatenate([d_query, d_key, d_value], 1)
    grad_qkv = dot(normed_attn.T, d_qkv).astype(BF)
    d_normed_attn = dot(after(d_qkv, grad_qkv), full_qkv.T)
    d_attn_own = collect(d_normed_attn, 6)
    bias_grads = jnp.sum(d_qkv.astype(F32), axis=0)
    grad_gain_one = jnp.sum(d_attn_own * inputs * attn_rms, axis=0)
    grad_tokens = d_hidden + norm_back(d_attn_own, inputs, attn_rms, gain_one)
    grad_qkv = lax.psum_scatter(grad_qkv, "fsdp", scatter_dimension=0, tiled=True).astype(F32)
    if own_kernels:
        grad_gu, grad_ed = expert_grads(*after(kept[:4], d_attn_own))
    output = (hidden + live_rows * mixer_out).astype(BF)
    grad_expert_gate = grad_gu[..., :hidden_units]
    grad_expert_up = grad_gu[..., hp : hp + hidden_units]
    grad_expert_down = grad_ed[:, :hidden_units]
    grad_router = jnp.sum(grad_gu[..., hidden_units : hidden_units + expert_count], axis=0)
    grad_mix = grad_sgu[:, share]
    grad_shared_gate, grad_shared_up, grad_shared_down = (
        packed_grad[:, :, n * share : (n + 1) * share].reshape(-1, fsdp_count * share).astype(F32)
        for n in range(3)
    )
    bias_place = lax.dynamic_update_slice(
        jnp.zeros((3, sp_count * head_width), F32), bias_grads.reshape(3, -1), (0, sp_place * head_width)
    )
    small = jnp.concatenate(
        [jnp.stack([grad_gain_one, grad_gain_two, grad_mix]), bias_place, grad_router.T], 0
    )
    for axis_name in ("sp", "fsdp"):
        bit = 1
        while bit < lax.axis_size(axis_name):
            small = small + swap(small, axis_name, bit)
            bit *= 2
    sum_gain_one, sum_gain_two, sum_mix = small[0], small[1], small[2]
    own_bias = lax.dynamic_slice_in_dim(small[3:6], sp_place * head_width, head_width, 1)
    sum_router = small[6:].T
    return (
        output,
        grad_tokens,
        sum_gain_one,
        grad_qkv[:, :head_width],
        grad_qkv[:, head_width : 2 * head_width],
        grad_qkv[:, 2 * head_width :],
        own_bias[0],
        own_bias[1],
        own_bias[2],
        grad_w_out.T,
        sum_gain_two,
        sum_router,
        sum_mix,
        grad_shared_gate,
        grad_shared_up,
        grad_shared_down.T,
        grad_expert_gate,
        grad_expert_up,
        grad_expert_down,
    )


def solution(mesh):
    return jax.shard_map(
        local,
        mesh=mesh,
        in_specs=(
            P(("fsdp", "sp"), None),
            P("fsdp"),
            P("fsdp", None),
            P(("fsdp", "sp"), None),
            P(),
            P("fsdp", "sp"),
            P("fsdp", "sp"),
            P("fsdp", "sp"),
            P("sp"),
            P("sp"),
            P("sp"),
            P("sp", "fsdp"),
            P(),
            P(),
            P(),
            P("fsdp", "sp"),
            P("fsdp", "sp"),
            P("sp", "fsdp"),
            P("fsdp", None, "sp"),
            P("fsdp", None, "sp"),
            P("fsdp", "sp", None),
        ),
        out_specs=(
            P(("fsdp", "sp"), None),
            P(("fsdp", "sp"), None),
            P(),
            P("fsdp", "sp"),
            P("fsdp", "sp"),
            P("fsdp", "sp"),
            P("sp"),
            P("sp"),
            P("sp"),
            P("sp", "fsdp"),
            P(),
            P(),
            P(),
            P("fsdp", "sp"),
            P("fsdp", "sp"),
            P("sp", "fsdp"),
            P("fsdp", None, "sp"),
            P("fsdp", None, "sp"),
            P("fsdp", "sp", None),
        ),
        check_vma=False,
    )
```
